256 devices in a mesh: ctx: 16 (over z, x_lo), tp: 16 (over x_hi, y, core).
Axes of the slice: x: 4 (x_hi: 2, x_lo: 2; x = x_hi * 2 + x_lo), y: 4, z: 8, core: 2. Of those that a mesh axis runs over, the one named last changes fastest.
Arguments:
- queries: bfloat16 [4096, 16384], P('ctx', 'tp'), may hold values from -96 to 96
- keys_values: bfloat16 [2, 4096, 1024], P(None, 'ctx'), may hold values from -4 to 4
- out_grad: bfloat16 [4096, 16384], P(('ctx', 'tp')), may hold values from -6 to 6
- place: int32 [4096], P('ctx'), may hold values from 0 to 4095, as said below
- segments: int32 [4096], replicated, may hold values from 0 to 3, never falling along the last dimension, each value on 1 to 2304 neighbouring positions
- allow: int32 [32, 32], replicated, may hold values from 0 to 1, as said below
Outputs:
- grad_q: bfloat16 [4096, 16384], P('ctx', 'tp')
- key_value_gradient: bfloat16 [2, 4096, 1024], P(None, ('ctx', 'tp'))
The draws below stay inside these ranges and needn't reach their ends.
Inputs may be any that keep to these rules, and one draw needn't show every extreme that they name: place is a permutation of the packed positions; position p lies on context shard p // 256; the rows of one generator shard send at most 32 rows to one context shard, some pair sends exactly 32, and every context shard receives 256 rows. allow[i, i] is 1 and allow[i, j] is 0 for j > i.
All inputs are finite; a program needn't handle non-finite values.
Results may differ from the reference program's by a relative error of at most 0.019.
Values may be sent and summed in bfloat16 or wider, within the bound.
No kernel may reach another device: no remote copies, remote signals or barrier semaphores. Data moves between devices by JAX's collectives and lax.ppermute only.
A program may use at most 128 MiB of HBM per device.

```python
import math
import jax
import jax.numpy as jnp
import numpy as np
from jax import lax

QUERY_HEAD_COUNT = 128
KEY_VALUE_HEADS = 8
HEAD_SIZE = 128
TOK_DEV = 256
BLK = 128
DOCS = 4
SHARDS = 16
PACKED_TOKENS = 4096
NB = 32
DOC_MOST = 2304


def common_keys(key):
    drawn_sample = jax.random.normal(jax.random.fold_in(key, 11), (2, PACKED_TOKENS, KEY_VALUE_HEADS * HEAD_SIZE), jnp.float32)
    return jnp.clip(drawn_sample, -4.0, 4.0)


def draw_keys_values(key, part):
    return common_keys(key).astype(jnp.bfloat16)


def draw_queries(key, part):
    key = jax.random.fold_in(key, 1)
    fresh = jnp.clip(jax.random.normal(key, (PACKED_TOKENS, QUERY_HEAD_COUNT * HEAD_SIZE), jnp.float32), -4.0, 4.0)
    return fresh.astype(jnp.bfloat16)


def draw_place(key, part):
    key = jax.random.fold_in(key, 5)
    even = TOK_DEV // SHARDS
    first_key, order_key, slot_key = jax.random.split(key, 3)
    first = jax.random.permutation(first_key, SHARDS)
    second = jnp.roll(first, 1)
    owners = jnp.arange(SHARDS, dtype=jnp.int32)
    counts = even + even * (first[:, None] == owners[None, :]).astype(jnp.int32) - even * (second[:, None] == owners[None, :]).astype(jnp.int32)
    ends = jnp.cumsum(counts, axis=1)
    starts = ends - counts
    earlier = jnp.cumsum(counts, axis=0) - counts
    turn = jnp.arange(TOK_DEV, dtype=jnp.int32)
    dest = jnp.sum((ends[:, None, :] <= turn[None, :, None]).astype(jnp.int32), axis=2)
    rank = turn[None, :] - jnp.take_along_axis(starts, dest, axis=1)
    slot_index = jnp.take_along_axis(earlier, dest, axis=1) + rank
    orders = jax.vmap(lambda sub: jax.random.permutation(sub, TOK_DEV))(jax.random.split(order_key, SHARDS))
    shuffles = jax.vmap(lambda sub: jax.random.permutation(sub, TOK_DEV))(jax.random.split(slot_key, SHARDS))
    packed = dest * TOK_DEV + shuffles[dest, slot_index]
    rollout_rows = (owners[:, None] * TOK_DEV + orders).reshape(-1)
    return jnp.zeros((PACKED_TOKENS,), jnp.int32).at[rollout_rows].set(packed.reshape(-1).astype(jnp.int32))


def draw_allow(key, part):
    key = jax.random.fold_in(key, 7)
    bits = (jax.random.randint(key, (NB, NB), 0, 4) > 0).astype(jnp.int32)
    blocks = jnp.arange(NB, dtype=jnp.int32)
    lower = blocks[:, None] > blocks[None, :]
    diagonal = blocks[:, None] == blocks[None, :]
    return jnp.where(diagonal, 1, jnp.where(lower, bits, 0)).astype(jnp.int32)


def block_scale(rng, dims, shards, smallest, top_value):
    level = 1.0
    for dim, shards_of in shards:
        heights = jax.random.uniform(jax.random.fold_in(jax.random.fold_in(rng, 6), dim), (shards_of,), jnp.float32, smallest / len(shards), top_value / len(shards))
        level = level * jnp.repeat(jnp.exp(heights), dims[dim] // shards_of).reshape((-1,) + (1,) * (len(dims) - 1 - dim))
    return level


def split_up(number_of, total, reach, slope):
    loads = [(1 << 20) // math.isqrt(rank ** slope) + 1 for rank in range(2, number_of + 1)]
    rest, given = total - reach - (number_of - 1), [1] * (number_of - 1)
    while rest > 0:
        free = [i for i in range(number_of - 1) if given[i] < reach]
        pool, remaining = sum([loads[i] for i in free]), rest
        for i in free:
            more = min(reach - given[i], max(1, remaining * loads[i] // pool), rest)
            given[i] = given[i] + more
            rest = rest - more
    return np.array([reach] + given)


def uneven_parts(stream_key, amount, total, bound, slope):
    if amount == 2:
        one = jax.random.randint(stream_key, (), max(1, total - bound), min(bound, total - 1) + 1)
        return jnp.stack([one, total - one])
    tallies = jnp.asarray(split_up(amount, total, bound, slope), jnp.int32)
    twos = (amount - 1) // 2
    source_of, taker = tallies[1:1 + 2 * twos:2], tallies[2:2 + 2 * twos:2]
    slack = jnp.minimum(source_of - 1, bound - taker)
    passed = jax.random.randint(jax.random.fold_in(stream_key, 1), (twos,), 0, 1 << 20) % (slack + 1)
    tallies = tallies.at[1:1 + 2 * twos:2].set(source_of - passed).at[2:2 + 2 * twos:2].set(taker + passed)
    return tallies[jax.random.permutation(jax.random.fold_in(stream_key, 2), amount)]


def scatter_about(own_key, extent, width, bound, pieces=(), kind=jnp.bfloat16):
    values = width * jax.random.normal(own_key, extent, jnp.float32)
    if pieces:
        values = values * block_scale(own_key, extent, pieces, -0.22, 0.18)
    return jnp.clip(values, -bound, bound).astype(kind)


def setup_inputs(seed: int = 0) -> dict:
    seeds = jax.random.split(jax.random.key(seed), 7)
    queries = draw_queries(jax.random.fold_in(seeds[6], 71), 0)
    keys_values = draw_keys_values(jax.random.fold_in(seeds[6], 71), 0)
    out_grad = scatter_about(seeds[2], (PACKED_TOKENS, QUERY_HEAD_COUNT * HEAD_SIZE), 1.0, 6.0, ((0, 256),))
    place = draw_place(jax.random.fold_in(seeds[6], 71), 0)
    segments = jnp.searchsorted(jnp.cumsum(uneven_parts(seeds[4], DOCS, PACKED_TOKENS, DOC_MOST, 2)), jnp.arange(PACKED_TOKENS), side="right").astype(jnp.int32)
    allow = draw_allow(jax.random.fold_in(seeds[6], 71), 0)
    return dict(queries=queries, keys_values=keys_values, out_grad=out_grad, place=place, segments=segments, allow=allow)


NEG_FILL = -1e+30

def visible(query_pos, query_seg, query_allow, key_pos, key_seg):
    same_doc = query_seg[:, None] == key_seg[None, :]
    causal = key_pos[None, :] <= query_pos[:, None]
    block_ok = jnp.take(query_allow, key_pos // BLK, axis=1) > 0
    return same_doc & causal & block_ok

def reference(queries, keys_values, out_grad, place, segments, allow):
    count_of_tokens = queries.shape[0]
    packed_q = jnp.zeros_like(queries).at[place].set(queries)
    packed_kv = jnp.zeros_like(keys_values).at[:, place].set(keys_values)
    positions = jnp.arange(count_of_tokens, dtype=jnp.int32)
    visible_mask = visible(positions, segments, jnp.take(allow, positions // BLK, axis=0), positions, segments)
    score_scale = 1.0 / math.sqrt(HEAD_SIZE)
    group_head_count = QUERY_HEAD_COUNT // KEY_VALUE_HEADS

    def queries_per_key_head(kv_head):
        key_cols = lax.dynamic_slice_in_dim(packed_kv[0], kv_head * HEAD_SIZE, HEAD_SIZE, 1)
        value_cols = lax.dynamic_slice_in_dim(packed_kv[1], kv_head * HEAD_SIZE, HEAD_SIZE, 1)

        def per_query(running, member):
            head = kv_head * group_head_count + member
            query_cols = lax.dynamic_slice_in_dim(packed_q, head * HEAD_SIZE, HEAD_SIZE, 1)
            grad_cols = lax.dynamic_slice_in_dim(out_grad, head * HEAD_SIZE, HEAD_SIZE, 1)
            scores = jnp.dot(query_cols, key_cols.T, preferred_element_type=jnp.float32) * score_scale
            scores = jnp.where(visible_mask, scores, NEG_FILL)
            row_top = lax.optimization_barrier(jnp.max(scores, axis=1, keepdims=True))
            log_norm = row_top + jnp.log(lax.optimization_barrier(jnp.sum(jnp.where(visible_mask, jnp.exp(scores - row_top), 0.0), axis=1, keepdims=True)))
            weights = jnp.where(visible_mask, jnp.exp(scores - log_norm), 0.0)
            attended = jnp.dot(weights, value_cols.astype(jnp.float32), precision=lax.Precision.HIGHEST).astype(jnp.bfloat16)
            out_dot = lax.optimization_barrier(jnp.sum(grad_cols.astype(jnp.float32) * attended.astype(jnp.float32), axis=1, keepdims=True))
            weights_low = weights.astype(jnp.bfloat16)
            prob_grad = jnp.dot(grad_cols, value_cols.T, preferred_element_type=jnp.float32)
            score_grad = (weights * (prob_grad - out_dot)).astype(jnp.bfloat16)
            grad_query = (jnp.dot(score_grad, key_cols, preferred_element_type=jnp.float32) * score_scale).astype(jnp.bfloat16)
            key_term = jnp.dot(score_grad.T, query_cols, preferred_element_type=jnp.float32) * score_scale
            value_term = jnp.dot(weights_low.T, grad_cols, preferred_element_type=jnp.float32)
            return ((running[0] + key_term, running[1] + value_term), grad_query)
        zero_cols = jnp.zeros((count_of_tokens, HEAD_SIZE), jnp.float32)
        sums, query_gradient_rows = lax.scan(per_query, (zero_cols, zero_cols), jnp.arange(group_head_count, dtype=jnp.int32))
        return (sums[0].astype(jnp.bfloat16), sums[1].astype(jnp.bfloat16), query_gradient_rows)
    key_gradient_rows, value_gradient_rows, query_gradient_rows = lax.map(queries_per_key_head, jnp.arange(KEY_VALUE_HEADS, dtype=jnp.int32))
    grad_q = query_gradient_rows.reshape(QUERY_HEAD_COUNT, count_of_tokens, HEAD_SIZE).transpose(1, 0, 2).reshape(count_of_tokens, QUERY_HEAD_COUNT * HEAD_SIZE)
    key_value_gradient = jnp.stack([key_gradient_rows, value_gradient_rows]).transpose(0, 2, 1, 3).reshape(2, count_of_tokens, KEY_VALUE_HEADS * HEAD_SIZE)
    return (grad_q, key_value_gradient)
```

```python
import functools
import math

import jax
import jax.numpy as jnp
from jax import lax
from jax.experimental import pallas as pl
from jax.experimental.pallas import tpu as pltpu
from jax.sharding import PartitionSpec as P

QUERY_HEAD_COUNT = 128
KEY_VALUE_HEADS = 8
HEAD_SIZE = 128
BLK = 128
TOK = 256
SHARDS = 16
SLOTS = 32
DOC_MOST = 2304
BACK = -(-DOC_MOST // TOK)
WINDOW = BACK + 1
BLOCKS_BACK = -(-DOC_MOST // BLK)
MOST_BLOCKS = 2 * ((BLOCKS_BACK + 2) // 2)
LOCAL_HEADS = 8
GROUP = 4
LANES = GROUP * BLK
CHUNK = 2 * BLK
MOST_CHUNKS = MOST_BLOCKS // 2
NEG_FILL = -1e30
SCALE = 1.0 / math.sqrt(HEAD_SIZE)
EXP2_SCALE = SCALE * math.log2(math.e)
F32 = jnp.float32
BF16 = jnp.bfloat16


def iota(shape, dim):
    return lax.broadcasted_iota(jnp.int32, shape, dim)


def dot(a, b):
    return jnp.dot(a, b, preferred_element_type=F32)


def ranks_within(member):
    earlier = (iota((TOK, TOK), 0) < iota((TOK, TOK), 1)).astype(F32).astype(BF16)
    counts = dot(member.astype(F32).astype(BF16), earlier)
    return jnp.where(member, counts, -1.0)


def pack_kernel(place_ref, rows_ref, out_ref):
    owner = place_ref[...] >> 8
    rank = ranks_within(owner == iota((SHARDS, TOK), 0))
    slot = iota((SLOTS, TOK), 0).astype(F32)
    picks = jnp.concatenate(
        [(rank[s : s + 1, :] == slot).astype(F32) for s in range(SHARDS)], axis=0
    ).astype(BF16)
    for first in range(0, rows_ref.shape[1], 256):
        cols = pl.ds(first, 256)
        out_ref[:, cols] = dot(picks, rows_ref[:, cols]).astype(BF16)


def permute_kernel(info_ref, place_ref, kv_ref, out_ref, unpack_ref):
    shard = info_ref[0]
    base = jnp.maximum(shard - BACK, 0)
    place = place_ref[...]
    rank = ranks_within((place >> 8) == shard)
    within = ((place & (TOK - 1)) + 1).astype(F32)
    slot = iota((SLOTS, TOK), 0).astype(F32)
    lane = (iota((SLOTS, TOK), 1) + 1).astype(F32)
    for s in range(SHARDS):
        hit = rank[s : s + 1, :] == slot
        landing = jnp.sum(jnp.where(hit, within[s : s + 1, :], 0.0), axis=1, keepdims=True)
        unpack_ref[s * SLOTS : (s + 1) * SLOTS, :] = (landing == lane).astype(F32).astype(BF16)

    def one_shard(i, carry):
        rows = iota((TOK, TOK), 0) + (base + i) * TOK
        total = jnp.zeros((TOK, 2 * HEAD_SIZE), F32)
        for s in range(SHARDS):
            picks = (place_ref[s : s + 1, :] == rows).astype(F32).astype(BF16)
            total = total + dot(picks, kv_ref[s * TOK : (s + 1) * TOK, :])
        out_ref[pl.ds(pl.multiple_of(i * TOK, TOK), TOK), :] = total.astype(BF16)
        return carry

    lax.fori_loop(0, shard - base + 1, one_shard, 0)


def attention_kernel(
    info_ref,
    seg_ref,
    allow_ref,
    segv_ref,
    unpack_ref,
    recv_ref,
    grad_ref,
    kv_ref,
    dq_ref,
    keep_ref,
    send_ref,
    q_s,
    qr_s,
    gr_s,
    qt_s,
    gt_s,
    k_s,
    v_s,
    kt_s,
    bias_s,
    e_s,
    dp_s,
    top_s,
    dqt_s,
    dk_s,
    dv_s,
    acc_s,
    list_s,
):
    shard = info_ref[0]
    core = info_ref[1]
    base = jnp.maximum(shard - BACK, 0)
    acc_s[...] = jnp.zeros_like(acc_s)
    for first in range(0, LOCAL_HEADS * HEAD_SIZE, 256):
        cols = pl.ds(first, 256)
        q_s[:, cols] = lax.dot_general(
            unpack_ref[...],
            recv_ref[:, cols],
            (((0,), (0,)), ((), ())),
            preferred_element_type=F32,
        ).astype(BF16)

    def query_block(half, carry):
        qb = shard * 2 + half
        row0 = pl.multiple_of(half * BLK, BLK)
        q_seg = segv_ref[pl.ds(qb, 1), :]
        q_first = seg_ref[qb * BLK]

        def scan(kb, count):
            seen = jnp.logical_and(
                seg_ref[kb * BLK + BLK - 1] >= q_first, allow_ref[qb, kb] != 0
            )

            @pl.when(seen)
            def _():
                list_s[count] = kb
                src = pl.ds(pl.multiple_of((kb - 2 * base) * BLK, BLK), BLK)
                dst = pl.ds(pl.multiple_of(count * BLK, BLK), BLK)
                k_blk = kv_ref[src, :HEAD_SIZE]
                k_s[dst, :] = k_blk
                v_s[dst, :] = kv_ref[src, HEAD_SIZE:]
                lanes = pl.ds(pl.multiple_of((count % 2) * BLK, BLK), BLK)
                kt_s[count // 2, :, lanes] = k_blk.astype(F32).T.astype(BF16)
                k_seg = jnp.broadcast_to(segv_ref[pl.ds(kb, 1), :].astype(F32), (BLK, BLK)).T
                k_pos = kb * BLK + iota((BLK, BLK), 0)
                q_pos = qb * BLK + iota((BLK, BLK), 1)
                ok = (k_seg == q_seg.astype(F32)) & (k_pos <= q_pos)
                bias_s[dst, :] = jnp.where(ok, 0.0, NEG_FILL)

            return count + seen.astype(jnp.int32)

        count = lax.fori_loop(jnp.maximum(qb - BLOCKS_BACK, 0), qb + 1, scan, 0)

        @pl.when(count % 2 == 1)
        def _():
            dst = pl.ds(pl.multiple_of(count * BLK, BLK), BLK)
            k_s[dst, :] = jnp.zeros((BLK, HEAD_SIZE), BF16)
            v_s[dst, :] = jnp.zeros((BLK, HEAD_SIZE), BF16)
            kt_s[count // 2, :, BLK:] = jnp.zeros((HEAD_SIZE, BLK), BF16)
            bias_s[dst, :] = jnp.full((BLK, BLK), NEG_FILL, F32)

        chunks = (count + 1) // 2

        def clear(ch, c):
            rows = pl.ds(pl.multiple_of(ch * CHUNK, CHUNK), CHUNK)
            dk_s[rows, :] = jnp.zeros((CHUNK, HEAD_SIZE), F32)
            dv_s[rows, :] = jnp.zeros((CHUNK, HEAD_SIZE), F32)
            return c

        lax.fori_loop(0, chunks, clear, 0)
        rows = pl.ds(row0, BLK)
        for hg in range(LOCAL_HEADS // GROUP):
            for i in range(GROUP):
                cols = pl.ds((hg * GROUP + i) * HEAD_SIZE, HEAD_SIZE)
                mine = pl.ds(i * BLK, BLK)
                q_blk = q_s[rows, cols]
                g_blk = grad_ref[rows, cols]
                qr_s[mine, :] = q_blk
                gr_s[mine, :] = g_blk
                qt_s[:, mine] = q_blk.astype(F32).T.astype(BF16)
                gt_s[:, mine] = g_blk.astype(F32).T.astype(BF16)

            def first_pass(ch, state):
                top, total, weighed = state
                rows_c = pl.ds(pl.multiple_of(ch * CHUNK, CHUNK), CHUNK)
                scores = dot(k_s[rows_c, :], qt_s[...])
                scores = scores + jnp.concatenate([bias_s[rows_c, :]] * GROUP, axis=1)
                new_top = jnp.maximum(top, jnp.max(scores, axis=0, keepdims=True))
                factor = jnp.exp2((top - new_top) * EXP2_SCALE)
                e = jnp.exp2((scores - new_top) * EXP2_SCALE)
                dp = dot(v_s[rows_c, :], gt_s[...])
                e_s[ch] = e
                dp_s[ch] = dp
                top_s[ch] = new_top
                total = total * factor + jnp.sum(e.reshape(-1, 8, LANES), axis=0)
                weighed = weighed * factor + jnp.sum((e * dp).reshape(-1, 8, LANES), axis=0)
                return (new_top, total, weighed)

            start = (
                jnp.full((1, LANES), NEG_FILL, F32),
                jnp.zeros((8, LANES), F32),
                jnp.zeros((8, LANES), F32),
            )
            top, total, weighed = lax.fori_loop(0, chunks, first_pass, start)
            inverse = 1.0 / jnp.sum(total, axis=0, keepdims=True)
            out_dot = jnp.sum(weighed, axis=0, keepdims=True) * inverse
            dqt_s[...] = jnp.zeros_like(dqt_s)

            def second_pass(ch, c):
                rows_c = pl.ds(pl.multiple_of(ch * CHUNK, CHUNK), CHUNK)
                factor = jnp.exp2((top_s[ch] - top) * EXP2_SCALE) * inverse
                weights = e_s[ch] * factor
                score_grad = (weights * (dp_s[ch] - out_dot)).astype(BF16)
                dv_s[rows_c, :] += dot(weights.astype(BF16), gr_s[...])
                dk_s[rows_c, :] += dot(score_grad, qr_s[...])
                dqt_s[...] += dot(kt_s[ch], score_grad)
                return c

            lax.fori_loop(0, chunks, second_pass, 0)
            for i in range(GROUP):
                cols = pl.ds((hg * GROUP + i) * HEAD_SIZE, HEAD_SIZE)
                dq_ref[rows, cols] = (dqt_s[:, i * BLK : (i + 1) * BLK] * SCALE).T.astype(BF16)

        def spread(n, c):
            src = pl.ds(pl.multiple_of(n * BLK, BLK), BLK)
            dst = pl.ds(pl.multiple_of((list_s[n] - 2 * base) * BLK, BLK), BLK)
            acc_s[0, dst, :] += dk_s[src, :]
            acc_s[1, dst, :] += dv_s[src, :]
            return c

        lax.fori_loop(0, count, spread, 0)
        return carry

    lax.fori_loop(0, 2, query_block, 0)

    @pl.when(core == 0)
    def _():
        keep_ref[...] = acc_s[0] * SCALE
        send_ref[...] = acc_s[1].astype(BF16)

    @pl.when(core == 1)
    def _():
        keep_ref[...] = acc_s[1]
        send_ref[...] = (acc_s[0] * SCALE).astype(BF16)


def merge_kernel(info_ref, keep_ref, recv_ref, out_ref):
    base = jnp.maximum(info_ref[0] - BACK, 0)
    out_ref[...] = jnp.zeros_like(out_ref)
    rows = pl.ds(pl.multiple_of(base * TOK, TOK), WINDOW * TOK)
    out_ref[rows, :] = (keep_ref[...] + recv_ref[...].astype(F32)).astype(BF16)


VMEM = pl.BlockSpec(memory_space=pltpu.VMEM)
SMEM = pl.BlockSpec(memory_space=pltpu.SMEM)


def call_attention(info, segments, allow, unpack, q_recv, g_local, kv_window):
    width = g_local.shape[1]
    return pl.pallas_call(
        attention_kernel,
        in_specs=[SMEM, SMEM, SMEM] + [VMEM] * 5,
        out_specs=[VMEM, VMEM, VMEM],
        out_shape=[
            jax.ShapeDtypeStruct((TOK, width), BF16),
            jax.ShapeDtypeStruct((WINDOW * TOK, HEAD_SIZE), F32),
            jax.ShapeDtypeStruct((WINDOW * TOK, HEAD_SIZE), BF16),
        ],
        scratch_shapes=[
            pltpu.VMEM((TOK, width), BF16),
            pltpu.VMEM((LANES, HEAD_SIZE), BF16),
            pltpu.VMEM((LANES, HEAD_SIZE), BF16),
            pltpu.VMEM((HEAD_SIZE, LANES), BF16),
            pltpu.VMEM((HEAD_SIZE, LANES), BF16),
            pltpu.VMEM((MOST_BLOCKS * BLK, HEAD_SIZE), BF16),
            pltpu.VMEM((MOST_BLOCKS * BLK, HEAD_SIZE), BF16),
            pltpu.VMEM((MOST_CHUNKS, HEAD_SIZE, CHUNK), BF16),
            pltpu.VMEM((MOST_BLOCKS * BLK, BLK), F32),
            pltpu.VMEM((MOST_CHUNKS, CHUNK, LANES), F32),
            pltpu.VMEM((MOST_CHUNKS, CHUNK, LANES), F32),
            pltpu.VMEM((MOST_CHUNKS, 1, LANES), F32),
            pltpu.VMEM((HEAD_SIZE, LANES), F32),
            pltpu.VMEM((MOST_BLOCKS * BLK, HEAD_SIZE), F32),
            pltpu.VMEM((MOST_BLOCKS * BLK, HEAD_SIZE), F32),
            pltpu.VMEM((2, WINDOW * TOK, HEAD_SIZE), F32),
            pltpu.SMEM((MOST_BLOCKS,), jnp.int32),
        ],
        compiler_params=pltpu.CompilerParams(vmem_limit_bytes=48 * 2**20),
        name="attention",
    )(info, segments, allow, segments.reshape(-1, BLK), unpack, q_recv, g_local, kv_window)


def on_device(queries, keys_values, out_grad, place, segments, allow):
    tp_index = lax.axis_index("tp")
    ctx_index = lax.axis_index("ctx")
    tp_size = lax.axis_size("tp")
    width = LOCAL_HEADS * HEAD_SIZE
    info = jnp.stack([ctx_index, tp_index % 2]).astype(jnp.int32)
    kv_first = (tp_index // 2) * HEAD_SIZE
    kv_mine = lax.dynamic_slice_in_dim(keys_values, kv_first, HEAD_SIZE, 2)
    kv_rows = jnp.concatenate([kv_mine[0], kv_mine[1]], axis=1)
    place_all = lax.all_gather(place, "ctx", axis=0, tiled=True).reshape(SHARDS, TOK)
    kv_all = lax.all_gather(kv_rows, "ctx", axis=0, tiled=True)
    g_local = lax.all_to_all(out_grad, "tp", split_axis=1, concat_axis=0, tiled=True)
    q_send = pl.pallas_call(
        pack_kernel,
        in_specs=[VMEM, VMEM],
        out_specs=VMEM,
        out_shape=jax.ShapeDtypeStruct((SHARDS * SLOTS, width), BF16),
        name="pack",
    )(place.reshape(1, TOK), queries)
    q_recv = lax.all_to_all(q_send, "ctx", split_axis=0, concat_axis=0, tiled=True)
    kv_window, unpack = pl.pallas_call(
        permute_kernel,
        in_specs=[SMEM, VMEM, VMEM],
        out_specs=[VMEM, VMEM],
        out_shape=[
            jax.ShapeDtypeStruct((WINDOW * TOK, 2 * HEAD_SIZE), BF16),
            jax.ShapeDtypeStruct((SHARDS * SLOTS, TOK), BF16),
        ],
        compiler_params=pltpu.CompilerParams(vmem_limit_bytes=32 * 2**20),
        name="permute",
    )(info, place_all, kv_all)
    grad_q, keep, send = call_attention(
        info, segments, allow, unpack, q_recv, g_local, kv_window
    )
    recv = lax.ppermute(send, "tp", [(k, k ^ 1) for k in range(tp_size)])
    part = pl.pallas_call(
        merge_kernel,
        in_specs=[SMEM, VMEM, VMEM],
        out_specs=VMEM,
        out_shape=jax.ShapeDtypeStruct((SHARDS * TOK, HEAD_SIZE), BF16),
        name="merge",
    )(info, keep, recv)
    parts = lax.all_to_all(
        part.reshape(SHARDS, TOK, HEAD_SIZE), "ctx", split_axis=0, concat_axis=0, tiled=True
    )
    owned = jnp.sum(parts.astype(F32), axis=0).astype(BF16)
    heads = lax.all_to_all(
        owned.reshape(tp_size, TOK // tp_size, HEAD_SIZE),
        "tp",
        split_axis=0,
        concat_axis=0,
        tiled=True,
    )
    key_value_gradient = (
        heads.reshape(KEY_VALUE_HEADS, 2, TOK // tp_size, HEAD_SIZE)
        .transpose(1, 2, 0, 3)
        .reshape(2, TOK // tp_size, KEY_VALUE_HEADS * HEAD_SIZE)
    )
    return (grad_q, key_value_gradient)


def solution(mesh):
    in_specs = (P("ctx", "tp"), P(None, "ctx", None), P(("ctx", "tp"), None), P("ctx"), P(), P())
    out_specs = (P("ctx", "tp"), P(None, ("ctx", "tp"), None))
    return jax.shard_map(
        on_device, mesh=mesh, in_specs=in_specs, out_specs=out_specs, check_vma=False
    )
```

```python
import functools
import math

import jax
import jax.numpy as jnp
from jax import lax
from jax.experimental import pallas as pl
from jax.experimental.pallas import tpu as pltpu
from jax.sharding import PartitionSpec as P

QUERY_HEAD_COUNT = 128
KEY_VALUE_HEADS = 8
HEAD_SIZE = 128
BLK = 128
TOK = 256
SHARDS = 16
SLOTS = 32
META = 16
Z_CHIPS = SHARDS // 2
RING = Z_CHIPS // 2
DOC_MOST = 2304
BACK = -(-DOC_MOST // TOK)
WINDOW = BACK + 1
BLOCKS_BACK = -(-DOC_MOST // BLK)
MOST_BLOCKS = 2 * ((BLOCKS_BACK + 2) // 2)
LOCAL_HEADS = 8
GROUP = 4
LANES = GROUP * BLK
CHUNK = 2 * BLK
MOST_CHUNKS = MOST_BLOCKS // 2
NEG_FILL = -1e30
SCALE = 1.0 / math.sqrt(HEAD_SIZE)
EXP2_SCALE = SCALE * math.log2(math.e)
F32 = jnp.float32
BF16 = jnp.bfloat16


def iota(shape, dim):
    return lax.broadcasted_iota(jnp.int32, shape, dim)


def dot(a, b):
    return jnp.dot(a, b, preferred_element_type=F32)


def ranks_within(member):
    earlier = (iota((TOK, TOK), 0) < iota((TOK, TOK), 1)).astype(F32).astype(BF16)
    counts = dot(member.astype(F32).astype(BF16), earlier)
    return jnp.where(member, counts, -1.0)


def pack_kernel(place_ref, rows_ref, out_ref):
    owner = place_ref[...] >> 8
    rank = ranks_within(owner == iota((SHARDS, TOK), 0))
    slot = iota((SLOTS, TOK), 0).astype(F32)
    picks = jnp.concatenate(
        [(rank[s : s + 1, :] == slot).astype(F32) for s in range(SHARDS)], axis=0
    ).astype(BF16)
    for first in range(0, rows_ref.shape[1], 256):
        cols = pl.ds(first, 256)
        out_ref[:, cols] = dot(picks, rows_ref[:, cols]).astype(BF16)


def stage_kernel(info_ref, place_ref, kv_ref, out_ref):
    place = place_ref[...]
    out_ref[:TOK, :HEAD_SIZE] = kv_ref[0]
    out_ref[:TOK, HEAD_SIZE:] = kv_ref[1]
    row = iota((META, TOK), 0)
    owner = jnp.broadcast_to((place >> 8).astype(F32), (META, TOK))
    within = jnp.broadcast_to((place & (TOK - 1)).astype(F32), (META, TOK))
    meta = jnp.where(row == 0, owner, jnp.where(row == 1, within, 0.0))
    out_ref[TOK:, :] = meta.astype(BF16)


def permute_kernel(info_ref, own_ref, *refs):
    mine, theirs = refs[:RING], refs[RING : 2 * RING]
    out_ref, unpack_ref = refs[2 * RING :]
    shard = info_ref[0]
    core = info_ref[1]
    base = jnp.maximum(shard - BACK, 0)
    z, x = shard // 2, shard % 2
    sources = [(own_ref.at[j], shard ^ j) for j in range(2)]
    for refs_k, side in ((mine, core), (theirs, 1 - core)):
        for k in range(1, RING):
            far = (z + k * (2 * side - 1) + Z_CHIPS) % Z_CHIPS
            sources += [(refs_k[k - 1].at[j], 2 * far + (x ^ j)) for j in range(2)]
        far = (z + RING) % Z_CHIPS
        sources += [(refs_k[RING - 1], 2 * far + (x ^ side))]
    owners = jnp.concatenate([ref[TOK : TOK + 1, :].astype(F32) for ref, _ in sources], axis=0)
    within = jnp.concatenate([ref[TOK + 1 : TOK + 2, :].astype(F32) for ref, _ in sources], axis=0)
    rank = ranks_within(owners == shard.astype(F32))
    slot = iota((SLOTS, TOK), 0).astype(F32)
    lane = iota((SLOTS, TOK), 1).astype(F32)
    for i, (_, source) in enumerate(sources):
        hit = rank[i : i + 1, :] == slot
        landing = jnp.sum(jnp.where(hit, within[i : i + 1, :] + 1.0, 0.0), axis=1, keepdims=True)
        rows = pl.ds(pl.multiple_of(source * SLOTS, SLOTS), SLOTS)
        unpack_ref[rows, :] = (landing == lane + 1.0).astype(F32).astype(BF16)

    def one_shard(i, carry):
        rows = iota((TOK, TOK), 0).astype(F32)
        goal = jnp.where(owners == (base + i).astype(F32), within, -1.0)
        total = jnp.zeros((TOK, 2 * HEAD_SIZE), F32)
        for n, (ref, _) in enumerate(sources):
            picks = (goal[n : n + 1, :] == rows).astype(F32).astype(BF16)
            total = total + dot(picks, ref[:TOK, :])
        out_ref[pl.ds(pl.multiple_of(i * TOK, TOK), TOK), :] = total.astype(BF16)
        return carry

    lax.fori_loop(0, shard - base + 1, one_shard, 0)


def attention_kernel(
    info_ref,
    seg_ref,
    allow_ref,
    segv_ref,
    unpack_ref,
    recv_ref,
    grad_ref,
    kv_ref,
    dq_ref,
    keep_ref,
    send_ref,
    q_s,
    qr_s,
    gr_s,
    qt_s,
    gt_s,
    k_s,
    v_s,
    kt_s,
    bias_s,
    e_s,
    dp_s,
    top_s,
    dqt_s,
    dk_s,
    dv_s,
    acc_s,
    list_s,
):
    shard = info_ref[0]
    core = info_ref[1]
    base = jnp.maximum(shard - BACK, 0)
    acc_s[...] = jnp.zeros_like(acc_s)
    for first in range(0, LOCAL_HEADS * HEAD_SIZE, 256):
        cols = pl.ds(first, 256)
        q_s[:, cols] = lax.dot_general(
            unpack_ref[...],
            recv_ref[:, cols],
            (((0,), (0,)), ((), ())),
            preferred_element_type=F32,
        ).astype(BF16)

    def query_block(half, carry):
        qb = shard * 2 + half
        row0 = pl.multiple_of(half * BLK, BLK)
        q_seg = segv_ref[pl.ds(qb, 1), :]
        q_first = seg_ref[qb * BLK]

        def scan(kb, count):
            seen = jnp.logical_and(
                seg_ref[kb * BLK + BLK - 1] >= q_first, allow_ref[qb, kb] != 0
            )

            @pl.when(seen)
            def _():
                list_s[count] = kb
                src = pl.ds(pl.multiple_of((kb - 2 * base) * BLK, BLK), BLK)
                dst = pl.ds(pl.multiple_of(count * BLK, BLK), BLK)
                k_blk = kv_ref[src, :HEAD_SIZE]
                k_s[dst, :] = k_blk
                v_s[dst, :] = kv_ref[src, HEAD_SIZE:]
                lanes = pl.ds(pl.multiple_of((count % 2) * BLK, BLK), BLK)
                kt_s[count // 2, :, lanes] = k_blk.astype(F32).T.astype(BF16)
                k_seg = jnp.broadcast_to(segv_ref[pl.ds(kb, 1), :].astype(F32), (BLK, BLK)).T
                k_pos = kb * BLK + iota((BLK, BLK), 0)
                q_pos = qb * BLK + iota((BLK, BLK), 1)
                ok = (k_seg == q_seg.astype(F32)) & (k_pos <= q_pos)
                bias_s[dst, :] = jnp.where(ok, 0.0, NEG_FILL)

            return count + seen.astype(jnp.int32)

        count = lax.fori_loop(jnp.maximum(qb - BLOCKS_BACK, 0), qb + 1, scan, 0)

        @pl.when(count % 2 == 1)
        def _():
            dst = pl.ds(pl.multiple_of(count * BLK, BLK), BLK)
            k_s[dst, :] = jnp.zeros((BLK, HEAD_SIZE), BF16)
            v_s[dst, :] = jnp.zeros((BLK, HEAD_SIZE), BF16)
            kt_s[count // 2, :, BLK:] = jnp.zeros((HEAD_SIZE, BLK), BF16)
            bias_s[dst, :] = jnp.full((BLK, BLK), NEG_FILL, F32)

        chunks = (count + 1) // 2

        def clear(ch, c):
            rows = pl.ds(pl.multiple_of(ch * CHUNK, CHUNK), CHUNK)
            dk_s[rows, :] = jnp.zeros((CHUNK, HEAD_SIZE), F32)
            dv_s[rows, :] = jnp.zeros((CHUNK, HEAD_SIZE), F32)
            return c

        lax.fori_loop(0, chunks, clear, 0)
        rows = pl.ds(row0, BLK)
        for hg in range(LOCAL_HEADS // GROUP):
            for i in range(GROUP):
                cols = pl.ds((hg * GROUP + i) * HEAD_SIZE, HEAD_SIZE)
                mine = pl.ds(i * BLK, BLK)
                q_blk = q_s[rows, cols]
                g_blk = grad_ref[rows, cols]
                qr_s[mine, :] = q_blk
                gr_s[mine, :] = g_blk
                qt_s[:, mine] = q_blk.astype(F32).T.astype(BF16)
                gt_s[:, mine] = g_blk.astype(F32).T.astype(BF16)

            def first_pass(ch, state):
                top, total, weighed = state
                rows_c = pl.ds(pl.multiple_of(ch * CHUNK, CHUNK), CHUNK)
                scores = dot(k_s[rows_c, :], qt_s[...])
                scores = scores + jnp.concatenate([bias_s[rows_c, :]] * GROUP, axis=1)
                new_top = jnp.maximum(top, jnp.max(scores, axis=0, keepdims=True))
                factor = jnp.exp2((top - new_top) * EXP2_SCALE)
                e = jnp.exp2((scores - new_top) * EXP2_SCALE)
                dp = dot(v_s[rows_c, :], gt_s[...])
                e_s[ch] = e
                dp_s[ch] = dp
                top_s[ch] = new_top
                total = total * factor + jnp.sum(e.reshape(-1, 8, LANES), axis=0)
                weighed = weighed * factor + jnp.sum((e * dp).reshape(-1, 8, LANES), axis=0)
                return (new_top, total, weighed)

            start = (
                jnp.full((1, LANES), NEG_FILL, F32),
                jnp.zeros((8, LANES), F32),
                jnp.zeros((8, LANES), F32),
            )
            top, total, weighed = lax.fori_loop(0, chunks, first_pass, start)
            inverse = 1.0 / jnp.sum(total, axis=0, keepdims=True)
            out_dot = jnp.sum(weighed, axis=0, keepdims=True) * inverse
            dqt_s[...] = jnp.zeros_like(dqt_s)

            def second_pass(ch, c):
                rows_c = pl.ds(pl.multiple_of(ch * CHUNK, CHUNK), CHUNK)
                factor = jnp.exp2((top_s[ch] - top) * EXP2_SCALE) * inverse
                weights = e_s[ch] * factor
                score_grad = (weights * (dp_s[ch] - out_dot)).astype(BF16)
                dv_s[rows_c, :] += dot(weights.astype(BF16), gr_s[...])
                dk_s[rows_c, :] += dot(score_grad, qr_s[...])
                dqt_s[...] += dot(kt_s[ch], score_grad)
                return c

            lax.fori_loop(0, chunks, second_pass, 0)
            for i in range(GROUP):
                cols = pl.ds((hg * GROUP + i) * HEAD_SIZE, HEAD_SIZE)
                dq_ref[rows, cols] = (dqt_s[:, i * BLK : (i + 1) * BLK] * SCALE).T.astype(BF16)

        def spread(n, c):
            src = pl.ds(pl.multiple_of(n * BLK, BLK), BLK)
            dst = pl.ds(pl.multiple_of((list_s[n] - 2 * base) * BLK, BLK), BLK)
            acc_s[0, dst, :] += dk_s[src, :]
            acc_s[1, dst, :] += dv_s[src, :]
            return c

        lax.fori_loop(0, count, spread, 0)
        return carry

    lax.fori_loop(0, 2, query_block, 0)

    @pl.when(core == 0)
    def _():
        keep_ref[...] = acc_s[0] * SCALE
        send_ref[...] = acc_s[1].astype(BF16)

    @pl.when(core == 1)
    def _():
        keep_ref[...] = acc_s[1]
        send_ref[...] = (acc_s[0] * SCALE).astype(BF16)


def merge_kernel(info_ref, keep_ref, recv_ref, out_ref):
    base = jnp.maximum(info_ref[0] - BACK, 0)
    out_ref[...] = jnp.zeros_like(out_ref)
    rows = pl.ds(pl.multiple_of(base * TOK, TOK), WINDOW * TOK)
    out_ref[rows, :] = (keep_ref[...] + recv_ref[...].astype(F32)).astype(BF16)


VMEM = pl.BlockSpec(memory_space=pltpu.VMEM)
SMEM = pl.BlockSpec(memory_space=pltpu.SMEM)


def call_attention(info, segments, allow, unpack, q_recv, g_local, kv_window):
    width = g_local.shape[1]
    return pl.pallas_call(
        attention_kernel,
        in_specs=[SMEM, SMEM, SMEM] + [VMEM] * 5,
        out_specs=[VMEM, VMEM, VMEM],
        out_shape=[
            jax.ShapeDtypeStruct((TOK, width), BF16),
            jax.ShapeDtypeStruct((WINDOW * TOK, HEAD_SIZE), F32),
            jax.ShapeDtypeStruct((WINDOW * TOK, HEAD_SIZE), BF16),
        ],
        scratch_shapes=[
            pltpu.VMEM((TOK, width), BF16),
            pltpu.VMEM((LANES, HEAD_SIZE), BF16),
            pltpu.VMEM((LANES, HEAD_SIZE), BF16),
            pltpu.VMEM((HEAD_SIZE, LANES), BF16),
            pltpu.VMEM((HEAD_SIZE, LANES), BF16),
            pltpu.VMEM((MOST_BLOCKS * BLK, HEAD_SIZE), BF16),
            pltpu.VMEM((MOST_BLOCKS * BLK, HEAD_SIZE), BF16),
            pltpu.VMEM((MOST_CHUNKS, HEAD_SIZE, CHUNK), BF16),
            pltpu.VMEM((MOST_BLOCKS * BLK, BLK), F32),
            pltpu.VMEM((MOST_CHUNKS, CHUNK, LANES), F32),
            pltpu.VMEM((MOST_CHUNKS, CHUNK, LANES), F32),
            pltpu.VMEM((MOST_CHUNKS, 1, LANES), F32),
            pltpu.VMEM((HEAD_SIZE, LANES), F32),
            pltpu.VMEM((MOST_BLOCKS * BLK, HEAD_SIZE), F32),
            pltpu.VMEM((MOST_BLOCKS * BLK, HEAD_SIZE), F32),
            pltpu.VMEM((2, WINDOW * TOK, HEAD_SIZE), F32),
            pltpu.SMEM((MOST_BLOCKS,), jnp.int32),
        ],
        compiler_params=pltpu.CompilerParams(vmem_limit_bytes=48 * 2**20),
        name="attention",
    )(info, segments, allow, segments.reshape(-1, BLK), unpack, q_recv, g_local, kv_window)


def on_device(queries, keys_values, out_grad, place, segments, allow):
    tp_index = lax.axis_index("tp")
    ctx_index = lax.axis_index("ctx")
    tp_size = lax.axis_size("tp")
    width = LOCAL_HEADS * HEAD_SIZE
    info = jnp.stack([ctx_index, tp_index % 2, tp_index // 2]).astype(jnp.int32)
    staged = pl.pallas_call(
        stage_kernel,
        grid_spec=pltpu.PrefetchScalarGridSpec(
            num_scalar_prefetch=1,
            grid=(1,),
            in_specs=[
                pl.BlockSpec((1, TOK), lambda i, info: (0, 0)),
                pl.BlockSpec((2, TOK, HEAD_SIZE), lambda i, info: (0, 0, info[2])),
            ],
            out_specs=pl.BlockSpec((TOK + META, 2 * HEAD_SIZE), lambda i, info: (0, 0)),
        ),
        out_shape=jax.ShapeDtypeStruct((TOK + META, 2 * HEAD_SIZE), BF16),
        name="stage",
    )(info, place.reshape(1, TOK), keys_values)
    beside = lax.ppermute(staged, "ctx", [(k, k ^ 1) for k in range(SHARDS)])
    own = jnp.stack([staged, beside])
    turn = []
    for k in range(SHARDS * tp_size):
        ctx, tp = k // tp_size, k % tp_size
        near = (ctx + (2 if tp % 2 == 0 else SHARDS - 2)) % SHARDS
        turn.append((k, near * tp_size + tp))
    swap = [(k, k ^ 1) for k in range(tp_size)]
    mine, theirs = [], []
    moving = own
    for step in range(1, RING + 1):
        if step == RING:
            moving = lax.dynamic_index_in_dim(moving, tp_index % 2, 0, keepdims=False)
        moving = lax.ppermute(moving, ("ctx", "tp"), turn)
        mine.append(moving)
        theirs.append(lax.ppermute(moving, "tp", swap))
    g_local = lax.all_to_all(out_grad, "tp", split_axis=1, concat_axis=0, tiled=True)
    q_send = pl.pallas_call(
        pack_kernel,
        in_specs=[VMEM, VMEM],
        out_specs=VMEM,
        out_shape=jax.ShapeDtypeStruct((SHARDS * SLOTS, width), BF16),
        name="pack",
    )(place.reshape(1, TOK), queries)
    q_recv = lax.all_to_all(q_send, "ctx", split_axis=0, concat_axis=0, tiled=True)
    kv_window, unpack = pl.pallas_call(
        permute_kernel,
        in_specs=[SMEM] + [VMEM] * (2 * RING + 1),
        out_specs=[VMEM, VMEM],
        out_shape=[
            jax.ShapeDtypeStruct((WINDOW * TOK, 2 * HEAD_SIZE), BF16),
            jax.ShapeDtypeStruct((SHARDS * SLOTS, TOK), BF16),
        ],
        compiler_params=pltpu.CompilerParams(vmem_limit_bytes=32 * 2**20),
        name="permute",
    )(info, own, *mine, *theirs)
    grad_q, keep, send = call_attention(
        info, segments, allow, unpack, q_recv, g_local, kv_window
    )
    recv = lax.ppermute(send, "tp", swap)
    part = pl.pallas_call(
        merge_kernel,
        in_specs=[SMEM, VMEM, VMEM],
        out_specs=VMEM,
        out_shape=jax.ShapeDtypeStruct((SHARDS * TOK, HEAD_SIZE), BF16),
        name="merge",
    )(info, keep, recv)
    parts = lax.all_to_all(
        part.reshape(SHARDS, TOK, HEAD_SIZE), "ctx", split_axis=0, concat_axis=0, tiled=True
    )
    owned = jnp.sum(parts.astype(F32), axis=0).astype(BF16)
    heads = lax.all_to_all(
        owned.reshape(tp_size, TOK // tp_size, HEAD_SIZE),
        "tp",
        split_axis=0,
        concat_axis=0,
        tiled=True,
    )
    key_value_gradient = (
        heads.reshape(KEY_VALUE_HEADS, 2, TOK // tp_size, HEAD_SIZE)
        .transpose(1, 2, 0, 3)
        .reshape(2, TOK // tp_size, KEY_VALUE_HEADS * HEAD_SIZE)
    )
    return (grad_q, key_value_gradient)


def solution(mesh):
    in_specs = (P("ctx", "tp"), P(None, "ctx", None), P(("ctx", "tp"), None), P("ctx"), P(), P())
    out_specs = (P("ctx", "tp"), P(None, ("ctx", "tp"), None))
    return jax.shard_map(
        on_device, mesh=mesh, in_specs=in_specs, out_specs=out_specs, check_vma=False
    )
```

```python
import functools
import math

import jax
import jax.numpy as jnp
from jax import lax
from jax.experimental import pallas as pl
from jax.experimental.pallas import tpu as pltpu
from jax.sharding import PartitionSpec as P

QUERY_HEAD_COUNT = 128
KEY_VALUE_HEADS = 8
HEAD_SIZE = 128
BLK = 128
TOK = 256
SHARDS = 16
SLOTS = 32
META = 16
Z_CHIPS = SHARDS // 2
RING = Z_CHIPS // 2
DOC_MOST = 2304
BACK = -(-DOC_MOST // TOK)
WINDOW = BACK + 1
BLOCKS_BACK = -(-DOC_MOST // BLK)
MOST_BLOCKS = 2 * ((BLOCKS_BACK + 2) // 2)
LOCAL_HEADS = 8
GROUP = 4
LANES = GROUP * BLK
CHUNK = 2 * BLK
MOST_CHUNKS = MOST_BLOCKS // 2
NEG_FILL = -1e30
SCALE = 1.0 / math.sqrt(HEAD_SIZE)
EXP2_SCALE = SCALE * math.log2(math.e)
F32 = jnp.float32
BF16 = jnp.bfloat16


def iota(shape, dim):
    return lax.broadcasted_iota(jnp.int32, shape, dim)


def dot(a, b):
    return jnp.dot(a, b, preferred_element_type=F32)


def ranks_within(member):
    earlier = (iota((TOK, TOK), 0) < iota((TOK, TOK), 1)).astype(F32).astype(BF16)
    counts = dot(member.astype(F32).astype(BF16), earlier)
    return jnp.where(member, counts, -1.0)


def pack_kernel(place_ref, rows_ref, out_ref):
    owner = place_ref[...] >> 8
    rank = ranks_within(owner == iota((SHARDS, TOK), 0))
    slot = iota((SLOTS, TOK), 0).astype(F32)
    picks = jnp.concatenate(
        [(rank[s : s + 1, :] == slot).astype(F32) for s in range(SHARDS)], axis=0
    ).astype(BF16)
    for first in range(0, rows_ref.shape[1], 256):
        cols = pl.ds(first, 256)
        out_ref[:, cols] = dot(picks, rows_ref[:, cols]).astype(BF16)


def stage_kernel(info_ref, place_ref, kv_ref, out_ref):
    place = place_ref[...]
    out_ref[:TOK, :HEAD_SIZE] = kv_ref[0]
    out_ref[:TOK, HEAD_SIZE:] = kv_ref[1]
    row = iota((META, TOK), 0)
    owner = jnp.broadcast_to((place >> 8).astype(F32), (META, TOK))
    within = jnp.broadcast_to((place & (TOK - 1)).astype(F32), (META, TOK))
    meta = jnp.where(row == 0, owner, jnp.where(row == 1, within, 0.0))
    out_ref[TOK:, :] = meta.astype(BF16)


def permute_kernel(info_ref, own_ref, *refs):
    mine, theirs = refs[:RING], refs[RING : 2 * RING]
    out_ref, unpack_ref = refs[2 * RING :]
    shard = info_ref[0]
    core = info_ref[1]
    base = jnp.maximum(shard - BACK, 0)
    z, x = shard // 2, shard % 2
    sources = [(own_ref.at[j], shard ^ j) for j in range(2)]
    for refs_k, side in ((mine, core), (theirs, 1 - core)):
        for k in range(1, RING):
            far = (z + k * (2 * side - 1) + Z_CHIPS) % Z_CHIPS
            sources += [(refs_k[k - 1].at[j], 2 * far + (x ^ j)) for j in range(2)]
        far = (z + RING) % Z_CHIPS
        sources += [(refs_k[RING - 1], 2 * far + (x ^ side))]
    owners = jnp.concatenate([ref[TOK : TOK + 1, :].astype(F32) for ref, _ in sources], axis=0)
    within = jnp.concatenate([ref[TOK + 1 : TOK + 2, :].astype(F32) for ref, _ in sources], axis=0)
    rank = ranks_within(owners == shard.astype(F32))
    slot = iota((SLOTS, TOK), 0).astype(F32)
    lane = iota((SLOTS, TOK), 1).astype(F32)
    for i, (_, source) in enumerate(sources):
        hit = rank[i : i + 1, :] == slot
        landing = jnp.sum(jnp.where(hit, within[i : i + 1, :] + 1.0, 0.0), axis=1, keepdims=True)
        rows = pl.ds(pl.multiple_of(source * SLOTS, SLOTS), SLOTS)
        unpack_ref[rows, :] = (landing == lane + 1.0).astype(F32).astype(BF16)

    def one_shard(i, carry):
        rows = iota((TOK, TOK), 0).astype(F32)
        goal = jnp.where(owners == (base + i).astype(F32), within, -1.0)
        total = jnp.zeros((TOK, 2 * HEAD_SIZE), F32)
        for n, (ref, _) in enumerate(sources):
            picks = (goal[n : n + 1, :] == rows).astype(F32).astype(BF16)
            total = total + dot(picks, ref[:TOK, :])
        out_ref[pl.ds(pl.multiple_of(i * TOK, TOK), TOK), :] = total.astype(BF16)
        return carry

    lax.fori_loop(0, shard - base + 1, one_shard, 0)


def attention_kernel(
    info_ref,
    seg_ref,
    allow_ref,
    segv_ref,
    unpack_ref,
    recv_ref,
    grad_ref,
    kv_ref,
    dq_ref,
    keep_ref,
    send_ref,
    q_s,
    qr_s,
    gr_s,
    qt_s,
    gt_s,
    k_s,
    v_s,
    kt_s,
    bias_s,
    e_s,
    dp_s,
    top_s,
    dqt_s,
    dk_s,
    dv_s,
    acc_s,
    list_s,
):
    shard = info_ref[0]
    core = info_ref[1]
    base = jnp.maximum(shard - BACK, 0)
    acc_s[...] = jnp.zeros_like(acc_s)
    for first in range(0, LOCAL_HEADS * HEAD_SIZE, 256):
        cols = pl.ds(first, 256)
        q_s[:, cols] = lax.dot_general(
            unpack_ref[...],
            recv_ref[:, cols],
            (((0,), (0,)), ((), ())),
            preferred_element_type=F32,
        ).astype(BF16)

    def query_block(half, carry):
        qb = shard * 2 + half
        row0 = pl.multiple_of(half * BLK, BLK)
        q_seg = segv_ref[pl.ds(qb, 1), :]
        q_first = seg_ref[qb * BLK]

        def scan(kb, count):
            seen = jnp.logical_and(
                seg_ref[kb * BLK + BLK - 1] >= q_first, allow_ref[qb, kb] != 0
            )

            @pl.when(seen)
            def _():
                list_s[count] = kb
                src = pl.ds(pl.multiple_of((kb - 2 * base) * BLK, BLK), BLK)
                dst = pl.ds(pl.multiple_of(count * BLK, BLK), BLK)
                k_blk = kv_ref[src, :HEAD_SIZE]
                k_s[dst, :] = k_blk
                v_s[dst, :] = kv_ref[src, HEAD_SIZE:]
                lanes = pl.ds(pl.multiple_of((count % 2) * BLK, BLK), BLK)
                kt_s[count // 2, :, lanes] = k_blk.astype(F32).T.astype(BF16)
                k_seg = jnp.broadcast_to(segv_ref[pl.ds(kb, 1), :].astype(F32), (BLK, BLK)).T
                k_pos = kb * BLK + iota((BLK, BLK), 0)
                q_pos = qb * BLK + iota((BLK, BLK), 1)
                ok = (k_seg == q_seg.astype(F32)) & (k_pos <= q_pos)
                bias_s[dst, :] = jnp.where(ok, 0.0, NEG_FILL)

            return count + seen.astype(jnp.int32)

        count = lax.fori_loop(jnp.maximum(qb - BLOCKS_BACK, 0), qb + 1, scan, 0)

        @pl.when(count % 2 == 1)
        def _():
            dst = pl.ds(pl.multiple_of(count * BLK, BLK), BLK)
            k_s[dst, :] = jnp.zeros((BLK, HEAD_SIZE), BF16)
            v_s[dst, :] = jnp.zeros((BLK, HEAD_SIZE), BF16)
            kt_s[count // 2, :, BLK:] = jnp.zeros((HEAD_SIZE, BLK), BF16)
            bias_s[dst, :] = jnp.full((BLK, BLK), NEG_FILL, F32)

        chunks = (count + 1) // 2

        def clear(ch, c):
            rows = pl.ds(pl.multiple_of(ch * CHUNK, CHUNK), CHUNK)
            dk_s[rows, :] = jnp.zeros((CHUNK, HEAD_SIZE), F32)
            dv_s[rows, :] = jnp.zeros((CHUNK, HEAD_SIZE), F32)
            return c

        lax.fori_loop(0, chunks, clear, 0)
        rows = pl.ds(row0, BLK)
        for hg in range(LOCAL_HEADS // GROUP):
            for i in range(GROUP):
                cols = pl.ds((hg * GROUP + i) * HEAD_SIZE, HEAD_SIZE)
                mine = pl.ds(i * BLK, BLK)
                q_blk = q_s[rows, cols]
                g_blk = grad_ref[rows, cols]
                qr_s[mine, :] = q_blk
                gr_s[mine, :] = g_blk
                qt_s[:, mine] = q_blk.astype(F32).T.astype(BF16)
                gt_s[:, mine] = g_blk.astype(F32).T.astype(BF16)

            def first_pass(ch, state):
                top, total, weighed = state
                rows_c = pl.ds(pl.multiple_of(ch * CHUNK, CHUNK), CHUNK)
                scores = dot(k_s[rows_c, :], qt_s[...])
                scores = scores + jnp.concatenate([bias_s[rows_c, :]] * GROUP, axis=1)
                new_top = jnp.maximum(top, jnp.max(scores, axis=0, keepdims=True))
                factor = jnp.exp2((top - new_top) * EXP2_SCALE)
                e = jnp.exp2((scores - new_top) * EXP2_SCALE)
                dp = dot(v_s[rows_c, :], gt_s[...])
                e_s[ch] = e
                dp_s[ch] = dp
                top_s[ch] = new_top
                total = total * factor + jnp.sum(e.reshape(-1, 8, LANES), axis=0)
                weighed = weighed * factor + jnp.sum((e * dp).reshape(-1, 8, LANES), axis=0)
                return (new_top, total, weighed)

            start = (
                jnp.full((1, LANES), NEG_FILL, F32),
                jnp.zeros((8, LANES), F32),
                jnp.zeros((8, LANES), F32),
            )
            top, total, weighed = lax.fori_loop(0, chunks, first_pass, start)
            inverse = 1.0 / jnp.sum(total, axis=0, keepdims=True)
            out_dot = jnp.sum(weighed, axis=0, keepdims=True) * inverse
            dqt_s[...] = jnp.zeros_like(dqt_s)

            def second_pass(ch, c):
                rows_c = pl.ds(pl.multiple_of(ch * CHUNK, CHUNK), CHUNK)
                factor = jnp.exp2((top_s[ch] - top) * EXP2_SCALE) * inverse
                weights = e_s[ch] * factor
                score_grad = (weights * (dp_s[ch] - out_dot)).astype(BF16)
                dv_s[rows_c, :] += dot(weights.astype(BF16), gr_s[...])
                dk_s[rows_c, :] += dot(score_grad, qr_s[...])
                dqt_s[...] += dot(kt_s[ch], score_grad)
                return c

            lax.fori_loop(0, chunks, second_pass, 0)
            for i in range(GROUP):
                cols = pl.ds((hg * GROUP + i) * HEAD_SIZE, HEAD_SIZE)
                dq_ref[rows, cols] = (dqt_s[:, i * BLK : (i + 1) * BLK] * SCALE).T.astype(BF16)

        def spread(n, c):
            src = pl.ds(pl.multiple_of(n * BLK, BLK), BLK)
            dst = pl.ds(pl.multiple_of((list_s[n] - 2 * base) * BLK, BLK), BLK)
            acc_s[0, dst, :] += dk_s[src, :]
            acc_s[1, dst, :] += dv_s[src, :]
            return c

        lax.fori_loop(0, count, spread, 0)
        return carry

    lax.fori_loop(0, 2, query_block, 0)

    @pl.when(core == 0)
    def _():
        keep_ref[...] = acc_s[0] * SCALE
        send_ref[...] = acc_s[1].astype(BF16)

    @pl.when(core == 1)
    def _():
        keep_ref[...] = acc_s[1]
        send_ref[...] = (acc_s[0] * SCALE).astype(BF16)


def merge_kernel(info_ref, keep_ref, recv_ref, out_ref):
    base = jnp.maximum(info_ref[0] - BACK, 0)
    out_ref[...] = jnp.zeros_like(out_ref)
    rows = pl.ds(pl.multiple_of(base * TOK, TOK), WINDOW * TOK)
    out_ref[rows, :] = (keep_ref[...] + recv_ref[...].astype(F32)).astype(BF16)


VMEM = pl.BlockSpec(memory_space=pltpu.VMEM)
SMEM = pl.BlockSpec(memory_space=pltpu.SMEM)


def call_attention(info, segments, allow, unpack, q_recv, g_local, kv_window):
    width = g_local.shape[1]
    return pl.pallas_call(
        attention_kernel,
        in_specs=[SMEM, SMEM, SMEM] + [VMEM] * 5,
        out_specs=[VMEM, VMEM, VMEM],
        out_shape=[
            jax.ShapeDtypeStruct((TOK, width), BF16),
            jax.ShapeDtypeStruct((WINDOW * TOK, HEAD_SIZE), F32),
            jax.ShapeDtypeStruct((WINDOW * TOK, HEAD_SIZE), BF16),
        ],
        scratch_shapes=[
            pltpu.VMEM((TOK, width), BF16),
            pltpu.VMEM((LANES, HEAD_SIZE), BF16),
            pltpu.VMEM((LANES, HEAD_SIZE), BF16),
            pltpu.VMEM((HEAD_SIZE, LANES), BF16),
            pltpu.VMEM((HEAD_SIZE, LANES), BF16),
            pltpu.VMEM((MOST_BLOCKS * BLK, HEAD_SIZE), BF16),
            pltpu.VMEM((MOST_BLOCKS * BLK, HEAD_SIZE), BF16),
            pltpu.VMEM((MOST_CHUNKS, HEAD_SIZE, CHUNK), BF16),
            pltpu.VMEM((MOST_BLOCKS * BLK, BLK), F32),
            pltpu.VMEM((MOST_CHUNKS, CHUNK, LANES), F32),
            pltpu.VMEM((MOST_CHUNKS, CHUNK, LANES), F32),
            pltpu.VMEM((MOST_CHUNKS, 1, LANES), F32),
            pltpu.VMEM((HEAD_SIZE, LANES), F32),
            pltpu.VMEM((MOST_BLOCKS * BLK, HEAD_SIZE), F32),
            pltpu.VMEM((MOST_BLOCKS * BLK, HEAD_SIZE), F32),
            pltpu.VMEM((2, WINDOW * TOK, HEAD_SIZE), F32),
            pltpu.SMEM((MOST_BLOCKS,), jnp.int32),
        ],
        compiler_params=pltpu.CompilerParams(vmem_limit_bytes=48 * 2**20),
        name="attention",
    )(info, segments, allow, segments.reshape(-1, BLK), unpack, q_recv, g_local, kv_window)


def on_device(queries, keys_values, out_grad, place, segments, allow):
    tp_index = lax.axis_index("tp")
    ctx_index = lax.axis_index("ctx")
    tp_size = lax.axis_size("tp")
    width = LOCAL_HEADS * HEAD_SIZE
    info = jnp.stack([ctx_index, tp_index % 2, tp_index // 2]).astype(jnp.int32)
    staged = pl.pallas_call(
        stage_kernel,
        grid_spec=pltpu.PrefetchScalarGridSpec(
            num_scalar_prefetch=1,
            grid=(1,),
            in_specs=[
                pl.BlockSpec((1, TOK), lambda i, info: (0, 0)),
                pl.BlockSpec((2, TOK, HEAD_SIZE), lambda i, info: (0, 0, info[2])),
            ],
            out_specs=pl.BlockSpec((TOK + META, 2 * HEAD_SIZE), lambda i, info: (0, 0)),
        ),
        out_shape=jax.ShapeDtypeStruct((TOK + META, 2 * HEAD_SIZE), BF16),
        name="stage",
    )(info, place.reshape(1, TOK), keys_values)
    beside = lax.ppermute(staged, "ctx", [(k, k ^ 1) for k in range(SHARDS)])
    own = jnp.stack([staged, beside])
    turn = []
    for k in range(SHARDS * tp_size):
        ctx, tp = k // tp_size, k % tp_size
        near = (ctx + (2 if tp % 2 == 0 else SHARDS - 2)) % SHARDS
        turn.append((k, near * tp_size + tp))
    swap = [(k, k ^ 1) for k in range(tp_size)]
    mine, theirs = [], []
    moving = own
    for step in range(1, RING + 1):
        if step == RING:
            moving = lax.dynamic_index_in_dim(moving, tp_index % 2, 0, keepdims=False)
        moving = lax.ppermute(moving, ("ctx", "tp"), turn)
        if step == 2:
            moving, queries = lax.optimization_barrier((moving, queries))
        mine.append(moving)
        theirs.append(lax.ppermute(moving, "tp", swap))
    g_local = lax.all_to_all(out_grad, "tp", split_axis=1, concat_axis=0, tiled=True)
    q_send = pl.pallas_call(
        pack_kernel,
        in_specs=[VMEM, VMEM],
        out_specs=VMEM,
        out_shape=jax.ShapeDtypeStruct((SHARDS * SLOTS, width), BF16),
        name="pack",
    )(place.reshape(1, TOK), queries)
    q_recv = lax.all_to_all(q_send, "ctx", split_axis=0, concat_axis=0, tiled=True)
    kv_window, unpack = pl.pallas_call(
        permute_kernel,
        in_specs=[SMEM] + [VMEM] * (2 * RING + 1),
        out_specs=[VMEM, VMEM],
        out_shape=[
            jax.ShapeDtypeStruct((WINDOW * TOK, 2 * HEAD_SIZE), BF16),
            jax.ShapeDtypeStruct((SHARDS * SLOTS, TOK), BF16),
        ],
        compiler_params=pltpu.CompilerParams(vmem_limit_bytes=32 * 2**20),
        name="permute",
    )(info, own, *mine, *theirs)
    grad_q, keep, send = call_attention(
        info, segments, allow, unpack, q_recv, g_local, kv_window
    )
    recv = lax.ppermute(send, "tp", swap)
    part = pl.pallas_call(
        merge_kernel,
        in_specs=[SMEM, VMEM, VMEM],
        out_specs=VMEM,
        out_shape=jax.ShapeDtypeStruct((SHARDS * TOK, HEAD_SIZE), BF16),
        name="merge",
    )(info, keep, recv)
    parts = lax.all_to_all(
        part.reshape(SHARDS, TOK, HEAD_SIZE), "ctx", split_axis=0, concat_axis=0, tiled=True
    )
    owned = jnp.sum(parts.astype(F32), axis=0).astype(BF16)
    heads = lax.all_to_all(
        owned.reshape(tp_size, TOK // tp_size, HEAD_SIZE),
        "tp",
        split_axis=0,
        concat_axis=0,
        tiled=True,
    )
    key_value_gradient = (
        heads.reshape(KEY_VALUE_HEADS, 2, TOK // tp_size, HEAD_SIZE)
        .transpose(1, 2, 0, 3)
        .reshape(2, TOK // tp_size, KEY_VALUE_HEADS * HEAD_SIZE)
    )
    return (grad_q, key_value_gradient)


def solution(mesh):
    in_specs = (P("ctx", "tp"), P(None, "ctx", None), P(("ctx", "tp"), None), P("ctx"), P(), P())
    out_specs = (P("ctx", "tp"), P(None, ("ctx", "tp"), None))
    return jax.shard_map(
        on_device, mesh=mesh, in_specs=in_specs, out_specs=out_specs, check_vma=False
    )
```

```python
import functools
import math

import jax
import jax.numpy as jnp
from jax import lax
from jax.experimental import pallas as pl
from jax.experimental.pallas import tpu as pltpu
from jax.sharding import PartitionSpec as P

QUERY_HEAD_COUNT = 128
KEY_VALUE_HEADS = 8
HEAD_SIZE = 128
BLK = 128
TOK = 256
SHARDS = 16
SLOTS = 32
META = 16
Z_CHIPS = SHARDS // 2
RING = Z_CHIPS // 2
DOC_MOST = 2304
BACK = -(-DOC_MOST // TOK)
WINDOW = BACK + 1
BLOCKS_BACK = -(-DOC_MOST // BLK)
MOST_BLOCKS = 2 * ((BLOCKS_BACK + 2) // 2)
LOCAL_HEADS = 8
GROUP = 4
LANES = GROUP * BLK
CHUNK = 2 * BLK
MOST_CHUNKS = MOST_BLOCKS // 2
NEG_FILL = -1e30
SCALE = 1.0 / math.sqrt(HEAD_SIZE)
EXP2_SCALE = SCALE * math.log2(math.e)
F32 = jnp.float32
BF16 = jnp.bfloat16


def iota(shape, dim):
    return lax.broadcasted_iota(jnp.int32, shape, dim)


def dot(a, b):
    return jnp.dot(a, b, preferred_element_type=F32)


def ranks_within(member):
    earlier = (iota((TOK, TOK), 0) < iota((TOK, TOK), 1)).astype(F32).astype(BF16)
    counts = dot(member.astype(F32).astype(BF16), earlier)
    return jnp.where(member, counts, -1.0)


def pack_kernel(place_ref, rows_ref, out_ref):
    owner = place_ref[...] >> 8
    rank = ranks_within(owner == iota((SHARDS, TOK), 0))
    slot = iota((SLOTS, TOK), 0).astype(F32)
    picks = jnp.concatenate(
        [(rank[s : s + 1, :] == slot).astype(F32) for s in range(SHARDS)], axis=0
    ).astype(BF16)
    for first in range(0, rows_ref.shape[1], 256):
        cols = pl.ds(first, 256)
        out_ref[:, cols] = dot(picks, rows_ref[:, cols]).astype(BF16)


def stage_kernel(place_ref, kv_ref, out_ref, arrived):
    cols = pl.ds(pl.multiple_of((lax.axis_index("tp") // 2) * HEAD_SIZE, HEAD_SIZE), HEAD_SIZE)
    copies = [
        pltpu.make_async_copy(
            kv_ref.at[i, :, cols],
            out_ref.at[pl.ds(0, TOK), pl.ds(i * HEAD_SIZE, HEAD_SIZE)],
            arrived.at[i],
        )
        for i in range(2)
    ]
    for copy in copies:
        copy.start()
    place = place_ref[...]
    row = iota((META, TOK), 0)
    owner = jnp.broadcast_to((place >> 8).astype(F32), (META, TOK))
    within = jnp.broadcast_to((place & (TOK - 1)).astype(F32), (META, TOK))
    meta = jnp.where(row == 0, owner, jnp.where(row == 1, within, 0.0))
    out_ref[TOK:, :] = meta.astype(BF16)
    for copy in copies:
        copy.wait()


def permute_kernel(info_ref, own_ref, *refs):
    mine, theirs = refs[:RING], refs[RING : 2 * RING]
    out_ref, unpack_ref = refs[2 * RING :]
    shard = info_ref[0]
    core = info_ref[1]
    base = jnp.maximum(shard - BACK, 0)
    z, x = shard // 2, shard % 2
    sources = [(own_ref.at[j], shard ^ j) for j in range(2)]
    for refs_k, side in ((mine, core), (theirs, 1 - core)):
        for k in range(1, RING):
            far = (z + k * (2 * side - 1) + Z_CHIPS) % Z_CHIPS
            sources += [(refs_k[k - 1].at[j], 2 * far + (x ^ j)) for j in range(2)]
        far = (z + RING) % Z_CHIPS
        sources += [(refs_k[RING - 1], 2 * far + (x ^ side))]
    owners = jnp.concatenate([ref[TOK : TOK + 1, :].astype(F32) for ref, _ in sources], axis=0)
    within = jnp.concatenate([ref[TOK + 1 : TOK + 2, :].astype(F32) for ref, _ in sources], axis=0)
    rank = ranks_within(owners == shard.astype(F32))
    slot = iota((SLOTS, TOK), 0).astype(F32)
    lane = iota((SLOTS, TOK), 1).astype(F32)
    for i, (_, source) in enumerate(sources):
        hit = rank[i : i + 1, :] == slot
        landing = jnp.sum(jnp.where(hit, within[i : i + 1, :] + 1.0, 0.0), axis=1, keepdims=True)
        rows = pl.ds(pl.multiple_of(source * SLOTS, SLOTS), SLOTS)
        unpack_ref[rows, :] = (landing == lane + 1.0).astype(F32).astype(BF16)

    def one_shard(i, carry):
        rows = iota((TOK, TOK), 0).astype(F32)
        goal = jnp.where(owners == (base + i).astype(F32), within, -1.0)
        total = jnp.zeros((TOK, 2 * HEAD_SIZE), F32)
        for n, (ref, _) in enumerate(sources):
            picks = (goal[n : n + 1, :] == rows).astype(F32).astype(BF16)
            total = total + dot(picks, ref[:TOK, :])
        out_ref[pl.ds(pl.multiple_of(i * TOK, TOK), TOK), :] = total.astype(BF16)
        return carry

    lax.fori_loop(0, shard - base + 1, one_shard, 0)


def attention_kernel(
    info_ref,
    seg_ref,
    allow_ref,
    segv_ref,
    unpack_ref,
    recv_ref,
    grad_ref,
    kv_ref,
    dq_ref,
    keep_ref,
    send_ref,
    q_s,
    qr_s,
    gr_s,
    qt_s,
    gt_s,
    k_s,
    v_s,
    kt_s,
    bias_s,
    e_s,
    dp_s,
    top_s,
    dqt_s,
    dk_s,
    dv_s,
    acc_s,
    list_s,
):
    shard = info_ref[0]
    core = info_ref[1]
    base = jnp.maximum(shard - BACK, 0)
    acc_s[...] = jnp.zeros_like(acc_s)
    for first in range(0, LOCAL_HEADS * HEAD_SIZE, 256):
        cols = pl.ds(first, 256)
        q_s[:, cols] = lax.dot_general(
            unpack_ref[...],
            recv_ref[:, cols],
            (((0,), (0,)), ((), ())),
            preferred_element_type=F32,
        ).astype(BF16)

    def query_block(half, carry):
        qb = shard * 2 + half
        row0 = pl.multiple_of(half * BLK, BLK)
        q_seg = segv_ref[pl.ds(qb, 1), :]
        q_first = seg_ref[qb * BLK]

        def scan(kb, count):
            seen = jnp.logical_and(
                seg_ref[kb * BLK + BLK - 1] >= q_first, allow_ref[qb, kb] != 0
            )

            @pl.when(seen)
            def _():
                list_s[count] = kb
                src = pl.ds(pl.multiple_of((kb - 2 * base) * BLK, BLK), BLK)
                dst = pl.ds(pl.multiple_of(count * BLK, BLK), BLK)
                k_blk = kv_ref[src, :HEAD_SIZE]
                k_s[dst, :] = k_blk
                v_s[dst, :] = kv_ref[src, HEAD_SIZE:]
                lanes = pl.ds(pl.multiple_of((count % 2) * BLK, BLK), BLK)
                kt_s[count // 2, :, lanes] = k_blk.astype(F32).T.astype(BF16)
                k_seg = jnp.broadcast_to(segv_ref[pl.ds(kb, 1), :].astype(F32), (BLK, BLK)).T
                k_pos = kb * BLK + iota((BLK, BLK), 0)
                q_pos = qb * BLK + iota((BLK, BLK), 1)
                ok = (k_seg == q_seg.astype(F32)) & (k_pos <= q_pos)
                bias_s[dst, :] = jnp.where(ok, 0.0, NEG_FILL)

            return count + seen.astype(jnp.int32)

        count = lax.fori_loop(jnp.maximum(qb - BLOCKS_BACK, 0), qb + 1, scan, 0)

        @pl.when(count % 2 == 1)
        def _():
            dst = pl.ds(pl.multiple_of(count * BLK, BLK), BLK)
            k_s[dst, :] = jnp.zeros((BLK, HEAD_SIZE), BF16)
            v_s[dst, :] = jnp.zeros((BLK, HEAD_SIZE), BF16)
            kt_s[count // 2, :, BLK:] = jnp.zeros((HEAD_SIZE, BLK), BF16)
            bias_s[dst, :] = jnp.full((BLK, BLK), NEG_FILL, F32)

        chunks = (count + 1) // 2

        def clear(ch, c):
            rows = pl.ds(pl.multiple_of(ch * CHUNK, CHUNK), CHUNK)
            dk_s[rows, :] = jnp.zeros((CHUNK, HEAD_SIZE), F32)
            dv_s[rows, :] = jnp.zeros((CHUNK, HEAD_SIZE), F32)
            return c

        lax.fori_loop(0, chunks, clear, 0)
        rows = pl.ds(row0, BLK)
        for hg in range(LOCAL_HEADS // GROUP):
            for i in range(GROUP):
                cols = pl.ds((hg * GROUP + i) * HEAD_SIZE, HEAD_SIZE)
                mine = pl.ds(i * BLK, BLK)
                q_blk = q_s[rows, cols]
                g_blk = grad_ref[rows, cols]
                qr_s[mine, :] = q_blk
                gr_s[mine, :] = g_blk
                qt_s[:, mine] = q_blk.astype(F32).T.astype(BF16)
                gt_s[:, mine] = g_blk.astype(F32).T.astype(BF16)

            def first_pass(ch, state):
                top, total, weighed = state
                rows_c = pl.ds(pl.multiple_of(ch * CHUNK, CHUNK), CHUNK)
                scores = dot(k_s[rows_c, :], qt_s[...])
                scores = scores + jnp.concatenate([bias_s[rows_c, :]] * GROUP, axis=1)
                new_top = jnp.maximum(top, jnp.max(scores, axis=0, keepdims=True))
                factor = jnp.exp2((top - new_top) * EXP2_SCALE)
                e = jnp.exp2((scores - new_top) * EXP2_SCALE)
                dp = dot(v_s[rows_c, :], gt_s[...])
                e_s[ch] = e
                dp_s[ch] = dp
                top_s[ch] = new_top
                total = total * factor + jnp.sum(e.reshape(-1, 8, LANES), axis=0)
                weighed = weighed * factor + jnp.sum((e * dp).reshape(-1, 8, LANES), axis=0)
                return (new_top, total, weighed)

            start = (
                jnp.full((1, LANES), NEG_FILL, F32),
                jnp.zeros((8, LANES), F32),
                jnp.zeros((8, LANES), F32),
            )
            top, total, weighed = lax.fori_loop(0, chunks, first_pass, start)
            inverse = 1.0 / jnp.sum(total, axis=0, keepdims=True)
            out_dot = jnp.sum(weighed, axis=0, keepdims=True) * inverse
            dqt_s[...] = jnp.zeros_like(dqt_s)

            def second_pass(ch, c):
                rows_c = pl.ds(pl.multiple_of(ch * CHUNK, CHUNK), CHUNK)
                factor = jnp.exp2((top_s[ch] - top) * EXP2_SCALE) * inverse
                weights = e_s[ch] * factor
                score_grad = (weights * (dp_s[ch] - out_dot)).astype(BF16)
                dv_s[rows_c, :] += dot(weights.astype(BF16), gr_s[...])
                dk_s[rows_c, :] += dot(score_grad, qr_s[...])
                dqt_s[...] += dot(kt_s[ch], score_grad)
                return c

            lax.fori_loop(0, chunks, second_pass, 0)
            for i in range(GROUP):
                cols = pl.ds((hg * GROUP + i) * HEAD_SIZE, HEAD_SIZE)
                dq_ref[rows, cols] = (dqt_s[:, i * BLK : (i + 1) * BLK] * SCALE).T.astype(BF16)

        def spread(n, c):
            src = pl.ds(pl.multiple_of(n * BLK, BLK), BLK)
            dst = pl.ds(pl.multiple_of((list_s[n] - 2 * base) * BLK, BLK), BLK)
            acc_s[0, dst, :] += dk_s[src, :]
            acc_s[1, dst, :] += dv_s[src, :]
            return c

        lax.fori_loop(0, count, spread, 0)
        return carry

    lax.fori_loop(0, 2, query_block, 0)

    @pl.when(core == 0)
    def _():
        keep_ref[...] = acc_s[0] * SCALE
        send_ref[...] = acc_s[1].astype(BF16)

    @pl.when(core == 1)
    def _():
        keep_ref[...] = acc_s[1]
        send_ref[...] = (acc_s[0] * SCALE).astype(BF16)


def merge_kernel(info_ref, keep_ref, recv_ref, out_ref):
    base = jnp.maximum(info_ref[0] - BACK, 0)
    out_ref[...] = jnp.zeros_like(out_ref)
    rows = pl.ds(pl.multiple_of(base * TOK, TOK), WINDOW * TOK)
    out_ref[rows, :] = (keep_ref[...] + recv_ref[...].astype(F32)).astype(BF16)


VMEM = pl.BlockSpec(memory_space=pltpu.VMEM)
SMEM = pl.BlockSpec(memory_space=pltpu.SMEM)


def call_attention(info, segments, allow, unpack, q_recv, g_local, kv_window):
    width = g_local.shape[1]
    return pl.pallas_call(
        attention_kernel,
        in_specs=[SMEM, SMEM, SMEM] + [VMEM] * 5,
        out_specs=[VMEM, VMEM, VMEM],
        out_shape=[
            jax.ShapeDtypeStruct((TOK, width), BF16),
            jax.ShapeDtypeStruct((WINDOW * TOK, HEAD_SIZE), F32),
            jax.ShapeDtypeStruct((WINDOW * TOK, HEAD_SIZE), BF16),
        ],
        scratch_shapes=[
            pltpu.VMEM((TOK, width), BF16),
            pltpu.VMEM((LANES, HEAD_SIZE), BF16),
            pltpu.VMEM((LANES, HEAD_SIZE), BF16),
            pltpu.VMEM((HEAD_SIZE, LANES), BF16),
            pltpu.VMEM((HEAD_SIZE, LANES), BF16),
            pltpu.VMEM((MOST_BLOCKS * BLK, HEAD_SIZE), BF16),
            pltpu.VMEM((MOST_BLOCKS * BLK, HEAD_SIZE), BF16),
            pltpu.VMEM((MOST_CHUNKS, HEAD_SIZE, CHUNK), BF16),
            pltpu.VMEM((MOST_BLOCKS * BLK, BLK), F32),
            pltpu.VMEM((MOST_CHUNKS, CHUNK, LANES), F32),
            pltpu.VMEM((MOST_CHUNKS, CHUNK, LANES), F32),
            pltpu.VMEM((MOST_CHUNKS, 1, LANES), F32),
            pltpu.VMEM((HEAD_SIZE, LANES), F32),
            pltpu.VMEM((MOST_BLOCKS * BLK, HEAD_SIZE), F32),
            pltpu.VMEM((MOST_BLOCKS * BLK, HEAD_SIZE), F32),
            pltpu.VMEM((2, WINDOW * TOK, HEAD_SIZE), F32),
            pltpu.SMEM((MOST_BLOCKS,), jnp.int32),
        ],
        compiler_params=pltpu.CompilerParams(vmem_limit_bytes=48 * 2**20),
        name="attention",
    )(info, segments, allow, segments.reshape(-1, BLK), unpack, q_recv, g_local, kv_window)


def on_device(queries, keys_values, out_grad, place, segments, allow):
    tp_index = lax.axis_index("tp")
    ctx_index = lax.axis_index("ctx")
    tp_size = lax.axis_size("tp")
    width = LOCAL_HEADS * HEAD_SIZE
    info = jnp.stack([ctx_index, tp_index % 2]).astype(jnp.int32)
    staged = pl.pallas_call(
        stage_kernel,
        in_specs=[VMEM, pl.BlockSpec(memory_space=pl.ANY)],
        out_specs=VMEM,
        out_shape=jax.ShapeDtypeStruct((TOK + META, 2 * HEAD_SIZE), BF16),
        scratch_shapes=[pltpu.SemaphoreType.DMA((2,))],
        name="stage",
    )(place.reshape(1, TOK), keys_values)
    beside = lax.ppermute(staged, "ctx", [(k, k ^ 1) for k in range(SHARDS)])
    own = jnp.stack([staged, beside])

    def around(hops):
        pairs = []
        for k in range(SHARDS * tp_size):
            ctx, tp = k // tp_size, k % tp_size
            far = (ctx + (2 * hops if tp % 2 == 0 else -2 * hops)) % SHARDS
            pairs.append((k, far * tp_size + tp))
        return pairs

    swap = [(k, k ^ 1) for k in range(tp_size)]
    first = lax.ppermute(own, ("ctx", "tp"), around(1))
    second = lax.ppermute(first, ("ctx", "tp"), around(1))
    third = lax.ppermute(second, ("ctx", "tp"), around(1))
    half = lax.dynamic_index_in_dim(second, tp_index % 2, 0, keepdims=False)
    fourth = lax.ppermute(half, ("ctx", "tp"), around(2))
    mine = [first, second, third, fourth]
    theirs = [lax.ppermute(piece, "tp", swap) for piece in mine]
    g_local = lax.all_to_all(out_grad, "tp", split_axis=1, concat_axis=0, tiled=True)
    q_send = pl.pallas_call(
        pack_kernel,
        in_specs=[VMEM, VMEM],
        out_specs=VMEM,
        out_shape=jax.ShapeDtypeStruct((SHARDS * SLOTS, width), BF16),
        name="pack",
    )(place.reshape(1, TOK), queries)
    q_send, theirs[1] = lax.optimization_barrier((q_send, theirs[1]))
    q_recv = lax.all_to_all(q_send, "ctx", split_axis=0, concat_axis=0, tiled=True)
    kv_window, unpack = pl.pallas_call(
        permute_kernel,
        in_specs=[SMEM] + [VMEM] * (2 * RING + 1),
        out_specs=[VMEM, VMEM],
        out_shape=[
            jax.ShapeDtypeStruct((WINDOW * TOK, 2 * HEAD_SIZE), BF16),
            jax.ShapeDtypeStruct((SHARDS * SLOTS, TOK), BF16),
        ],
        compiler_params=pltpu.CompilerParams(vmem_limit_bytes=32 * 2**20),
        name="permute",
    )(info, own, *mine, *theirs)
    grad_q, keep, send = call_attention(
        info, segments, allow, unpack, q_recv, g_local, kv_window
    )
    recv = lax.ppermute(send, "tp", swap)
    part = pl.pallas_call(
        merge_kernel,
        in_specs=[SMEM, VMEM, VMEM],
        out_specs=VMEM,
        out_shape=jax.ShapeDtypeStruct((SHARDS * TOK, HEAD_SIZE), BF16),
        name="merge",
    )(info, keep, recv)
    parts = lax.all_to_all(
        part.reshape(SHARDS, TOK, HEAD_SIZE), "ctx", split_axis=0, concat_axis=0, tiled=True
    )
    owned = jnp.sum(parts.astype(F32), axis=0).astype(BF16)
    heads = lax.all_to_all(
        owned.reshape(tp_size, TOK // tp_size, HEAD_SIZE),
        "tp",
        split_axis=0,
        concat_axis=0,
        tiled=True,
    )
    key_value_gradient = (
        heads.reshape(KEY_VALUE_HEADS, 2, TOK // tp_size, HEAD_SIZE)
        .transpose(1, 2, 0, 3)
        .reshape(2, TOK // tp_size, KEY_VALUE_HEADS * HEAD_SIZE)
    )
    return (grad_q, key_value_gradient)


def solution(mesh):
    in_specs = (P("ctx", "tp"), P(None, "ctx", None), P(("ctx", "tp"), None), P("ctx"), P(), P())
    out_specs = (P("ctx", "tp"), P(None, ("ctx", "tp"), None))
    return jax.shard_map(
        on_device, mesh=mesh, in_specs=in_specs, out_specs=out_specs, check_vma=False
    )
```

```python
import functools
import math

import jax
import jax.numpy as jnp
from jax import lax
from jax.experimental import pallas as pl
from jax.experimental.pallas import tpu as pltpu
from jax.sharding import PartitionSpec as P

QUERY_HEAD_COUNT = 128
KEY_VALUE_HEADS = 8
HEAD_SIZE = 128
BLK = 128
TOK = 256
SHARDS = 16
SLOTS = 32
META = 16
Z_CHIPS = SHARDS // 2
RING = Z_CHIPS // 2
DOC_MOST = 2304
BACK = -(-DOC_MOST // TOK)
WINDOW = BACK + 1
BLOCKS_BACK = -(-DOC_MOST // BLK)
MOST_BLOCKS = 2 * ((BLOCKS_BACK + 2) // 2)
LOCAL_HEADS = 8
GROUP = 4
LANES = GROUP * BLK
CHUNK = 2 * BLK
MOST_CHUNKS = MOST_BLOCKS // 2
NEG_FILL = -1e30
SCALE = 1.0 / math.sqrt(HEAD_SIZE)
EXP2_SCALE = SCALE * math.log2(math.e)
F32 = jnp.float32
BF16 = jnp.bfloat16


def iota(shape, dim):
    return lax.broadcasted_iota(jnp.int32, shape, dim)


def dot(a, b):
    return jnp.dot(a, b, preferred_element_type=F32)


def ranks_within(member):
    earlier = (iota((TOK, TOK), 0) < iota((TOK, TOK), 1)).astype(F32).astype(BF16)
    counts = dot(member.astype(F32).astype(BF16), earlier)
    return jnp.where(member, counts, -1.0)


def pack_kernel(place_ref, rows_ref, out_ref):
    owner = place_ref[...] >> 8
    rank = ranks_within(owner == iota((SHARDS, TOK), 0))
    slot = iota((SLOTS, TOK), 0).astype(F32)
    picks = jnp.concatenate(
        [(rank[s : s + 1, :] == slot).astype(F32) for s in range(SHARDS)], axis=0
    ).astype(BF16)
    for first in range(0, rows_ref.shape[1], 256):
        cols = pl.ds(first, 256)
        out_ref[:, cols] = dot(picks, rows_ref[:, cols]).astype(BF16)


def stage_kernel(place_ref, kv_ref, out_ref, arrived):
    cols = pl.ds(pl.multiple_of((lax.axis_index("tp") // 2) * HEAD_SIZE, HEAD_SIZE), HEAD_SIZE)
    copies = [
        pltpu.make_async_copy(
            kv_ref.at[i, :, cols],
            out_ref.at[pl.ds(0, TOK), pl.ds(i * HEAD_SIZE, HEAD_SIZE)],
            arrived.at[i],
        )
        for i in range(2)
    ]
    for copy in copies:
        copy.start()
    place = place_ref[...]
    row = iota((META, TOK), 0)
    owner = jnp.broadcast_to((place >> 8).astype(F32), (META, TOK))
    within = jnp.broadcast_to((place & (TOK - 1)).astype(F32), (META, TOK))
    meta = jnp.where(row == 0, owner, jnp.where(row == 1, within, 0.0))
    out_ref[TOK:, :] = meta.astype(BF16)
    for copy in copies:
        copy.wait()


def permute_kernel(info_ref, own_ref, *refs):
    mine, theirs = refs[:RING], refs[RING : 2 * RING]
    out_ref, unpack_ref = refs[2 * RING :]
    shard = info_ref[0]
    core = info_ref[1]
    base = jnp.maximum(shard - BACK, 0)
    z, x = shard // 2, shard % 2
    sources = [(own_ref.at[j], shard ^ j) for j in range(2)]
    for refs_k, side in ((mine, core), (theirs, 1 - core)):
        for k in range(1, RING):
            far = (z + k * (2 * side - 1) + Z_CHIPS) % Z_CHIPS
            sources += [(refs_k[k - 1].at[j], 2 * far + (x ^ j)) for j in range(2)]
        far = (z + RING) % Z_CHIPS
        sources += [(refs_k[RING - 1], 2 * far + (x ^ side))]
    owners = jnp.concatenate([ref[TOK : TOK + 1, :].astype(F32) for ref, _ in sources], axis=0)
    within = jnp.concatenate([ref[TOK + 1 : TOK + 2, :].astype(F32) for ref, _ in sources], axis=0)
    rank = ranks_within(owners == shard.astype(F32))
    slot = iota((SLOTS, TOK), 0).astype(F32)
    lane = iota((SLOTS, TOK), 1).astype(F32)
    for i, (_, source) in enumerate(sources):
        hit = rank[i : i + 1, :] == slot
        landing = jnp.sum(jnp.where(hit, within[i : i + 1, :] + 1.0, 0.0), axis=1, keepdims=True)
        rows = pl.ds(pl.multiple_of(source * SLOTS, SLOTS), SLOTS)
        unpack_ref[rows, :] = (landing == lane + 1.0).astype(F32).astype(BF16)

    def one_shard(i, carry):
        rows = iota((TOK, TOK), 0).astype(F32)
        goal = jnp.where(owners == (base + i).astype(F32), within, -1.0)
        total = jnp.zeros((TOK, 2 * HEAD_SIZE), F32)
        for n, (ref, _) in enumerate(sources):
            picks = (goal[n : n + 1, :] == rows).astype(F32).astype(BF16)
            total = total + dot(picks, ref[:TOK, :])
        out_ref[pl.ds(pl.multiple_of(i * TOK, TOK), TOK), :] = total.astype(BF16)
        return carry

    lax.fori_loop(0, shard - base + 1, one_shard, 0)


def attention_kernel(
    info_ref,
    seg_ref,
    allow_ref,
    segv_ref,
    unpack_ref,
    recv_ref,
    grad_ref,
    kv_ref,
    dq_ref,
    keep_ref,
    send_ref,
    q_s,
    qr_s,
    gr_s,
    qt_s,
    gt_s,
    k_s,
    v_s,
    kt_s,
    bias_s,
    e_s,
    dp_s,
    top_s,
    dqt_s,
    dk_s,
    dv_s,
    acc_s,
    list_s,
):
    shard = info_ref[0]
    core = info_ref[1]
    base = jnp.maximum(shard - BACK, 0)
    acc_s[...] = jnp.zeros_like(acc_s)
    for first in range(0, LOCAL_HEADS * HEAD_SIZE, 256):
        cols = pl.ds(first, 256)
        q_s[:, cols] = lax.dot_general(
            unpack_ref[...],
            recv_ref[:, cols],
            (((0,), (0,)), ((), ())),
            preferred_element_type=F32,
        ).astype(BF16)

    def query_block(half, carry):
        qb = shard * 2 + half
        row0 = pl.multiple_of(half * BLK, BLK)
        q_seg = segv_ref[pl.ds(qb, 1), :]
        q_first = seg_ref[qb * BLK]

        def scan(kb, count):
            seen = jnp.logical_and(
                seg_ref[kb * BLK + BLK - 1] >= q_first, allow_ref[qb, kb] != 0
            )

            @pl.when(seen)
            def _():
                list_s[count] = kb
                src = pl.ds(pl.multiple_of((kb - 2 * base) * BLK, BLK), BLK)
                dst = pl.ds(pl.multiple_of(count * BLK, BLK), BLK)
                k_blk = kv_ref[src, :HEAD_SIZE]
                k_s[dst, :] = k_blk
                v_s[dst, :] = kv_ref[src, HEAD_SIZE:]
                lanes = pl.ds(pl.multiple_of((count % 2) * BLK, BLK), BLK)
                kt_s[count // 2, :, lanes] = k_blk.astype(F32).T.astype(BF16)
                k_seg = jnp.broadcast_to(segv_ref[pl.ds(kb, 1), :].astype(F32), (BLK, BLK)).T
                k_pos = kb * BLK + iota((BLK, BLK), 0)
                q_pos = qb * BLK + iota((BLK, BLK), 1)
                ok = (k_seg == q_seg.astype(F32)) & (k_pos <= q_pos)
                bias_s[dst, :] = jnp.where(ok, 0.0, NEG_FILL)

            return count + seen.astype(jnp.int32)

        count = lax.fori_loop(jnp.maximum(qb - BLOCKS_BACK, 0), qb + 1, scan, 0)

        @pl.when(count % 2 == 1)
        def _():
            dst = pl.ds(pl.multiple_of(count * BLK, BLK), BLK)
            k_s[dst, :] = jnp.zeros((BLK, HEAD_SIZE), BF16)
            v_s[dst, :] = jnp.zeros((BLK, HEAD_SIZE), BF16)
            kt_s[count // 2, :, BLK:] = jnp.zeros((HEAD_SIZE, BLK), BF16)
            bias_s[dst, :] = jnp.full((BLK, BLK), NEG_FILL, F32)

        chunks = (count + 1) // 2

        def clear(ch, c):
            rows = pl.ds(pl.multiple_of(ch * CHUNK, CHUNK), CHUNK)
            dk_s[rows, :] = jnp.zeros((CHUNK, HEAD_SIZE), F32)
            dv_s[rows, :] = jnp.zeros((CHUNK, HEAD_SIZE), F32)
            return c

        lax.fori_loop(0, chunks, clear, 0)
        rows = pl.ds(row0, BLK)
        for hg in range(LOCAL_HEADS // GROUP):
            for i in range(GROUP):
                cols = pl.ds((hg * GROUP + i) * HEAD_SIZE, HEAD_SIZE)
                mine = pl.ds(i * BLK, BLK)
                q_blk = q_s[rows, cols]
                g_blk = grad_ref[rows, cols]
                qr_s[mine, :] = q_blk
                gr_s[mine, :] = g_blk
                qt_s[:, mine] = q_blk.astype(F32).T.astype(BF16)
                gt_s[:, mine] = g_blk.astype(F32).T.astype(BF16)

            def first_pass(ch, state):
                top, total, weighed = state
                rows_c = pl.ds(pl.multiple_of(ch * CHUNK, CHUNK), CHUNK)
                scores = dot(k_s[rows_c, :], qt_s[...])
                scores = scores + jnp.concatenate([bias_s[rows_c, :]] * GROUP, axis=1)
                new_top = jnp.maximum(top, jnp.max(scores, axis=0, keepdims=True))
                factor = jnp.exp2((top - new_top) * EXP2_SCALE)
                e = jnp.exp2((scores - new_top) * EXP2_SCALE)
                dp = dot(v_s[rows_c, :], gt_s[...])
                e_s[ch] = e
                dp_s[ch] = dp
                top_s[ch] = new_top
                total = total * factor + jnp.sum(e.reshape(-1, 8, LANES), axis=0)
                weighed = weighed * factor + jnp.sum((e * dp).reshape(-1, 8, LANES), axis=0)
                return (new_top, total, weighed)

            start = (
                jnp.full((1, LANES), NEG_FILL, F32),
                jnp.zeros((8, LANES), F32),
                jnp.zeros((8, LANES), F32),
            )
            top, total, weighed = lax.fori_loop(0, chunks, first_pass, start)
            inverse = 1.0 / jnp.sum(total, axis=0, keepdims=True)
            out_dot = jnp.sum(weighed, axis=0, keepdims=True) * inverse
            dqt_s[...] = jnp.zeros_like(dqt_s)

            def second_pass(ch, c):
                rows_c = pl.ds(pl.multiple_of(ch * CHUNK, CHUNK), CHUNK)
                factor = jnp.exp2((top_s[ch] - top) * EXP2_SCALE) * inverse
                weights = e_s[ch] * factor
                score_grad = (weights * (dp_s[ch] - out_dot)).astype(BF16)
                dv_s[rows_c, :] += dot(weights.astype(BF16), gr_s[...])
                dk_s[rows_c, :] += dot(score_grad, qr_s[...])
                dqt_s[...] += dot(kt_s[ch], score_grad)
                return c

            lax.fori_loop(0, chunks, second_pass, 0)
            for i in range(GROUP):
                cols = pl.ds((hg * GROUP + i) * HEAD_SIZE, HEAD_SIZE)
                dq_ref[rows, cols] = (dqt_s[:, i * BLK : (i + 1) * BLK] * SCALE).T.astype(BF16)

        def spread(n, c):
            src = pl.ds(pl.multiple_of(n * BLK, BLK), BLK)
            dst = pl.ds(pl.multiple_of((list_s[n] - 2 * base) * BLK, BLK), BLK)
            acc_s[0, dst, :] += dk_s[src, :]
            acc_s[1, dst, :] += dv_s[src, :]
            return c

        lax.fori_loop(0, count, spread, 0)
        return carry

    lax.fori_loop(0, 2, query_block, 0)

    @pl.when(core == 0)
    def _():
        keep_ref[...] = acc_s[0] * SCALE
        send_ref[...] = acc_s[1].astype(BF16)

    @pl.when(core == 1)
    def _():
        keep_ref[...] = acc_s[1]
        send_ref[...] = (acc_s[0] * SCALE).astype(BF16)


def merge_kernel(info_ref, keep_ref, recv_ref, out_ref):
    base = jnp.maximum(info_ref[0] - BACK, 0)
    out_ref[...] = jnp.zeros_like(out_ref)
    rows = pl.ds(pl.multiple_of(base * TOK, TOK), WINDOW * TOK)
    out_ref[rows, :] = (keep_ref[...] + recv_ref[...].astype(F32)).astype(BF16)


VMEM = pl.BlockSpec(memory_space=pltpu.VMEM)
SMEM = pl.BlockSpec(memory_space=pltpu.SMEM)


def call_attention(info, segments, allow, unpack, q_recv, g_local, kv_window):
    width = g_local.shape[1]
    return pl.pallas_call(
        attention_kernel,
        in_specs=[SMEM, SMEM, SMEM] + [VMEM] * 5,
        out_specs=[VMEM, VMEM, VMEM],
        out_shape=[
            jax.ShapeDtypeStruct((TOK, width), BF16),
            jax.ShapeDtypeStruct((WINDOW * TOK, HEAD_SIZE), F32),
            jax.ShapeDtypeStruct((WINDOW * TOK, HEAD_SIZE), BF16),
        ],
        scratch_shapes=[
            pltpu.VMEM((TOK, width), BF16),
            pltpu.VMEM((LANES, HEAD_SIZE), BF16),
            pltpu.VMEM((LANES, HEAD_SIZE), BF16),
            pltpu.VMEM((HEAD_SIZE, LANES), BF16),
            pltpu.VMEM((HEAD_SIZE, LANES), BF16),
            pltpu.VMEM((MOST_BLOCKS * BLK, HEAD_SIZE), BF16),
            pltpu.VMEM((MOST_BLOCKS * BLK, HEAD_SIZE), BF16),
            pltpu.VMEM((MOST_CHUNKS, HEAD_SIZE, CHUNK), BF16),
            pltpu.VMEM((MOST_BLOCKS * BLK, BLK), F32),
            pltpu.VMEM((MOST_CHUNKS, CHUNK, LANES), F32),
            pltpu.VMEM((MOST_CHUNKS, CHUNK, LANES), F32),
            pltpu.VMEM((MOST_CHUNKS, 1, LANES), F32),
            pltpu.VMEM((HEAD_SIZE, LANES), F32),
            pltpu.VMEM((MOST_BLOCKS * BLK, HEAD_SIZE), F32),
            pltpu.VMEM((MOST_BLOCKS * BLK, HEAD_SIZE), F32),
            pltpu.VMEM((2, WINDOW * TOK, HEAD_SIZE), F32),
            pltpu.SMEM((MOST_BLOCKS,), jnp.int32),
        ],
        compiler_params=pltpu.CompilerParams(vmem_limit_bytes=48 * 2**20),
        name="attention",
    )(info, segments, allow, segments.reshape(-1, BLK), unpack, q_recv, g_local, kv_window)


def on_device(queries, keys_values, out_grad, place, segments, allow):
    tp_index = lax.axis_index("tp")
    ctx_index = lax.axis_index("ctx")
    tp_size = lax.axis_size("tp")
    width = LOCAL_HEADS * HEAD_SIZE
    info = jnp.stack([ctx_index, tp_index % 2]).astype(jnp.int32)
    staged = pl.pallas_call(
        stage_kernel,
        in_specs=[VMEM, pl.BlockSpec(memory_space=pl.ANY)],
        out_specs=VMEM,
        out_shape=jax.ShapeDtypeStruct((TOK + META, 2 * HEAD_SIZE), BF16),
        scratch_shapes=[pltpu.SemaphoreType.DMA((2,))],
        name="stage",
    )(place.reshape(1, TOK), keys_values)
    beside = lax.ppermute(staged, "ctx", [(k, k ^ 1) for k in range(SHARDS)])
    own = jnp.stack([staged, beside])

    def around(hops):
        pairs = []
        for k in range(SHARDS * tp_size):
            ctx, tp = k // tp_size, k % tp_size
            far = (ctx + (2 * hops if tp % 2 == 0 else -2 * hops)) % SHARDS
            pairs.append((k, far * tp_size + tp))
        return pairs

    swap = [(k, k ^ 1) for k in range(tp_size)]
    first = lax.ppermute(own, ("ctx", "tp"), around(1))
    second = lax.ppermute(first, ("ctx", "tp"), around(1))
    third = lax.ppermute(second, ("ctx", "tp"), around(1))
    half = lax.dynamic_index_in_dim(second, tp_index % 2, 0, keepdims=False)
    fourth = lax.ppermute(half, ("ctx", "tp"), around(2))
    mine = [first, second, third, fourth]
    g_local = lax.all_to_all(out_grad, "tp", split_axis=1, concat_axis=0, tiled=True)
    q_send = pl.pallas_call(
        pack_kernel,
        in_specs=[VMEM, VMEM],
        out_specs=VMEM,
        out_shape=jax.ShapeDtypeStruct((SHARDS * SLOTS, width), BF16),
        name="pack",
    )(place.reshape(1, TOK), queries)
    q_send, *mine = lax.optimization_barrier((q_send, *mine))
    theirs = [lax.ppermute(piece, "tp", swap) for piece in mine]
    q_recv = lax.all_to_all(q_send, "ctx", split_axis=0, concat_axis=0, tiled=True)
    kv_window, unpack = pl.pallas_call(
        permute_kernel,
        in_specs=[SMEM] + [VMEM] * (2 * RING + 1),
        out_specs=[VMEM, VMEM],
        out_shape=[
            jax.ShapeDtypeStruct((WINDOW * TOK, 2 * HEAD_SIZE), BF16),
            jax.ShapeDtypeStruct((SHARDS * SLOTS, TOK), BF16),
        ],
        compiler_params=pltpu.CompilerParams(vmem_limit_bytes=32 * 2**20),
        name="permute",
    )(info, own, *mine, *theirs)
    grad_q, keep, send = call_attention(
        info, segments, allow, unpack, q_recv, g_local, kv_window
    )
    recv = lax.ppermute(send, "tp", swap)
    part = pl.pallas_call(
        merge_kernel,
        in_specs=[SMEM, VMEM, VMEM],
        out_specs=VMEM,
        out_shape=jax.ShapeDtypeStruct((SHARDS * TOK, HEAD_SIZE), BF16),
        name="merge",
    )(info, keep, recv)
    parts = lax.all_to_all(
        part.reshape(SHARDS, TOK, HEAD_SIZE), "ctx", split_axis=0, concat_axis=0, tiled=True
    )
    owned = jnp.sum(parts.astype(F32), axis=0).astype(BF16)
    heads = lax.all_to_all(
        owned.reshape(tp_size, TOK // tp_size, HEAD_SIZE),
        "tp",
        split_axis=0,
        concat_axis=0,
        tiled=True,
    )
    key_value_gradient = (
        heads.reshape(KEY_VALUE_HEADS, 2, TOK // tp_size, HEAD_SIZE)
        .transpose(1, 2, 0, 3)
        .reshape(2, TOK // tp_size, KEY_VALUE_HEADS * HEAD_SIZE)
    )
    return (grad_q, key_value_gradient)


def solution(mesh):
    in_specs = (P("ctx", "tp"), P(None, "ctx", None), P(("ctx", "tp"), None), P("ctx"), P(), P())
    out_specs = (P("ctx", "tp"), P(None, ("ctx", "tp"), None))
    return jax.shard_map(
        on_device, mesh=mesh, in_specs=in_specs, out_specs=out_specs, check_vma=False
    )
```

```python
import functools
import math

import jax
import jax.numpy as jnp
from jax import lax
from jax.experimental import pallas as pl
from jax.experimental.pallas import tpu as pltpu
from jax.sharding import PartitionSpec as P

QUERY_HEAD_COUNT = 128
KEY_VALUE_HEADS = 8
HEAD_SIZE = 128
BLK = 128
TOK = 256
SHARDS = 16
SLOTS = 32
META = 16
Z_CHIPS = SHARDS // 2
RING = Z_CHIPS // 2
DOC_MOST = 2304
BACK = -(-DOC_MOST // TOK)
WINDOW = BACK + 1
BLOCKS_BACK = -(-DOC_MOST // BLK)
WIDE = 4
NARROW = 2
MOST_BLOCKS = WIDE * -(-(BLOCKS_BACK + 1) // WIDE)
LOCAL_HEADS = 8
LANES = LOCAL_HEADS * BLK
NEG_FILL = -1e30
SCALE = 1.0 / math.sqrt(HEAD_SIZE)
EXP2_SCALE = SCALE * math.log2(math.e)
F32 = jnp.float32
BF16 = jnp.bfloat16


def iota(shape, dim):
    return lax.broadcasted_iota(jnp.int32, shape, dim)


def dot(a, b):
    return jnp.dot(a, b, preferred_element_type=F32)


def ranks_within(member):
    earlier = (iota((TOK, TOK), 0) < iota((TOK, TOK), 1)).astype(F32).astype(BF16)
    counts = dot(member.astype(F32).astype(BF16), earlier)
    return jnp.where(member, counts, -1.0)


def pack_kernel(place_ref, rows_ref, out_ref):
    owner = place_ref[...] >> 8
    rank = ranks_within(owner == iota((SHARDS, TOK), 0))
    slot = iota((SLOTS, TOK), 0).astype(F32)
    picks = jnp.concatenate(
        [(rank[s : s + 1, :] == slot).astype(F32) for s in range(SHARDS)], axis=0
    ).astype(BF16)
    for first in range(0, rows_ref.shape[1], 256):
        cols = pl.ds(first, 256)
        out_ref[:, cols] = dot(picks, rows_ref[:, cols]).astype(BF16)


def stage_kernel(place_ref, kv_ref, out_ref, arrived):
    cols = pl.ds(pl.multiple_of((lax.axis_index("tp") // 2) * HEAD_SIZE, HEAD_SIZE), HEAD_SIZE)
    copies = [
        pltpu.make_async_copy(
            kv_ref.at[i, :, cols],
            out_ref.at[pl.ds(0, TOK), pl.ds(i * HEAD_SIZE, HEAD_SIZE)],
            arrived.at[i],
        )
        for i in range(2)
    ]
    for copy in copies:
        copy.start()
    place = place_ref[...]
    row = iota((META, TOK), 0)
    owner = jnp.broadcast_to((place >> 8).astype(F32), (META, TOK))
    within = jnp.broadcast_to((place & (TOK - 1)).astype(F32), (META, TOK))
    meta = jnp.where(row == 0, owner, jnp.where(row == 1, within, 0.0))
    out_ref[TOK:, :] = meta.astype(BF16)
    for copy in copies:
        copy.wait()


def permute_kernel(info_ref, grad_ref, own_ref, *refs):
    mine, theirs = refs[:RING], refs[RING : 2 * RING]
    out_ref, unpack_ref, gr_ref, gt_ref, slots_s = refs[2 * RING :]
    shard = info_ref[0]
    core = info_ref[1]
    base = jnp.maximum(shard - BACK, 0)
    z, x = shard // 2, shard % 2
    sources = [(own_ref.at[j], shard ^ j) for j in range(2)]
    for refs_k, side in ((mine, core), (theirs, 1 - core)):
        for k in range(1, RING):
            far = (z + k * (2 * side - 1) + Z_CHIPS) % Z_CHIPS
            sources += [(refs_k[k - 1].at[j], 2 * far + (x ^ j)) for j in range(2)]
        far = (z + RING) % Z_CHIPS
        sources += [(refs_k[RING - 1], 2 * far + (x ^ side))]
    owners = jnp.concatenate([ref[TOK : TOK + 1, :].astype(F32) for ref, _ in sources], axis=0)
    within = jnp.concatenate([ref[TOK + 1 : TOK + 2, :].astype(F32) for ref, _ in sources], axis=0)
    rank = ranks_within(owners == shard.astype(F32))
    slot = iota((SLOTS, TOK), 0).astype(F32)
    lane = iota((SLOTS, TOK), 1).astype(F32)
    for i, (_, source) in enumerate(sources):
        hit = rank[i : i + 1, :] == slot
        landing = jnp.sum(jnp.where(hit, within[i : i + 1, :] + 1.0, 0.0), axis=1, keepdims=True)
        rows = pl.ds(pl.multiple_of(source * SLOTS, SLOTS), SLOTS)
        slots_s[rows, :] = (landing == lane + 1.0).astype(F32)
    unpack_ref[...] = slots_s[...].T.astype(BF16)
    for half in range(2):
        for h in range(LOCAL_HEADS):
            block = grad_ref[half * BLK : (half + 1) * BLK, h * HEAD_SIZE : (h + 1) * HEAD_SIZE]
            gr_ref[half, h * BLK : (h + 1) * BLK, :] = block
            gt_ref[half, :, h * BLK : (h + 1) * BLK] = block.astype(F32).T.astype(BF16)

    def one_shard(i, carry):
        rows = iota((TOK, TOK), 0).astype(F32)
        goal = jnp.where(owners == (base + i).astype(F32), within, -1.0)
        total = jnp.zeros((TOK, 2 * HEAD_SIZE), F32)
        for n, (ref, _) in enumerate(sources):
            picks = (goal[n : n + 1, :] == rows).astype(F32).astype(BF16)
            total = total + dot(picks, ref[:TOK, :])
        out_ref[pl.ds(pl.multiple_of(i * TOK, TOK), TOK), :] = total.astype(BF16)
        return carry

    lax.fori_loop(0, shard - base + 1, one_shard, 0)


def visible_blocks(qb, seg_ref, allow_ref, on_block):
    q_first = seg_ref[qb * BLK]

    def scan(kb, count):
        seen = jnp.logical_and(seg_ref[kb * BLK + BLK - 1] >= q_first, allow_ref[qb, kb] != 0)

        @pl.when(seen)
        def _():
            on_block(kb, count)

        return count + seen.astype(jnp.int32)

    count = lax.fori_loop(jnp.maximum(qb - BLOCKS_BACK, 0), qb + 1, scan, 0)
    wide = (count + 1) // WIDE
    narrow = (count + WIDE - 1) // WIDE - wide
    return count, wide, narrow


def block_rows(n, blocks=1):
    return pl.ds(pl.multiple_of(n * BLK, BLK), blocks * BLK)


def attention_kernel(
    info_ref,
    seg_ref,
    allow_ref,
    segv_ref,
    unpack_ref,
    recv_ref,
    gr_ref,
    gt_ref,
    kv_ref,
    keep_ref,
    send_ref,
    sg_ref,
    qr_s,
    qt_s,
    k_s,
    v_s,
    bias_s,
    e_s,
    dp_s,
    top_s,
    acc_s,
    sg_s,
    list_s,
    sent,
):
    shard = info_ref[0]
    core = info_ref[1]
    base = jnp.maximum(shard - BACK, 0)
    acc_s[...] = jnp.zeros_like(acc_s)

    def query_block(half, carry):
        qb = shard * 2 + half
        q_seg = segv_ref[pl.ds(qb, 1), :]
        q_last = seg_ref[qb * BLK + BLK - 1]

        def on_block(kb, count):
            list_s[count] = kb - 2 * base
            src = block_rows(kb - 2 * base)
            dst = block_rows(count)
            k_s[dst, :] = kv_ref[src, :HEAD_SIZE]
            v_s[dst, :] = kv_ref[src, HEAD_SIZE:]
            whole = jnp.logical_and(kb < qb, seg_ref[kb * BLK] == q_last)

            @pl.when(whole)
            def _():
                bias_s[dst, :] = jnp.zeros((BLK, BLK), F32)

            @pl.when(jnp.logical_not(whole))
            def _():
                k_seg = jnp.broadcast_to(segv_ref[pl.ds(kb, 1), :].astype(F32), (BLK, BLK)).T
                k_pos = kb * BLK + iota((BLK, BLK), 0)
                q_pos = qb * BLK + iota((BLK, BLK), 1)
                ok = (k_seg == q_seg.astype(F32)) & (k_pos <= q_pos)
                bias_s[dst, :] = jnp.where(ok, 0.0, NEG_FILL)

        count, wide, narrow = visible_blocks(qb, seg_ref, allow_ref, on_block)

        def fill(n, c):
            list_s[n] = 2 * WINDOW
            dst = block_rows(n)
            k_s[dst, :] = jnp.zeros((BLK, HEAD_SIZE), BF16)
            v_s[dst, :] = jnp.zeros((BLK, HEAD_SIZE), BF16)
            bias_s[dst, :] = jnp.full((BLK, BLK), NEG_FILL, F32)
            return c

        lax.fori_loop(count, wide * WIDE + narrow * NARROW, fill, 0)
        picks = unpack_ref[block_rows(half), :]
        for pair in range(LOCAL_HEADS // 2):
            q_two = dot(picks, recv_ref[:, pair * 256 : (pair + 1) * 256])
            for i in range(2):
                mine = slice((2 * pair + i) * BLK, (2 * pair + i + 1) * BLK)
                q_one = q_two[:, i * HEAD_SIZE : (i + 1) * HEAD_SIZE]
                qr_s[mine, :] = q_one.astype(BF16)
                qt_s[:, mine] = q_one.T.astype(BF16)

        def first_pass(start, blocks, slot, state):
            top, total, weighed = state
            rows = block_rows(start, blocks)
            scores = dot(k_s[rows, :], qt_s[...])
            scores = scores + jnp.concatenate([bias_s[rows, :]] * LOCAL_HEADS, axis=1)
            new_top = jnp.maximum(top, jnp.max(scores, axis=0, keepdims=True))
            factor = jnp.exp2((top - new_top) * EXP2_SCALE)
            e = jnp.exp2((scores - new_top) * EXP2_SCALE)
            dp = dot(v_s[rows, :], gt_ref[half])
            e_s[rows, :] = e
            dp_s[rows, :] = dp
            top_s[slot] = new_top
            total = total * factor + jnp.sum(e.reshape(-1, 8, LANES), axis=0)
            weighed = weighed * factor + jnp.sum((e * dp).reshape(-1, 8, LANES), axis=0)
            return (new_top, total, weighed)

        state = (
            jnp.full((1, LANES), NEG_FILL, F32),
            jnp.zeros((8, LANES), F32),
            jnp.zeros((8, LANES), F32),
        )
        state = lax.fori_loop(
            0, wide, lambda n, st: first_pass(n * WIDE, WIDE, n, st), state
        )
        top, total, weighed = lax.fori_loop(
            0, narrow, lambda n, st: first_pass(wide * WIDE, NARROW, wide, st), state
        )
        inverse = 1.0 / jnp.sum(total, axis=0, keepdims=True)
        out_dot = jnp.sum(weighed, axis=0, keepdims=True) * inverse

        def copy_out(start, blocks, buffer):
            return pltpu.make_async_copy(
                sg_s.at[buffer, pl.ds(0, blocks * BLK), :],
                sg_ref.at[half, block_rows(start, blocks), :],
                sent.at[buffer],
            )

        def second_pass(start, blocks, slot, buffer):
            rows = block_rows(start, blocks)
            factor = jnp.exp2((top_s[slot] - top) * EXP2_SCALE) * inverse
            weights = e_s[rows, :] * factor
            score_grad = (weights * (dp_s[rows, :] - out_dot)).astype(BF16)
            sg_s[buffer, : blocks * BLK, :] = score_grad
            copy_out(start, blocks, buffer).start()
            value_terms = dot(weights.astype(BF16), gr_ref[half])
            key_terms = dot(score_grad, qr_s[...])
            for n in range(blocks):
                dst = block_rows(list_s[start + n])
                acc_s[0, dst, :] += key_terms[n * BLK : (n + 1) * BLK, :]
                acc_s[1, dst, :] += value_terms[n * BLK : (n + 1) * BLK, :]

        def wide_step(n, c):
            @pl.when(n >= 2)
            def _():
                copy_out((n - 2) * WIDE, WIDE, n % 2).wait()

            second_pass(n * WIDE, WIDE, n, n % 2)
            return c

        lax.fori_loop(0, wide, wide_step, 0)

        @pl.when(narrow > 0)
        def _():
            second_pass(wide * WIDE, NARROW, wide, 2)
            copy_out(wide * WIDE, NARROW, 2).wait()

        for late in (1, 2):

            @pl.when(wide >= late)
            def _():
                copy_out((wide - late) * WIDE, WIDE, (wide - late) % 2).wait()

        return carry

    lax.fori_loop(0, 2, query_block, 0)
    rows = slice(0, WINDOW * TOK)

    @pl.when(core == 0)
    def _():
        keep_ref[...] = (acc_s[0, rows, :] * SCALE).astype(BF16)
        send_ref[...] = acc_s[1, rows, :].astype(BF16)

    @pl.when(core == 1)
    def _():
        keep_ref[...] = acc_s[1, rows, :].astype(BF16)
        send_ref[...] = (acc_s[0, rows, :] * SCALE).astype(BF16)


def query_grad_kernel(
    info_ref, seg_ref, allow_ref, kv_ref, sg_ref, dq_ref, kt_s, dqt_s, sg_s, arrived
):
    shard = info_ref[0]
    base = jnp.maximum(shard - BACK, 0)

    def query_block(half, carry):
        def on_block(kb, count):
            lanes = block_rows(count % NARROW)
            k_blk = kv_ref[block_rows(kb - 2 * base), :HEAD_SIZE]
            kt_s[count // NARROW, :, lanes] = k_blk.astype(F32).T.astype(BF16)

        count, wide, narrow = visible_blocks(shard * 2 + half, seg_ref, allow_ref, on_block)
        steps = wide * (WIDE // NARROW) + narrow

        def fill(n, c):
            lanes = block_rows(n % NARROW)
            kt_s[n // NARROW, :, lanes] = jnp.zeros((HEAD_SIZE, BLK), BF16)
            return c

        lax.fori_loop(count, steps * NARROW, fill, 0)

        def fetch(step):
            return pltpu.make_async_copy(
                sg_ref.at[half, block_rows(step * NARROW, NARROW), :],
                sg_s.at[step % 2],
                arrived.at[step % 2],
            )

        fetch(0).start()
        dqt_s[...] = jnp.zeros_like(dqt_s)

        def one_step(step, c):
            @pl.when(step + 1 < steps)
            def _():
                fetch(step + 1).start()

            fetch(step).wait()
            dqt_s[...] += dot(kt_s[step], sg_s[step % 2])
            return c

        lax.fori_loop(0, steps, one_step, 0)
        for h in range(LOCAL_HEADS):
            block = dqt_s[:, h * BLK : (h + 1) * BLK] * SCALE
            dq_ref[block_rows(half), h * HEAD_SIZE : (h + 1) * HEAD_SIZE] = block.T.astype(BF16)
        return carry

    lax.fori_loop(0, 2, query_block, 0)


def merge_kernel(info_ref, keep_ref, recv_ref, out_ref):
    base = jnp.maximum(info_ref[0] - BACK, 0)
    out_ref[...] = jnp.zeros_like(out_ref)
    rows = pl.ds(pl.multiple_of(base * TOK, TOK), WINDOW * TOK)
    out_ref[rows, :] = (keep_ref[...].astype(F32) + recv_ref[...].astype(F32)).astype(BF16)


VMEM = pl.BlockSpec(memory_space=pltpu.VMEM)
SMEM = pl.BlockSpec(memory_space=pltpu.SMEM)


ANY = pl.BlockSpec(memory_space=pl.ANY)


def call_permute(info, grad, own, mine, theirs):
    return pl.pallas_call(
        permute_kernel,
        in_specs=[SMEM] + [VMEM] * (2 * RING + 2),
        out_specs=[VMEM] * 4,
        out_shape=[
            jax.ShapeDtypeStruct((WINDOW * TOK, 2 * HEAD_SIZE), BF16),
            jax.ShapeDtypeStruct((TOK, SHARDS * SLOTS), BF16),
            jax.ShapeDtypeStruct((2, LANES, HEAD_SIZE), BF16),
            jax.ShapeDtypeStruct((2, HEAD_SIZE, LANES), BF16),
        ],
        scratch_shapes=[pltpu.VMEM((SHARDS * SLOTS, TOK), F32)],
        compiler_params=pltpu.CompilerParams(vmem_limit_bytes=32 * 2**20),
        name="permute",
    )(info, grad, own, *mine, *theirs)


def call_attention(info, segments, allow, unpack, q_recv, gr, gt, kv_window):
    return pl.pallas_call(
        attention_kernel,
        in_specs=[SMEM, SMEM, SMEM] + [VMEM] * 6,
        out_specs=[VMEM, VMEM, ANY],
        out_shape=[
            jax.ShapeDtypeStruct((WINDOW * TOK, HEAD_SIZE), BF16),
            jax.ShapeDtypeStruct((WINDOW * TOK, HEAD_SIZE), BF16),
            jax.ShapeDtypeStruct((2, MOST_BLOCKS * BLK, LANES), BF16),
        ],
        scratch_shapes=[
            pltpu.VMEM((LANES, HEAD_SIZE), BF16),
            pltpu.VMEM((HEAD_SIZE, LANES), BF16),
            pltpu.VMEM((MOST_BLOCKS * BLK, HEAD_SIZE), BF16),
            pltpu.VMEM((MOST_BLOCKS * BLK, HEAD_SIZE), BF16),
            pltpu.VMEM((MOST_BLOCKS * BLK, BLK), F32),
            pltpu.VMEM((MOST_BLOCKS * BLK, LANES), F32),
            pltpu.VMEM((MOST_BLOCKS * BLK, LANES), F32),
            pltpu.VMEM((MOST_BLOCKS // WIDE + 1, 1, LANES), F32),
            pltpu.VMEM((2, WINDOW * TOK + BLK, HEAD_SIZE), F32),
            pltpu.VMEM((3, WIDE * BLK, LANES), BF16),
            pltpu.SMEM((MOST_BLOCKS,), jnp.int32),
            pltpu.SemaphoreType.DMA((3,)),
        ],
        compiler_params=pltpu.CompilerParams(vmem_limit_bytes=48 * 2**20),
        name="attention",
    )(info, segments, allow, segments.reshape(-1, BLK), unpack, q_recv, gr, gt, kv_window)


def call_query_grad(info, segments, allow, kv_window, score_grad):
    return pl.pallas_call(
        query_grad_kernel,
        in_specs=[SMEM, SMEM, SMEM, VMEM, ANY],
        out_specs=VMEM,
        out_shape=jax.ShapeDtypeStruct((TOK, LOCAL_HEADS * HEAD_SIZE), BF16),
        scratch_shapes=[
            pltpu.VMEM((MOST_BLOCKS // NARROW, HEAD_SIZE, NARROW * BLK), BF16),
            pltpu.VMEM((HEAD_SIZE, LANES), F32),
            pltpu.VMEM((2, NARROW * BLK, LANES), BF16),
            pltpu.SemaphoreType.DMA((2,)),
        ],
        compiler_params=pltpu.CompilerParams(vmem_limit_bytes=32 * 2**20),
        cost_estimate=pl.CostEstimate(
            flops=2 * TOK * 2048 * LANES, bytes_accessed=12 * 2**20, transcendentals=0
        ),
        name="query_grad",
    )(info, segments, allow, kv_window, score_grad)


def on_device(queries, keys_values, out_grad, place, segments, allow):
    tp_index = lax.axis_index("tp")
    ctx_index = lax.axis_index("ctx")
    tp_size = lax.axis_size("tp")
    width = LOCAL_HEADS * HEAD_SIZE
    info = jnp.stack([ctx_index, tp_index % 2]).astype(jnp.int32)
    staged = pl.pallas_call(
        stage_kernel,
        in_specs=[VMEM, pl.BlockSpec(memory_space=pl.ANY)],
        out_specs=VMEM,
        out_shape=jax.ShapeDtypeStruct((TOK + META, 2 * HEAD_SIZE), BF16),
        scratch_shapes=[pltpu.SemaphoreType.DMA((2,))],
        name="stage",
    )(place.reshape(1, TOK), keys_values)
    beside = lax.ppermute(staged, "ctx", [(k, k ^ 1) for k in range(SHARDS)])
    own = jnp.stack([staged, beside])

    def around(hops):
        pairs = []
        for k in range(SHARDS * tp_size):
            ctx, tp = k // tp_size, k % tp_size
            far = (ctx + (2 * hops if tp % 2 == 0 else -2 * hops)) % SHARDS
            pairs.append((k, far * tp_size + tp))
        return pairs

    swap = [(k, k ^ 1) for k in range(tp_size)]
    first = lax.ppermute(own, ("ctx", "tp"), around(1))
    second = lax.ppermute(first, ("ctx", "tp"), around(1))
    third = lax.ppermute(second, ("ctx", "tp"), around(1))
    half = lax.dynamic_index_in_dim(second, tp_index % 2, 0, keepdims=False)
    fourth = lax.ppermute(half, ("ctx", "tp"), around(2))
    mine = [first, second, third, fourth]
    g_local = lax.all_to_all(out_grad, "tp", split_axis=1, concat_axis=0, tiled=True)
    q_send = pl.pallas_call(
        pack_kernel,
        in_specs=[VMEM, VMEM],
        out_specs=VMEM,
        out_shape=jax.ShapeDtypeStruct((SHARDS * SLOTS, width), BF16),
        name="pack",
    )(place.reshape(1, TOK), queries)
    q_send, *mine = lax.optimization_barrier((q_send, *mine))
    theirs = [lax.ppermute(piece, "tp", swap) for piece in mine]
    q_recv = lax.all_to_all(q_send, "ctx", split_axis=0, concat_axis=0, tiled=True)
    kv_window, unpack, gr, gt = call_permute(info, g_local, own, mine, theirs)
    keep, send, score_grad = call_attention(
        info, segments, allow, unpack, q_recv, gr, gt, kv_window
    )
    recv = lax.ppermute(send, "tp", swap)
    part = pl.pallas_call(
        merge_kernel,
        in_specs=[SMEM, VMEM, VMEM],
        out_specs=VMEM,
        out_shape=jax.ShapeDtypeStruct((SHARDS * TOK, HEAD_SIZE), BF16),
        name="merge",
    )(info, keep, recv)
    part, score_grad = lax.optimization_barrier((part, score_grad))
    parts = lax.all_to_all(
        part.reshape(SHARDS, TOK, HEAD_SIZE), "ctx", split_axis=0, concat_axis=0, tiled=True
    )
    grad_q = call_query_grad(info, segments, allow, kv_window, score_grad)
    owned = jnp.sum(parts.astype(F32), axis=0).astype(BF16)
    heads = lax.all_to_all(
        owned.reshape(tp_size, TOK // tp_size, HEAD_SIZE),
        "tp",
        split_axis=0,
        concat_axis=0,
        tiled=True,
    )
    key_value_gradient = (
        heads.reshape(KEY_VALUE_HEADS, 2, TOK // tp_size, HEAD_SIZE)
        .transpose(1, 2, 0, 3)
        .reshape(2, TOK // tp_size, KEY_VALUE_HEADS * HEAD_SIZE)
    )
    return (grad_q, key_value_gradient)


def solution(mesh):
    in_specs = (P("ctx", "tp"), P(None, "ctx", None), P(("ctx", "tp"), None), P("ctx"), P(), P())
    out_specs = (P("ctx", "tp"), P(None, ("ctx", "tp"), None))
    return jax.shard_map(
        on_device, mesh=mesh, in_specs=in_specs, out_specs=out_specs, check_vma=False
    )
```

```python
import functools
import math

import jax
import jax.numpy as jnp
from jax import lax
from jax.experimental import pallas as pl
from jax.experimental.pallas import tpu as pltpu
from jax.sharding import PartitionSpec as P

QUERY_HEAD_COUNT = 128
KEY_VALUE_HEADS = 8
HEAD_SIZE = 128
BLK = 128
TOK = 256
SHARDS = 16
SLOTS = 32
META = 16
Z_CHIPS = SHARDS // 2
RING = Z_CHIPS // 2
DOC_MOST = 2304
BACK = -(-DOC_MOST // TOK)
WINDOW = BACK + 1
BLOCKS_BACK = -(-DOC_MOST // BLK)
WIDE = 4
NARROW = 2
MOST_BLOCKS = WIDE * -(-(BLOCKS_BACK + 1) // WIDE)
LOCAL_HEADS = 8
LANES = LOCAL_HEADS * BLK
NEG_FILL = -1e30
VMEM_LIMIT = 60 * 2**20
SCALE = 1.0 / math.sqrt(HEAD_SIZE)
EXP2_SCALE = SCALE * math.log2(math.e)
F32 = jnp.float32
BF16 = jnp.bfloat16


def iota(shape, dim):
    return lax.broadcasted_iota(jnp.int32, shape, dim)


def dot(a, b):
    return jnp.dot(a, b, preferred_element_type=F32)


def ranks_within(member):
    earlier = (iota((TOK, TOK), 0) < iota((TOK, TOK), 1)).astype(F32).astype(BF16)
    counts = dot(member.astype(F32).astype(BF16), earlier)
    return jnp.where(member, counts, -1.0)


def pack_kernel(place_ref, rows_ref, out_ref):
    owner = place_ref[...] >> 8
    rank = ranks_within(owner == iota((SHARDS, TOK), 0))
    slot = iota((SLOTS, TOK), 0).astype(F32)
    picks = jnp.concatenate(
        [(rank[s : s + 1, :] == slot).astype(F32) for s in range(SHARDS)], axis=0
    ).astype(BF16)
    for first in range(0, rows_ref.shape[1], 256):
        cols = pl.ds(first, 256)
        out_ref[:, cols] = dot(picks, rows_ref[:, cols]).astype(BF16)


def stage_kernel(place_ref, kv_ref, out_ref, arrived):
    cols = pl.ds(pl.multiple_of((lax.axis_index("tp") // 2) * HEAD_SIZE, HEAD_SIZE), HEAD_SIZE)
    copies = [
        pltpu.make_async_copy(
            kv_ref.at[i, :, cols],
            out_ref.at[pl.ds(0, TOK), pl.ds(i * HEAD_SIZE, HEAD_SIZE)],
            arrived.at[i],
        )
        for i in range(2)
    ]
    for copy in copies:
        copy.start()
    place = place_ref[...]
    row = iota((META, TOK), 0)
    owner = jnp.broadcast_to((place >> 8).astype(F32), (META, TOK))
    within = jnp.broadcast_to((place & (TOK - 1)).astype(F32), (META, TOK))
    meta = jnp.where(row == 0, owner, jnp.where(row == 1, within, 0.0))
    out_ref[TOK:, :] = meta.astype(BF16)
    for copy in copies:
        copy.wait()


def fetch_all(sources, buffers, arrived):
    copies = [
        pltpu.make_async_copy(source, buffer, arrived.at[i])
        for i, (source, buffer) in enumerate(zip(sources, buffers))
    ]
    for copy in copies:
        copy.start()
    return copies


def permute_kernel(info_ref, *refs):
    count = 2 * RING + 2
    out_ref, unpack_ref, gr_ref, gt_ref, slots_s = refs[count : count + 5]
    grad_ref, own_ref = refs[count + 5 : count + 7]
    mine = refs[count + 7 : count + 7 + RING]
    theirs = refs[count + 7 + RING : count + 7 + 2 * RING]
    for copy in fetch_all(refs[:count], refs[count + 5 : -1], refs[-1]):
        copy.wait()
    shard = info_ref[0]
    core = info_ref[1]
    base = jnp.maximum(shard - BACK, 0)
    z, x = shard // 2, shard % 2
    sources = [(own_ref.at[j], shard ^ j) for j in range(2)]
    for refs_k, side in ((mine, core), (theirs, 1 - core)):
        for k in range(1, RING):
            far = (z + k * (2 * side - 1) + Z_CHIPS) % Z_CHIPS
            sources += [(refs_k[k - 1].at[j], 2 * far + (x ^ j)) for j in range(2)]
        far = (z + RING) % Z_CHIPS
        sources += [(refs_k[RING - 1], 2 * far + (x ^ side))]
    owners = jnp.concatenate([ref[TOK : TOK + 1, :].astype(F32) for ref, _ in sources], axis=0)
    within = jnp.concatenate([ref[TOK + 1 : TOK + 2, :].astype(F32) for ref, _ in sources], axis=0)
    rank = ranks_within(owners == shard.astype(F32))
    slot = iota((SLOTS, TOK), 0).astype(F32)
    lane = iota((SLOTS, TOK), 1).astype(F32)
    for i, (_, source) in enumerate(sources):
        hit = rank[i : i + 1, :] == slot
        landing = jnp.sum(jnp.where(hit, within[i : i + 1, :] + 1.0, 0.0), axis=1, keepdims=True)
        rows = pl.ds(pl.multiple_of(source * SLOTS, SLOTS), SLOTS)
        slots_s[rows, :] = (landing == lane + 1.0).astype(F32)
    unpack_ref[...] = slots_s[...].T.astype(BF16)
    for half in range(2):
        for h in range(LOCAL_HEADS):
            block = grad_ref[half * BLK : (half + 1) * BLK, h * HEAD_SIZE : (h + 1) * HEAD_SIZE]
            gr_ref[half, h * BLK : (h + 1) * BLK, :] = block
            gt_ref[half, :, h * BLK : (h + 1) * BLK] = block.astype(F32).T.astype(BF16)

    def one_shard(i, carry):
        rows = iota((TOK, TOK), 0).astype(F32)
        goal = jnp.where(owners == (base + i).astype(F32), within, -1.0)
        total = jnp.zeros((TOK, 2 * HEAD_SIZE), F32)
        for n, (ref, _) in enumerate(sources):
            picks = (goal[n : n + 1, :] == rows).astype(F32).astype(BF16)
            total = total + dot(picks, ref[:TOK, :])
        out_ref[pl.ds(pl.multiple_of(i * TOK, TOK), TOK), :] = total.astype(BF16)
        return carry

    lax.fori_loop(0, shard - base + 1, one_shard, 0)


def visible_blocks(qb, seg_ref, allow_ref, on_block):
    q_first = seg_ref[qb * BLK]

    def scan(kb, count):
        seen = jnp.logical_and(seg_ref[kb * BLK + BLK - 1] >= q_first, allow_ref[qb, kb] != 0)

        @pl.when(seen)
        def _():
            on_block(kb, count)

        return count + seen.astype(jnp.int32)

    count = lax.fori_loop(jnp.maximum(qb - BLOCKS_BACK, 0), qb + 1, scan, 0)
    wide = (count + 1) // WIDE
    narrow = (count + WIDE - 1) // WIDE - wide
    return count, wide, narrow


def block_rows(n, blocks=1):
    return pl.ds(pl.multiple_of(n * BLK, BLK), blocks * BLK)


def attention_kernel(
    info_ref,
    seg_ref,
    allow_ref,
    segv_ref,
    unpack_in,
    recv_in,
    gr_in,
    gt_in,
    kv_in,
    keep_ref,
    send_ref,
    sg_ref,
    qr_s,
    qt_s,
    k_s,
    v_s,
    bias_s,
    e_s,
    dp_s,
    top_s,
    acc_s,
    sg_s,
    list_s,
    sent,
    kv_ref,
    unpack_ref,
    recv_ref,
    gr_ref,
    gt_ref,
    arrived,
):
    shard = info_ref[0]
    core = info_ref[1]
    base = jnp.maximum(shard - BACK, 0)
    copies = fetch_all(
        (kv_in, unpack_in, recv_in, gr_in, gt_in),
        (kv_ref, unpack_ref, recv_ref, gr_ref, gt_ref),
        arrived,
    )
    acc_s[...] = jnp.zeros_like(acc_s)
    copies[0].wait()

    def query_block(half, carry):
        qb = shard * 2 + half
        q_seg = segv_ref[pl.ds(qb, 1), :]
        q_last = seg_ref[qb * BLK + BLK - 1]

        def on_block(kb, count):
            list_s[count] = kb - 2 * base
            src = block_rows(kb - 2 * base)
            dst = block_rows(count)
            k_s[dst, :] = kv_ref[src, :HEAD_SIZE]
            v_s[dst, :] = kv_ref[src, HEAD_SIZE:]
            whole = jnp.logical_and(kb < qb, seg_ref[kb * BLK] == q_last)

            @pl.when(whole)
            def _():
                bias_s[dst, :] = jnp.zeros((BLK, BLK), F32)

            @pl.when(jnp.logical_not(whole))
            def _():
                k_seg = jnp.broadcast_to(segv_ref[pl.ds(kb, 1), :].astype(F32), (BLK, BLK)).T
                k_pos = kb * BLK + iota((BLK, BLK), 0)
                q_pos = qb * BLK + iota((BLK, BLK), 1)
                ok = (k_seg == q_seg.astype(F32)) & (k_pos <= q_pos)
                bias_s[dst, :] = jnp.where(ok, 0.0, NEG_FILL)

        count, wide, narrow = visible_blocks(qb, seg_ref, allow_ref, on_block)

        def fill(n, c):
            list_s[n] = 2 * WINDOW
            dst = block_rows(n)
            k_s[dst, :] = jnp.zeros((BLK, HEAD_SIZE), BF16)
            v_s[dst, :] = jnp.zeros((BLK, HEAD_SIZE), BF16)
            bias_s[dst, :] = jnp.full((BLK, BLK), NEG_FILL, F32)
            return c

        lax.fori_loop(count, wide * WIDE + narrow * NARROW, fill, 0)

        @pl.when(half == 0)
        def _():
            for copy in copies[1:]:
                copy.wait()

        picks = unpack_ref[block_rows(half), :]
        for pair in range(LOCAL_HEADS // 2):
            q_two = dot(picks, recv_ref[:, pair * 256 : (pair + 1) * 256])
            for i in range(2):
                mine = slice((2 * pair + i) * BLK, (2 * pair + i + 1) * BLK)
                q_one = q_two[:, i * HEAD_SIZE : (i + 1) * HEAD_SIZE]
                qr_s[mine, :] = q_one.astype(BF16)
                qt_s[:, mine] = q_one.T.astype(BF16)

        def first_pass(start, blocks, slot, state):
            top, total, weighed = state
            rows = block_rows(start, blocks)
            scores = dot(k_s[rows, :], qt_s[...])
            scores = scores + jnp.concatenate([bias_s[rows, :]] * LOCAL_HEADS, axis=1)
            new_top = jnp.maximum(top, jnp.max(scores, axis=0, keepdims=True))
            factor = jnp.exp2((top - new_top) * EXP2_SCALE)
            e = jnp.exp2((scores - new_top) * EXP2_SCALE)
            dp = dot(v_s[rows, :], gt_ref[half])
            e_s[rows, :] = e
            dp_s[rows, :] = dp
            top_s[slot] = new_top
            total = total * factor + jnp.sum(e.reshape(-1, 8, LANES), axis=0)
            weighed = weighed * factor + jnp.sum((e * dp).reshape(-1, 8, LANES), axis=0)
            return (new_top, total, weighed)

        state = (
            jnp.full((1, LANES), NEG_FILL, F32),
            jnp.zeros((8, LANES), F32),
            jnp.zeros((8, LANES), F32),
        )
        state = lax.fori_loop(
            0, wide, lambda n, st: first_pass(n * WIDE, WIDE, n, st), state
        )
        top, total, weighed = lax.fori_loop(
            0, narrow, lambda n, st: first_pass(wide * WIDE, NARROW, wide, st), state
        )
        inverse = 1.0 / jnp.sum(total, axis=0, keepdims=True)
        out_dot = jnp.sum(weighed, axis=0, keepdims=True) * inverse

        def copy_out(start, blocks, buffer):
            return pltpu.make_async_copy(
                sg_s.at[buffer, pl.ds(0, blocks * BLK), :],
                sg_ref.at[half, block_rows(start, blocks), :],
                sent.at[buffer],
            )

        def second_pass(start, blocks, slot, buffer):
            rows = block_rows(start, blocks)
            factor = jnp.exp2((top_s[slot] - top) * EXP2_SCALE) * inverse
            weights = e_s[rows, :] * factor
            score_grad = (weights * (dp_s[rows, :] - out_dot)).astype(BF16)
            sg_s[buffer, : blocks * BLK, :] = score_grad
            copy_out(start, blocks, buffer).start()
            value_terms = dot(weights.astype(BF16), gr_ref[half])
            key_terms = dot(score_grad, qr_s[...])
            for n in range(blocks):
                dst = block_rows(list_s[start + n])
                acc_s[0, dst, :] += key_terms[n * BLK : (n + 1) * BLK, :]
                acc_s[1, dst, :] += value_terms[n * BLK : (n + 1) * BLK, :]

        def wide_step(n, c):
            @pl.when(n >= 2)
            def _():
                copy_out((n - 2) * WIDE, WIDE, n % 2).wait()

            second_pass(n * WIDE, WIDE, n, n % 2)
            return c

        lax.fori_loop(0, wide, wide_step, 0)

        @pl.when(narrow > 0)
        def _():
            second_pass(wide * WIDE, NARROW, wide, 2)
            copy_out(wide * WIDE, NARROW, 2).wait()

        for late in (1, 2):

            @pl.when(wide >= late)
            def _():
                copy_out((wide - late) * WIDE, WIDE, (wide - late) % 2).wait()

        return carry

    lax.fori_loop(0, 2, query_block, 0)
    rows = slice(0, WINDOW * TOK)

    @pl.when(core == 0)
    def _():
        keep_ref[...] = (acc_s[0, rows, :] * SCALE).astype(BF16)
        send_ref[...] = acc_s[1, rows, :].astype(BF16)

    @pl.when(core == 1)
    def _():
        keep_ref[...] = acc_s[1, rows, :].astype(BF16)
        send_ref[...] = (acc_s[0, rows, :] * SCALE).astype(BF16)


def query_grad_kernel(
    info_ref, seg_ref, allow_ref, kv_in, sg_ref, dq_ref, kt_s, dqt_s, sg_s, arrived, kv_ref, kv_sem
):
    shard = info_ref[0]
    base = jnp.maximum(shard - BACK, 0)
    copy = pltpu.make_async_copy(kv_in, kv_ref, kv_sem)
    copy.start()
    copy.wait()

    def query_block(half, carry):
        def on_block(kb, count):
            lanes = block_rows(count % NARROW)
            k_blk = kv_ref[block_rows(kb - 2 * base), :HEAD_SIZE]
            kt_s[count // NARROW, :, lanes] = k_blk.astype(F32).T.astype(BF16)

        count, wide, narrow = visible_blocks(shard * 2 + half, seg_ref, allow_ref, on_block)
        steps = wide * (WIDE // NARROW) + narrow

        def fill(n, c):
            lanes = block_rows(n % NARROW)
            kt_s[n // NARROW, :, lanes] = jnp.zeros((HEAD_SIZE, BLK), BF16)
            return c

        lax.fori_loop(count, steps * NARROW, fill, 0)

        def fetch(step):
            return pltpu.make_async_copy(
                sg_ref.at[half, block_rows(step * NARROW, NARROW), :],
                sg_s.at[step % 2],
                arrived.at[step % 2],
            )

        fetch(0).start()
        dqt_s[...] = jnp.zeros_like(dqt_s)

        def one_step(step, c):
            @pl.when(step + 1 < steps)
            def _():
                fetch(step + 1).start()

            fetch(step).wait()
            dqt_s[...] += dot(kt_s[step], sg_s[step % 2])
            return c

        lax.fori_loop(0, steps, one_step, 0)
        for h in range(LOCAL_HEADS):
            block = dqt_s[:, h * BLK : (h + 1) * BLK] * SCALE
            dq_ref[block_rows(half), h * HEAD_SIZE : (h + 1) * HEAD_SIZE] = block.T.astype(BF16)
        return carry

    lax.fori_loop(0, 2, query_block, 0)


def merge_kernel(info_ref, keep_in, recv_in, out_ref, keep_s, recv_s, sum_s, zero_s, sems):
    base = jnp.maximum(info_ref[0] - BACK, 0)
    loads = fetch_all((keep_in, recv_in), (keep_s, recv_s), sems)
    zero_s[...] = jnp.zeros_like(zero_s)
    stores = []
    for i in range(SHARDS - WINDOW):
        n = jnp.where(i < base, i, i + WINDOW)
        rows = pl.ds(pl.multiple_of(n * TOK, TOK), TOK)
        stores.append(pltpu.make_async_copy(zero_s, out_ref.at[rows, :], sems.at[2 + i]))
    for store in stores:
        store.start()
    for load in loads:
        load.wait()
    sum_s[...] = (keep_s[...].astype(F32) + recv_s[...].astype(F32)).astype(BF16)
    rows = pl.ds(pl.multiple_of(base * TOK, TOK), WINDOW * TOK)
    window = pltpu.make_async_copy(sum_s, out_ref.at[rows, :], sems.at[2 + SHARDS - WINDOW])
    window.start()
    for store in stores:
        store.wait()
    window.wait()


VMEM = pl.BlockSpec(memory_space=pltpu.VMEM)
SMEM = pl.BlockSpec(memory_space=pltpu.SMEM)


ANY = pl.BlockSpec(memory_space=pl.ANY)


def call_permute(info, grad, own, mine, theirs):
    return pl.pallas_call(
        permute_kernel,
        in_specs=[SMEM] + [ANY] * (2 * RING + 2),
        out_specs=[VMEM] * 4,
        out_shape=[
            jax.ShapeDtypeStruct((WINDOW * TOK, 2 * HEAD_SIZE), BF16),
            jax.ShapeDtypeStruct((TOK, SHARDS * SLOTS), BF16),
            jax.ShapeDtypeStruct((2, LANES, HEAD_SIZE), BF16),
            jax.ShapeDtypeStruct((2, HEAD_SIZE, LANES), BF16),
        ],
        scratch_shapes=[pltpu.VMEM((SHARDS * SLOTS, TOK), F32)]
        + [pltpu.VMEM(x.shape, x.dtype) for x in (grad, own, *mine, *theirs)]
        + [pltpu.SemaphoreType.DMA((2 * RING + 2,))],
        compiler_params=pltpu.CompilerParams(vmem_limit_bytes=VMEM_LIMIT),
        name="permute",
    )(info, grad, own, *mine, *theirs)


def call_attention(info, segments, allow, unpack, q_recv, gr, gt, kv_window):
    return pl.pallas_call(
        attention_kernel,
        in_specs=[SMEM, SMEM, SMEM, VMEM] + [ANY] * 5,
        out_specs=[VMEM, VMEM, ANY],
        out_shape=[
            jax.ShapeDtypeStruct((WINDOW * TOK, HEAD_SIZE), BF16),
            jax.ShapeDtypeStruct((WINDOW * TOK, HEAD_SIZE), BF16),
            jax.ShapeDtypeStruct((2, MOST_BLOCKS * BLK, LANES), BF16),
        ],
        scratch_shapes=[
            pltpu.VMEM((LANES, HEAD_SIZE), BF16),
            pltpu.VMEM((HEAD_SIZE, LANES), BF16),
            pltpu.VMEM((MOST_BLOCKS * BLK, HEAD_SIZE), BF16),
            pltpu.VMEM((MOST_BLOCKS * BLK, HEAD_SIZE), BF16),
            pltpu.VMEM((MOST_BLOCKS * BLK, BLK), F32),
            pltpu.VMEM((MOST_BLOCKS * BLK, LANES), F32),
            pltpu.VMEM((MOST_BLOCKS * BLK, LANES), F32),
            pltpu.VMEM((MOST_BLOCKS // WIDE + 1, 1, LANES), F32),
            pltpu.VMEM((2, WINDOW * TOK + BLK, HEAD_SIZE), F32),
            pltpu.VMEM((3, WIDE * BLK, LANES), BF16),
            pltpu.SMEM((MOST_BLOCKS,), jnp.int32),
            pltpu.SemaphoreType.DMA((3,)),
        ]
        + [pltpu.VMEM(x.shape, x.dtype) for x in (kv_window, unpack, q_recv, gr, gt)]
        + [pltpu.SemaphoreType.DMA((5,))],
        compiler_params=pltpu.CompilerParams(vmem_limit_bytes=VMEM_LIMIT),
        name="attention",
    )(info, segments, allow, segments.reshape(-1, BLK), unpack, q_recv, gr, gt, kv_window)


def call_query_grad(info, segments, allow, kv_window, score_grad):
    return pl.pallas_call(
        query_grad_kernel,
        in_specs=[SMEM, SMEM, SMEM, ANY, ANY],
        out_specs=VMEM,
        out_shape=jax.ShapeDtypeStruct((TOK, LOCAL_HEADS * HEAD_SIZE), BF16),
        scratch_shapes=[
            pltpu.VMEM((MOST_BLOCKS // NARROW, HEAD_SIZE, NARROW * BLK), BF16),
            pltpu.VMEM((HEAD_SIZE, LANES), F32),
            pltpu.VMEM((2, NARROW * BLK, LANES), BF16),
            pltpu.SemaphoreType.DMA((2,)),
            pltpu.VMEM(kv_window.shape, BF16),
            pltpu.SemaphoreType.DMA(()),
        ],
        compiler_params=pltpu.CompilerParams(vmem_limit_bytes=VMEM_LIMIT),
        cost_estimate=pl.CostEstimate(
            flops=2 * TOK * 2048 * LANES, bytes_accessed=12 * 2**20, transcendentals=0
        ),
        name="query_grad",
    )(info, segments, allow, kv_window, score_grad)


def on_device(queries, keys_values, out_grad, place, segments, allow):
    tp_index = lax.axis_index("tp")
    ctx_index = lax.axis_index("ctx")
    tp_size = lax.axis_size("tp")
    width = LOCAL_HEADS * HEAD_SIZE
    info = jnp.stack([ctx_index, tp_index % 2]).astype(jnp.int32)
    staged = pl.pallas_call(
        stage_kernel,
        in_specs=[VMEM, pl.BlockSpec(memory_space=pl.ANY)],
        out_specs=VMEM,
        out_shape=jax.ShapeDtypeStruct((TOK + META, 2 * HEAD_SIZE), BF16),
        scratch_shapes=[pltpu.SemaphoreType.DMA((2,))],
        name="stage",
    )(place.reshape(1, TOK), keys_values)
    beside = lax.ppermute(staged, "ctx", [(k, k ^ 1) for k in range(SHARDS)])
    own = jnp.stack([staged, beside])

    def around(hops):
        pairs = []
        for k in range(SHARDS * tp_size):
            ctx, tp = k // tp_size, k % tp_size
            far = (ctx + (2 * hops if tp % 2 == 0 else -2 * hops)) % SHARDS
            pairs.append((k, far * tp_size + tp))
        return pairs

    swap = [(k, k ^ 1) for k in range(tp_size)]
    first = lax.ppermute(own, ("ctx", "tp"), around(1))
    second = lax.ppermute(first, ("ctx", "tp"), around(1))
    third = lax.ppermute(second, ("ctx", "tp"), around(1))
    half = lax.dynamic_index_in_dim(second, tp_index % 2, 0, keepdims=False)
    fourth = lax.ppermute(half, ("ctx", "tp"), around(2))
    mine = [first, second, third, fourth]
    g_local = lax.all_to_all(out_grad, "tp", split_axis=1, concat_axis=0, tiled=True)
    q_send = pl.pallas_call(
        pack_kernel,
        in_specs=[VMEM, VMEM],
        out_specs=VMEM,
        out_shape=jax.ShapeDtypeStruct((SHARDS * SLOTS, width), BF16),
        name="pack",
    )(place.reshape(1, TOK), queries)
    q_send, *mine = lax.optimization_barrier((q_send, *mine))
    theirs = [lax.ppermute(piece, "tp", swap) for piece in mine]
    q_recv = lax.all_to_all(q_send, "ctx", split_axis=0, concat_axis=0, tiled=True)
    kv_window, unpack, gr, gt = call_permute(info, g_local, own, mine, theirs)
    keep, send, score_grad = call_attention(
        info, segments, allow, unpack, q_recv, gr, gt, kv_window
    )
    recv = lax.ppermute(send, "tp", swap)
    part = pl.pallas_call(
        merge_kernel,
        in_specs=[SMEM, ANY, ANY],
        out_specs=ANY,
        out_shape=jax.ShapeDtypeStruct((SHARDS * TOK, HEAD_SIZE), BF16),
        scratch_shapes=[pltpu.VMEM((WINDOW * TOK, HEAD_SIZE), BF16)] * 3
        + [
            pltpu.VMEM((TOK, HEAD_SIZE), BF16),
            pltpu.SemaphoreType.DMA((3 + SHARDS - WINDOW,)),
        ],
        compiler_params=pltpu.CompilerParams(vmem_limit_bytes=VMEM_LIMIT),
        name="merge",
    )(info, keep, recv)
    part, score_grad = lax.optimization_barrier((part, score_grad))
    parts = lax.all_to_all(
        part.reshape(SHARDS, TOK, HEAD_SIZE), "ctx", split_axis=0, concat_axis=0, tiled=True
    )
    grad_q = call_query_grad(info, segments, allow, kv_window, score_grad)
    owned = jnp.sum(parts.astype(F32), axis=0).astype(BF16)
    owned, grad_q = lax.optimization_barrier((owned, grad_q))
    heads = lax.all_to_all(
        owned.reshape(tp_size, TOK // tp_size, HEAD_SIZE),
        "tp",
        split_axis=0,
        concat_axis=0,
        tiled=True,
    )
    key_value_gradient = (
        heads.reshape(KEY_VALUE_HEADS, 2, TOK // tp_size, HEAD_SIZE)
        .transpose(1, 2, 0, 3)
        .reshape(2, TOK // tp_size, KEY_VALUE_HEADS * HEAD_SIZE)
    )
    return (grad_q, key_value_gradient)


def solution(mesh):
    in_specs = (P("ctx", "tp"), P(None, "ctx", None), P(("ctx", "tp"), None), P("ctx"), P(), P())
    out_specs = (P("ctx", "tp"), P(None, ("ctx", "tp"), None))
    return jax.shard_map(
        on_device, mesh=mesh, in_specs=in_specs, out_specs=out_specs, check_vma=False
    )
```

```python
import functools
import math

import jax
import jax.numpy as jnp
from jax import lax
from jax.experimental import pallas as pl
from jax.experimental.pallas import tpu as pltpu
from jax.sharding import Mesh
from jax.sharding import PartitionSpec as P

QUERY_HEAD_COUNT = 128
KEY_VALUE_HEADS = 8
HEAD_SIZE = 128
BLK = 128
TOK = 256
SHARDS = 16
SLOTS = 32
META = 16
Z_CHIPS = SHARDS // 2
RING = Z_CHIPS // 2
DOC_MOST = 2304
BACK = -(-DOC_MOST // TOK)
WINDOW = BACK + 1
BLOCKS_BACK = -(-DOC_MOST // BLK)
WIDE = 4
NARROW = 2
MOST_BLOCKS = WIDE * -(-(BLOCKS_BACK + 1) // WIDE)
LOCAL_HEADS = 8
LANES = LOCAL_HEADS * BLK
NEG_FILL = -1e30
VMEM_LIMIT = 60 * 2**20
SCALE = 1.0 / math.sqrt(HEAD_SIZE)
EXP2_SCALE = SCALE * math.log2(math.e)
F32 = jnp.float32
BF16 = jnp.bfloat16


def iota(shape, dim):
    return lax.broadcasted_iota(jnp.int32, shape, dim)


def dot(a, b):
    return jnp.dot(a, b, preferred_element_type=F32)


def ranks_within(member):
    earlier = (iota((TOK, TOK), 0) < iota((TOK, TOK), 1)).astype(F32).astype(BF16)
    counts = dot(member.astype(F32).astype(BF16), earlier)
    return jnp.where(member, counts, -1.0)


def pack_kernel(place_ref, rows_ref, out_ref):
    owner = place_ref[...] >> 8
    rank = ranks_within(owner == iota((SHARDS, TOK), 0))
    slot = iota((SLOTS, TOK), 0).astype(F32)
    picks = jnp.concatenate(
        [(rank[s : s + 1, :] == slot).astype(F32) for s in range(SHARDS)], axis=0
    ).astype(BF16)
    for first in range(0, rows_ref.shape[1], 256):
        cols = pl.ds(first, 256)
        out_ref[:, cols] = dot(picks, rows_ref[:, cols]).astype(BF16)


def stage_kernel(place_ref, kv_ref, out_ref, arrived):
    cols = pl.ds(pl.multiple_of((lax.axis_index("tp") // 2) * HEAD_SIZE, HEAD_SIZE), HEAD_SIZE)
    copies = [
        pltpu.make_async_copy(
            kv_ref.at[i, :, cols],
            out_ref.at[pl.ds(0, TOK), pl.ds(i * HEAD_SIZE, HEAD_SIZE)],
            arrived.at[i],
        )
        for i in range(2)
    ]
    for copy in copies:
        copy.start()
    place = place_ref[...]
    row = iota((META, TOK), 0)
    owner = jnp.broadcast_to((place >> 8).astype(F32), (META, TOK))
    within = jnp.broadcast_to((place & (TOK - 1)).astype(F32), (META, TOK))
    meta = jnp.where(row == 0, owner, jnp.where(row == 1, within, 0.0))
    out_ref[TOK:, :] = meta.astype(BF16)
    for copy in copies:
        copy.wait()


def fetch_all(sources, buffers, arrived):
    copies = [
        pltpu.make_async_copy(source, buffer, arrived.at[i])
        for i, (source, buffer) in enumerate(zip(sources, buffers))
    ]
    for copy in copies:
        copy.start()
    return copies


def permute_kernel(info_ref, *refs):
    count = 2 * RING + 2
    out_ref, unpack_ref, gr_ref, gt_ref, slots_s = refs[count : count + 5]
    grad_ref, own_ref = refs[count + 5 : count + 7]
    mine = refs[count + 7 : count + 7 + RING]
    theirs = refs[count + 7 + RING : count + 7 + 2 * RING]
    for copy in fetch_all(refs[:count], refs[count + 5 : -1], refs[-1]):
        copy.wait()
    shard = info_ref[0]
    core = info_ref[1]
    base = jnp.maximum(shard - BACK, 0)
    z, x = shard // 2, shard % 2
    sources = [(own_ref.at[j], shard ^ j) for j in range(2)]
    for refs_k, side in ((mine, core), (theirs, 1 - core)):
        for k in range(1, RING):
            far = (z + k * (2 * side - 1) + Z_CHIPS) % Z_CHIPS
            sources += [(refs_k[k - 1].at[j], 2 * far + (x ^ j)) for j in range(2)]
        far = (z + RING) % Z_CHIPS
        sources += [(refs_k[RING - 1], 2 * far + (x ^ side))]
    owners = jnp.concatenate([ref[TOK : TOK + 1, :].astype(F32) for ref, _ in sources], axis=0)
    within = jnp.concatenate([ref[TOK + 1 : TOK + 2, :].astype(F32) for ref, _ in sources], axis=0)
    rank = ranks_within(owners == shard.astype(F32))
    slot = iota((SLOTS, TOK), 0).astype(F32)
    lane = iota((SLOTS, TOK), 1).astype(F32)
    for i, (_, source) in enumerate(sources):
        hit = rank[i : i + 1, :] == slot
        landing = jnp.sum(jnp.where(hit, within[i : i + 1, :] + 1.0, 0.0), axis=1, keepdims=True)
        rows = pl.ds(pl.multiple_of(source * SLOTS, SLOTS), SLOTS)
        slots_s[rows, :] = (landing == lane + 1.0).astype(F32)
    unpack_ref[...] = slots_s[...].T.astype(BF16)
    for half in range(2):
        for h in range(LOCAL_HEADS):
            block = grad_ref[half * BLK : (half + 1) * BLK, h * HEAD_SIZE : (h + 1) * HEAD_SIZE]
            gr_ref[half, h * BLK : (h + 1) * BLK, :] = block
            gt_ref[half, :, h * BLK : (h + 1) * BLK] = block.astype(F32).T.astype(BF16)

    def one_shard(i, carry):
        rows = iota((TOK, TOK), 0).astype(F32)
        goal = jnp.where(owners == (base + i).astype(F32), within, -1.0)
        total = jnp.zeros((TOK, 2 * HEAD_SIZE), F32)
        for n, (ref, _) in enumerate(sources):
            picks = (goal[n : n + 1, :] == rows).astype(F32).astype(BF16)
            total = total + dot(picks, ref[:TOK, :])
        out_ref[pl.ds(pl.multiple_of(i * TOK, TOK), TOK), :] = total.astype(BF16)
        return carry

    lax.fori_loop(0, shard - base + 1, one_shard, 0)


def visible_blocks(qb, seg_ref, allow_ref, on_block):
    q_first = seg_ref[qb * BLK]

    def scan(kb, count):
        seen = jnp.logical_and(seg_ref[kb * BLK + BLK - 1] >= q_first, allow_ref[qb, kb] != 0)

        @pl.when(seen)
        def _():
            on_block(kb, count)

        return count + seen.astype(jnp.int32)

    count = lax.fori_loop(jnp.maximum(qb - BLOCKS_BACK, 0), qb + 1, scan, 0)
    wide = (count + 1) // WIDE
    narrow = (count + WIDE - 1) // WIDE - wide
    return count, wide, narrow


def parity_block(kb):
    shard = kb // 2
    return ((shard % 2) * Z_CHIPS + shard // 2) * 2 + kb % 2


def block_rows(n, blocks=1):
    return pl.ds(pl.multiple_of(n * BLK, BLK), blocks * BLK)


def attention_kernel(
    info_ref,
    seg_ref,
    allow_ref,
    segv_ref,
    unpack_in,
    recv_in,
    gr_in,
    gt_in,
    kv_in,
    keep_ref,
    send_ref,
    sg_ref,
    qr_s,
    qt_s,
    k_s,
    v_s,
    bias_s,
    e_s,
    dp_s,
    top_s,
    acc_s,
    sg_s,
    list_s,
    sent,
    kv_ref,
    unpack_ref,
    recv_ref,
    gr_ref,
    gt_ref,
    arrived,
):
    shard = info_ref[0]
    core = info_ref[1]
    base = jnp.maximum(shard - BACK, 0)
    copies = fetch_all(
        (kv_in, unpack_in, recv_in, gr_in, gt_in),
        (kv_ref, unpack_ref, recv_ref, gr_ref, gt_ref),
        arrived,
    )
    acc_s[...] = jnp.zeros_like(acc_s)
    copies[0].wait()

    def query_block(half, carry):
        qb = shard * 2 + half
        q_seg = segv_ref[pl.ds(qb, 1), :]
        q_last = seg_ref[qb * BLK + BLK - 1]

        def on_block(kb, count):
            list_s[count] = parity_block(kb)
            src = block_rows(kb - 2 * base)
            dst = block_rows(count)
            k_s[dst, :] = kv_ref[src, :HEAD_SIZE]
            v_s[dst, :] = kv_ref[src, HEAD_SIZE:]
            whole = jnp.logical_and(kb < qb, seg_ref[kb * BLK] == q_last)

            @pl.when(whole)
            def _():
                bias_s[dst, :] = jnp.zeros((BLK, BLK), F32)

            @pl.when(jnp.logical_not(whole))
            def _():
                k_seg = jnp.broadcast_to(segv_ref[pl.ds(kb, 1), :].astype(F32), (BLK, BLK)).T
                k_pos = kb * BLK + iota((BLK, BLK), 0)
                q_pos = qb * BLK + iota((BLK, BLK), 1)
                ok = (k_seg == q_seg.astype(F32)) & (k_pos <= q_pos)
                bias_s[dst, :] = jnp.where(ok, 0.0, NEG_FILL)

        count, wide, narrow = visible_blocks(qb, seg_ref, allow_ref, on_block)

        def fill(n, c):
            list_s[n] = 2 * SHARDS
            dst = block_rows(n)
            k_s[dst, :] = jnp.zeros((BLK, HEAD_SIZE), BF16)
            v_s[dst, :] = jnp.zeros((BLK, HEAD_SIZE), BF16)
            bias_s[dst, :] = jnp.full((BLK, BLK), NEG_FILL, F32)
            return c

        lax.fori_loop(count, wide * WIDE + narrow * NARROW, fill, 0)

        @pl.when(half == 0)
        def _():
            for copy in copies[1:]:
                copy.wait()

        picks = unpack_ref[block_rows(half), :]
        for pair in range(LOCAL_HEADS // 2):
            q_two = dot(picks, recv_ref[:, pair * 256 : (pair + 1) * 256])
            for i in range(2):
                mine = slice((2 * pair + i) * BLK, (2 * pair + i + 1) * BLK)
                q_one = q_two[:, i * HEAD_SIZE : (i + 1) * HEAD_SIZE]
                qr_s[mine, :] = q_one.astype(BF16)
                qt_s[:, mine] = q_one.T.astype(BF16)

        def first_pass(start, blocks, slot, state):
            top, total, weighed = state
            rows = block_rows(start, blocks)
            scores = dot(k_s[rows, :], qt_s[...])
            scores = scores + jnp.concatenate([bias_s[rows, :]] * LOCAL_HEADS, axis=1)
            new_top = jnp.maximum(top, jnp.max(scores, axis=0, keepdims=True))
            factor = jnp.exp2((top - new_top) * EXP2_SCALE)
            e = jnp.exp2((scores - new_top) * EXP2_SCALE)
            dp = dot(v_s[rows, :], gt_ref[half])
            e_s[rows, :] = e
            dp_s[rows, :] = dp
            top_s[slot] = new_top
            total = total * factor + jnp.sum(e.reshape(-1, 8, LANES), axis=0)
            weighed = weighed * factor + jnp.sum((e * dp).reshape(-1, 8, LANES), axis=0)
            return (new_top, total, weighed)

        state = (
            jnp.full((1, LANES), NEG_FILL, F32),
            jnp.zeros((8, LANES), F32),
            jnp.zeros((8, LANES), F32),
        )
        state = lax.fori_loop(
            0, wide, lambda n, st: first_pass(n * WIDE, WIDE, n, st), state
        )
        top, total, weighed = lax.fori_loop(
            0, narrow, lambda n, st: first_pass(wide * WIDE, NARROW, wide, st), state
        )
        inverse = 1.0 / jnp.sum(total, axis=0, keepdims=True)
        out_dot = jnp.sum(weighed, axis=0, keepdims=True) * inverse

        def copy_out(start, blocks, buffer):
            return pltpu.make_async_copy(
                sg_s.at[buffer, pl.ds(0, blocks * BLK), :],
                sg_ref.at[half, block_rows(start, blocks), :],
                sent.at[buffer],
            )

        def second_pass(start, blocks, slot, buffer):
            rows = block_rows(start, blocks)
            factor = jnp.exp2((top_s[slot] - top) * EXP2_SCALE) * inverse
            weights = e_s[rows, :] * factor
            score_grad = (weights * (dp_s[rows, :] - out_dot)).astype(BF16)
            sg_s[buffer, : blocks * BLK, :] = score_grad
            copy_out(start, blocks, buffer).start()
            value_terms = dot(weights.astype(BF16), gr_ref[half])
            key_terms = dot(score_grad, qr_s[...])
            for n in range(blocks):
                dst = block_rows(list_s[start + n])
                acc_s[0, dst, :] += key_terms[n * BLK : (n + 1) * BLK, :]
                acc_s[1, dst, :] += value_terms[n * BLK : (n + 1) * BLK, :]

        def wide_step(n, c):
            @pl.when(n >= 2)
            def _():
                copy_out((n - 2) * WIDE, WIDE, n % 2).wait()

            second_pass(n * WIDE, WIDE, n, n % 2)
            return c

        lax.fori_loop(0, wide, wide_step, 0)

        @pl.when(narrow > 0)
        def _():
            second_pass(wide * WIDE, NARROW, wide, 2)
            copy_out(wide * WIDE, NARROW, 2).wait()

        for late in (1, 2):

            @pl.when(wide >= late)
            def _():
                copy_out((wide - late) * WIDE, WIDE, (wide - late) % 2).wait()

        return carry

    lax.fori_loop(0, 2, query_block, 0)
    rows = slice(0, SHARDS * TOK)

    @pl.when(core == 0)
    def _():
        keep_ref[...] = (acc_s[0, rows, :] * SCALE).astype(BF16)
        send_ref[...] = acc_s[1, rows, :].astype(BF16)

    @pl.when(core == 1)
    def _():
        keep_ref[...] = acc_s[1, rows, :].astype(BF16)
        send_ref[...] = (acc_s[0, rows, :] * SCALE).astype(BF16)


def query_grad_kernel(
    info_ref, seg_ref, allow_ref, kv_in, sg_ref, dq_ref, kt_s, dqt_s, sg_s, arrived, kv_ref, kv_sem
):
    shard = info_ref[0]
    base = jnp.maximum(shard - BACK, 0)
    copy = pltpu.make_async_copy(kv_in, kv_ref, kv_sem)
    copy.start()
    copy.wait()

    def query_block(half, carry):
        def on_block(kb, count):
            lanes = block_rows(count % NARROW)
            k_blk = kv_ref[block_rows(kb - 2 * base), :HEAD_SIZE]
            kt_s[count // NARROW, :, lanes] = k_blk.astype(F32).T.astype(BF16)

        count, wide, narrow = visible_blocks(shard * 2 + half, seg_ref, allow_ref, on_block)
        steps = wide * (WIDE // NARROW) + narrow

        def fill(n, c):
            lanes = block_rows(n % NARROW)
            kt_s[n // NARROW, :, lanes] = jnp.zeros((HEAD_SIZE, BLK), BF16)
            return c

        lax.fori_loop(count, steps * NARROW, fill, 0)

        def fetch(step):
            return pltpu.make_async_copy(
                sg_ref.at[half, block_rows(step * NARROW, NARROW), :],
                sg_s.at[step % 2],
                arrived.at[step % 2],
            )

        fetch(0).start()
        dqt_s[...] = jnp.zeros_like(dqt_s)

        def one_step(step, c):
            @pl.when(step + 1 < steps)
            def _():
                fetch(step + 1).start()

            fetch(step).wait()
            dqt_s[...] += dot(kt_s[step], sg_s[step % 2])
            return c

        lax.fori_loop(0, steps, one_step, 0)
        for h in range(LOCAL_HEADS):
            block = dqt_s[:, h * BLK : (h + 1) * BLK] * SCALE
            dq_ref[block_rows(half), h * HEAD_SIZE : (h + 1) * HEAD_SIZE] = block.T.astype(BF16)
        return carry

    lax.fori_loop(0, 2, query_block, 0)


VMEM = pl.BlockSpec(memory_space=pltpu.VMEM)
SMEM = pl.BlockSpec(memory_space=pltpu.SMEM)


ANY = pl.BlockSpec(memory_space=pl.ANY)
HBM = pl.BlockSpec(memory_space=pltpu.HBM)


def call_permute(info, grad, own, mine, theirs):
    return pl.pallas_call(
        permute_kernel,
        in_specs=[SMEM] + [HBM] * (2 * RING + 2),
        out_specs=[VMEM] * 4,
        out_shape=[
            jax.ShapeDtypeStruct((WINDOW * TOK, 2 * HEAD_SIZE), BF16),
            jax.ShapeDtypeStruct((TOK, SHARDS * SLOTS), BF16),
            jax.ShapeDtypeStruct((2, LANES, HEAD_SIZE), BF16),
            jax.ShapeDtypeStruct((2, HEAD_SIZE, LANES), BF16),
        ],
        scratch_shapes=[pltpu.VMEM((SHARDS * SLOTS, TOK), F32)]
        + [pltpu.VMEM(x.shape, x.dtype) for x in (grad, own, *mine, *theirs)]
        + [pltpu.SemaphoreType.DMA((2 * RING + 2,))],
        compiler_params=pltpu.CompilerParams(vmem_limit_bytes=VMEM_LIMIT),
        name="permute",
    )(info, grad, own, *mine, *theirs)


def call_attention(info, segments, allow, unpack, q_recv, gr, gt, kv_window):
    return pl.pallas_call(
        attention_kernel,
        in_specs=[SMEM, SMEM, SMEM, VMEM] + [HBM] * 5,
        out_specs=[VMEM, VMEM, HBM],
        out_shape=[
            jax.ShapeDtypeStruct((SHARDS * TOK, HEAD_SIZE), BF16),
            jax.ShapeDtypeStruct((SHARDS * TOK, HEAD_SIZE), BF16),
            jax.ShapeDtypeStruct((2, MOST_BLOCKS * BLK, LANES), BF16),
        ],
        scratch_shapes=[
            pltpu.VMEM((LANES, HEAD_SIZE), BF16),
            pltpu.VMEM((HEAD_SIZE, LANES), BF16),
            pltpu.VMEM((MOST_BLOCKS * BLK, HEAD_SIZE), BF16),
            pltpu.VMEM((MOST_BLOCKS * BLK, HEAD_SIZE), BF16),
            pltpu.VMEM((MOST_BLOCKS * BLK, BLK), F32),
            pltpu.VMEM((MOST_BLOCKS * BLK, LANES), F32),
            pltpu.VMEM((MOST_BLOCKS * BLK, LANES), F32),
            pltpu.VMEM((MOST_BLOCKS // WIDE + 1, 1, LANES), F32),
            pltpu.VMEM((2, SHARDS * TOK + BLK, HEAD_SIZE), F32),
            pltpu.VMEM((3, WIDE * BLK, LANES), BF16),
            pltpu.SMEM((MOST_BLOCKS,), jnp.int32),
            pltpu.SemaphoreType.DMA((3,)),
        ]
        + [pltpu.VMEM(x.shape, x.dtype) for x in (kv_window, unpack, q_recv, gr, gt)]
        + [pltpu.SemaphoreType.DMA((5,))],
        compiler_params=pltpu.CompilerParams(vmem_limit_bytes=VMEM_LIMIT),
        name="attention",
    )(info, segments, allow, segments.reshape(-1, BLK), unpack, q_recv, gr, gt, kv_window)


def call_query_grad(info, segments, allow, kv_window, score_grad):
    return pl.pallas_call(
        query_grad_kernel,
        in_specs=[SMEM, SMEM, SMEM, HBM, HBM],
        out_specs=VMEM,
        out_shape=jax.ShapeDtypeStruct((TOK, LOCAL_HEADS * HEAD_SIZE), BF16),
        scratch_shapes=[
            pltpu.VMEM((MOST_BLOCKS // NARROW, HEAD_SIZE, NARROW * BLK), BF16),
            pltpu.VMEM((HEAD_SIZE, LANES), F32),
            pltpu.VMEM((2, NARROW * BLK, LANES), BF16),
            pltpu.SemaphoreType.DMA((2,)),
            pltpu.VMEM(kv_window.shape, BF16),
            pltpu.SemaphoreType.DMA(()),
        ],
        compiler_params=pltpu.CompilerParams(vmem_limit_bytes=VMEM_LIMIT),
        cost_estimate=pl.CostEstimate(
            flops=2 * TOK * 2048 * LANES, bytes_accessed=12 * 2**20, transcendentals=0
        ),
        name="query_grad",
    )(info, segments, allow, kv_window, score_grad)


def on_device(queries, keys_values, out_grad, place, segments, allow):
    tp_index = lax.axis_index("tp")
    ctx_index = lax.axis_index(("z", "x"))
    tp_size = lax.axis_size("tp")
    width = LOCAL_HEADS * HEAD_SIZE
    info = jnp.stack([ctx_index, tp_index % 2]).astype(jnp.int32)
    staged = pl.pallas_call(
        stage_kernel,
        in_specs=[VMEM, pl.BlockSpec(memory_space=pl.ANY)],
        out_specs=VMEM,
        out_shape=jax.ShapeDtypeStruct((TOK + META, 2 * HEAD_SIZE), BF16),
        scratch_shapes=[pltpu.SemaphoreType.DMA((2,))],
        name="stage",
    )(place.reshape(1, TOK), keys_values)
    beside = lax.ppermute(staged, "x", [(0, 1), (1, 0)])
    own = jnp.stack([staged, beside])

    def around(hops):
        pairs = []
        for k in range(SHARDS * tp_size):
            ctx, tp = k // tp_size, k % tp_size
            far = (ctx + (2 * hops if tp % 2 == 0 else -2 * hops)) % SHARDS
            pairs.append((k, far * tp_size + tp))
        return pairs

    swap = [(k, k ^ 1) for k in range(tp_size)]
    first = lax.ppermute(own, ("z", "x", "tp"), around(1))
    second = lax.ppermute(first, ("z", "x", "tp"), around(1))
    third = lax.ppermute(second, ("z", "x", "tp"), around(1))
    half = lax.dynamic_index_in_dim(second, tp_index % 2, 0, keepdims=False)
    fourth = lax.ppermute(half, ("z", "x", "tp"), around(2))
    mine = [first, second, third, fourth]
    g_local = lax.all_to_all(out_grad, "tp", split_axis=1, concat_axis=0, tiled=True)
    q_send = pl.pallas_call(
        pack_kernel,
        in_specs=[VMEM, VMEM],
        out_specs=VMEM,
        out_shape=jax.ShapeDtypeStruct((SHARDS * SLOTS, width), BF16),
        name="pack",
    )(place.reshape(1, TOK), queries)
    q_send, *mine = lax.optimization_barrier((q_send, *mine))
    theirs = [lax.ppermute(piece, "tp", swap) for piece in mine]
    q_recv = lax.all_to_all(q_send, ("z", "x"), split_axis=0, concat_axis=0, tiled=True)
    kv_window, unpack, gr, gt = call_permute(info, g_local, own, mine, theirs)
    keep, send, score_grad = call_attention(
        info, segments, allow, unpack, q_recv, gr, gt, kv_window
    )
    recv = lax.ppermute(send, "tp", swap)
    halves = (2, Z_CHIPS, TOK, HEAD_SIZE)
    x_index = lax.axis_index("x")

    def summed(parity):
        terms = [
            lax.dynamic_index_in_dim(term.reshape(halves), parity, 0, keepdims=False)
            for term in (keep, recv)
        ]
        return (terms[0].astype(F32) + terms[1].astype(F32)).astype(BF16)

    beside = lax.ppermute(summed(1 - x_index), "x", [(0, 1), (1, 0)])
    part = (summed(x_index).astype(F32) + beside.astype(F32)).astype(BF16)
    part, score_grad = lax.optimization_barrier((part, score_grad))
    parts = lax.all_to_all(part, "z", split_axis=0, concat_axis=0, tiled=True)
    grad_q = call_query_grad(info, segments, allow, kv_window, score_grad)
    owned = jnp.sum(parts.astype(F32), axis=0).astype(BF16)
    owned, grad_q = lax.optimization_barrier((owned, grad_q))
    heads = lax.all_to_all(
        owned.reshape(tp_size, TOK // tp_size, HEAD_SIZE),
        "tp",
        split_axis=0,
        concat_axis=0,
        tiled=True,
    )
    key_value_gradient = (
        heads.reshape(KEY_VALUE_HEADS, 2, TOK // tp_size, HEAD_SIZE)
        .transpose(1, 2, 0, 3)
        .reshape(2, TOK // tp_size, KEY_VALUE_HEADS * HEAD_SIZE)
    )
    return (grad_q, key_value_gradient)


def solution(mesh):
    tp_size = mesh.shape["tp"]
    split = Mesh(mesh.devices.reshape(Z_CHIPS, 2, tp_size), ("z", "x", "tp"))
    ctx = ("z", "x")
    in_specs = (P(ctx, "tp"), P(None, ctx, None), P((*ctx, "tp"), None), P(ctx), P(), P())
    out_specs = (P(ctx, "tp"), P(None, (*ctx, "tp"), None))
    return jax.shard_map(
        on_device, mesh=split, in_specs=in_specs, out_specs=out_specs, check_vma=False
    )
```

```python
import functools
import math

import jax
import jax.numpy as jnp
from jax import lax
from jax.experimental import pallas as pl
from jax.experimental.pallas import tpu as pltpu
from jax.sharding import Mesh
from jax.sharding import PartitionSpec as P

QUERY_HEAD_COUNT = 128
KEY_VALUE_HEADS = 8
HEAD_SIZE = 128
BLK = 128
TOK = 256
SHARDS = 16
SLOTS = 32
META = 16
Z_CHIPS = SHARDS // 2
RING = Z_CHIPS // 2
DOC_MOST = 2304
Z_BACK = -(-DOC_MOST // (2 * TOK))
Z_SPAN = min(Z_BACK + 1, Z_CHIPS)
BACK = -(-DOC_MOST // TOK)
WINDOW = BACK + 1
BLOCKS_BACK = -(-DOC_MOST // BLK)
WIDE = 4
NARROW = 2
MOST_BLOCKS = WIDE * -(-(BLOCKS_BACK + 1) // WIDE)
LOCAL_HEADS = 8
LANES = LOCAL_HEADS * BLK
NEG_FILL = -1e30
VMEM_LIMIT = 60 * 2**20
SCALE = 1.0 / math.sqrt(HEAD_SIZE)
EXP2_SCALE = SCALE * math.log2(math.e)
F32 = jnp.float32
BF16 = jnp.bfloat16


def iota(shape, dim):
    return lax.broadcasted_iota(jnp.int32, shape, dim)


def dot(a, b):
    return jnp.dot(a, b, preferred_element_type=F32)


def ranks_within(member):
    earlier = (iota((TOK, TOK), 0) < iota((TOK, TOK), 1)).astype(F32).astype(BF16)
    counts = dot(member.astype(F32).astype(BF16), earlier)
    return jnp.where(member, counts, -1.0)


def pack_kernel(place_ref, rows_ref, out_ref):
    owner = place_ref[...] >> 8
    rank = ranks_within(owner == iota((SHARDS, TOK), 0))
    slot = iota((SLOTS, TOK), 0).astype(F32)
    picks = jnp.concatenate(
        [(rank[s : s + 1, :] == slot).astype(F32) for s in range(SHARDS)], axis=0
    ).astype(BF16)
    for first in range(0, rows_ref.shape[1], 256):
        cols = pl.ds(first, 256)
        out_ref[:, cols] = dot(picks, rows_ref[:, cols]).astype(BF16)


def stage_kernel(place_ref, kv_ref, out_ref, arrived):
    cols = pl.ds(pl.multiple_of((lax.axis_index("tp") // 2) * HEAD_SIZE, HEAD_SIZE), HEAD_SIZE)
    copies = [
        pltpu.make_async_copy(
            kv_ref.at[i, :, cols],
            out_ref.at[pl.ds(0, TOK), pl.ds(i * HEAD_SIZE, HEAD_SIZE)],
            arrived.at[i],
        )
        for i in range(2)
    ]
    for copy in copies:
        copy.start()
    place = place_ref[...]
    row = iota((META, TOK), 0)
    owner = jnp.broadcast_to((place >> 8).astype(F32), (META, TOK))
    within = jnp.broadcast_to((place & (TOK - 1)).astype(F32), (META, TOK))
    meta = jnp.where(row == 0, owner, jnp.where(row == 1, within, 0.0))
    out_ref[TOK:, :] = meta.astype(BF16)
    for copy in copies:
        copy.wait()


def fetch_all(sources, buffers, arrived):
    copies = [
        pltpu.make_async_copy(source, buffer, arrived.at[i])
        for i, (source, buffer) in enumerate(zip(sources, buffers))
    ]
    for copy in copies:
        copy.start()
    return copies


def permute_kernel(info_ref, *refs):
    count = 2 * RING + 2
    out_ref, unpack_ref, gr_ref, gt_ref, slots_s = refs[count : count + 5]
    grad_ref, own_ref = refs[count + 5 : count + 7]
    mine = refs[count + 7 : count + 7 + RING]
    theirs = refs[count + 7 + RING : count + 7 + 2 * RING]
    for copy in fetch_all(refs[:count], refs[count + 5 : -1], refs[-1]):
        copy.wait()
    shard = info_ref[0]
    core = info_ref[1]
    base = jnp.maximum(shard - BACK, 0)
    z, x = shard // 2, shard % 2
    sources = [(own_ref.at[j], shard ^ j) for j in range(2)]
    for refs_k, side in ((mine, core), (theirs, 1 - core)):
        for k in range(1, RING):
            far = (z + k * (2 * side - 1) + Z_CHIPS) % Z_CHIPS
            sources += [(refs_k[k - 1].at[j], 2 * far + (x ^ j)) for j in range(2)]
        far = (z + RING) % Z_CHIPS
        sources += [(refs_k[RING - 1], 2 * far + (x ^ side))]
    owners = jnp.concatenate([ref[TOK : TOK + 1, :].astype(F32) for ref, _ in sources], axis=0)
    within = jnp.concatenate([ref[TOK + 1 : TOK + 2, :].astype(F32) for ref, _ in sources], axis=0)
    rank = ranks_within(owners == shard.astype(F32))
    slot = iota((SLOTS, TOK), 0).astype(F32)
    lane = iota((SLOTS, TOK), 1).astype(F32)
    for i, (_, source) in enumerate(sources):
        hit = rank[i : i + 1, :] == slot
        landing = jnp.sum(jnp.where(hit, within[i : i + 1, :] + 1.0, 0.0), axis=1, keepdims=True)
        rows = pl.ds(pl.multiple_of(source * SLOTS, SLOTS), SLOTS)
        slots_s[rows, :] = (landing == lane + 1.0).astype(F32)
    unpack_ref[...] = slots_s[...].T.astype(BF16)
    for half in range(2):
        for h in range(LOCAL_HEADS):
            block = grad_ref[half * BLK : (half + 1) * BLK, h * HEAD_SIZE : (h + 1) * HEAD_SIZE]
            gr_ref[half, h * BLK : (h + 1) * BLK, :] = block
            gt_ref[half, :, h * BLK : (h + 1) * BLK] = block.astype(F32).T.astype(BF16)

    def one_shard(i, carry):
        rows = iota((TOK, TOK), 0).astype(F32)
        goal = jnp.where(owners == (base + i).astype(F32), within, -1.0)
        total = jnp.zeros((TOK, 2 * HEAD_SIZE), F32)
        for n, (ref, _) in enumerate(sources):
            picks = (goal[n : n + 1, :] == rows).astype(F32).astype(BF16)
            total = total + dot(picks, ref[:TOK, :])
        out_ref[pl.ds(pl.multiple_of(i * TOK, TOK), TOK), :] = total.astype(BF16)
        return carry

    lax.fori_loop(0, shard - base + 1, one_shard, 0)


def visible_blocks(qb, seg_ref, allow_ref, on_block):
    q_first = seg_ref[qb * BLK]

    def scan(kb, count):
        seen = jnp.logical_and(seg_ref[kb * BLK + BLK - 1] >= q_first, allow_ref[qb, kb] != 0)

        @pl.when(seen)
        def _():
            on_block(kb, count)

        return count + seen.astype(jnp.int32)

    count = lax.fori_loop(jnp.maximum(qb - BLOCKS_BACK, 0), qb + 1, scan, 0)
    wide = (count + 1) // WIDE
    narrow = (count + WIDE - 1) // WIDE - wide
    return count, wide, narrow


def parity_block(kb):
    shard = kb // 2
    return ((shard % 2) * Z_CHIPS + shard // 2) * 2 + kb % 2


def block_rows(n, blocks=1):
    return pl.ds(pl.multiple_of(n * BLK, BLK), blocks * BLK)


def attention_kernel(
    info_ref,
    seg_ref,
    allow_ref,
    segv_ref,
    unpack_in,
    recv_in,
    gr_in,
    gt_in,
    kv_in,
    keep_ref,
    send_ref,
    sg_ref,
    qr_s,
    qt_s,
    k_s,
    v_s,
    bias_s,
    e_s,
    dp_s,
    top_s,
    acc_s,
    sg_s,
    list_s,
    sent,
    kv_ref,
    unpack_ref,
    recv_ref,
    gr_ref,
    gt_ref,
    arrived,
):
    shard = info_ref[0]
    core = info_ref[1]
    base = jnp.maximum(shard - BACK, 0)
    copies = fetch_all(
        (kv_in, unpack_in, recv_in, gr_in, gt_in),
        (kv_ref, unpack_ref, recv_ref, gr_ref, gt_ref),
        arrived,
    )
    acc_s[...] = jnp.zeros_like(acc_s)
    copies[0].wait()

    def query_block(half, carry):
        qb = shard * 2 + half
        q_seg = segv_ref[pl.ds(qb, 1), :]
        q_last = seg_ref[qb * BLK + BLK - 1]

        def on_block(kb, count):
            list_s[count] = parity_block(kb)
            src = block_rows(kb - 2 * base)
            dst = block_rows(count)
            k_s[dst, :] = kv_ref[src, :HEAD_SIZE]
            v_s[dst, :] = kv_ref[src, HEAD_SIZE:]
            whole = jnp.logical_and(kb < qb, seg_ref[kb * BLK] == q_last)

            @pl.when(whole)
            def _():
                bias_s[dst, :] = jnp.zeros((BLK, BLK), F32)

            @pl.when(jnp.logical_not(whole))
            def _():
                k_seg = jnp.broadcast_to(segv_ref[pl.ds(kb, 1), :].astype(F32), (BLK, BLK)).T
                k_pos = kb * BLK + iota((BLK, BLK), 0)
                q_pos = qb * BLK + iota((BLK, BLK), 1)
                ok = (k_seg == q_seg.astype(F32)) & (k_pos <= q_pos)
                bias_s[dst, :] = jnp.where(ok, 0.0, NEG_FILL)

        count, wide, narrow = visible_blocks(qb, seg_ref, allow_ref, on_block)

        def fill(n, c):
            list_s[n] = 2 * SHARDS
            dst = block_rows(n)
            k_s[dst, :] = jnp.zeros((BLK, HEAD_SIZE), BF16)
            v_s[dst, :] = jnp.zeros((BLK, HEAD_SIZE), BF16)
            bias_s[dst, :] = jnp.full((BLK, BLK), NEG_FILL, F32)
            return c

        lax.fori_loop(count, wide * WIDE + narrow * NARROW, fill, 0)

        @pl.when(half == 0)
        def _():
            for copy in copies[1:]:
                copy.wait()

        picks = unpack_ref[block_rows(half), :]
        for pair in range(LOCAL_HEADS // 2):
            q_two = dot(picks, recv_ref[:, pair * 256 : (pair + 1) * 256])
            for i in range(2):
                mine = slice((2 * pair + i) * BLK, (2 * pair + i + 1) * BLK)
                q_one = q_two[:, i * HEAD_SIZE : (i + 1) * HEAD_SIZE]
                qr_s[mine, :] = q_one.astype(BF16)
                qt_s[:, mine] = q_one.T.astype(BF16)

        def first_pass(start, blocks, slot, state):
            top, total, weighed = state
            rows = block_rows(start, blocks)
            scores = dot(k_s[rows, :], qt_s[...])
            scores = scores + jnp.concatenate([bias_s[rows, :]] * LOCAL_HEADS, axis=1)
            new_top = jnp.maximum(top, jnp.max(scores, axis=0, keepdims=True))
            factor = jnp.exp2((top - new_top) * EXP2_SCALE)
            e = jnp.exp2((scores - new_top) * EXP2_SCALE)
            dp = dot(v_s[rows, :], gt_ref[half])
            e_s[rows, :] = e
            dp_s[rows, :] = dp
            top_s[slot] = new_top
            total = total * factor + jnp.sum(e.reshape(-1, 8, LANES), axis=0)
            weighed = weighed * factor + jnp.sum((e * dp).reshape(-1, 8, LANES), axis=0)
            return (new_top, total, weighed)

        state = (
            jnp.full((1, LANES), NEG_FILL, F32),
            jnp.zeros((8, LANES), F32),
            jnp.zeros((8, LANES), F32),
        )
        state = lax.fori_loop(
            0, wide, lambda n, st: first_pass(n * WIDE, WIDE, n, st), state
        )
        top, total, weighed = lax.fori_loop(
            0, narrow, lambda n, st: first_pass(wide * WIDE, NARROW, wide, st), state
        )
        inverse = 1.0 / jnp.sum(total, axis=0, keepdims=True)
        out_dot = jnp.sum(weighed, axis=0, keepdims=True) * inverse

        def copy_out(start, blocks, buffer):
            return pltpu.make_async_copy(
                sg_s.at[buffer, pl.ds(0, blocks * BLK), :],
                sg_ref.at[half, block_rows(start, blocks), :],
                sent.at[buffer],
            )

        def second_pass(start, blocks, slot, buffer):
            rows = block_rows(start, blocks)
            factor = jnp.exp2((top_s[slot] - top) * EXP2_SCALE) * inverse
            weights = e_s[rows, :] * factor
            score_grad = (weights * (dp_s[rows, :] - out_dot)).astype(BF16)
            sg_s[buffer, : blocks * BLK, :] = score_grad
            copy_out(start, blocks, buffer).start()
            value_terms = dot(weights.astype(BF16), gr_ref[half])
            key_terms = dot(score_grad, qr_s[...])
            for n in range(blocks):
                dst = block_rows(list_s[start + n])
                acc_s[0, dst, :] += key_terms[n * BLK : (n + 1) * BLK, :]
                acc_s[1, dst, :] += value_terms[n * BLK : (n + 1) * BLK, :]

        def wide_step(n, c):
            @pl.when(n >= 2)
            def _():
                copy_out((n - 2) * WIDE, WIDE, n % 2).wait()

            second_pass(n * WIDE, WIDE, n, n % 2)
            return c

        lax.fori_loop(0, wide, wide_step, 0)

        @pl.when(narrow > 0)
        def _():
            second_pass(wide * WIDE, NARROW, wide, 2)
            copy_out(wide * WIDE, NARROW, 2).wait()

        for late in (1, 2):

            @pl.when(wide >= late)
            def _():
                copy_out((wide - late) * WIDE, WIDE, (wide - late) % 2).wait()

        return carry

    lax.fori_loop(0, 2, query_block, 0)
    rows = slice(0, SHARDS * TOK)

    @pl.when(core == 0)
    def _():
        keep_ref[...] = (acc_s[0, rows, :] * SCALE).astype(BF16)
        send_ref[...] = acc_s[1, rows, :].astype(BF16)

    @pl.when(core == 1)
    def _():
        keep_ref[...] = acc_s[1, rows, :].astype(BF16)
        send_ref[...] = (acc_s[0, rows, :] * SCALE).astype(BF16)


def query_grad_kernel(
    info_ref, seg_ref, allow_ref, kv_in, sg_ref, dq_ref, kt_s, dqt_s, sg_s, arrived, kv_ref, kv_sem
):
    shard = info_ref[0]
    base = jnp.maximum(shard - BACK, 0)
    copy = pltpu.make_async_copy(kv_in, kv_ref, kv_sem)
    copy.start()

    def fetch(half, step):
        rows = block_rows(step * NARROW, NARROW)
        return pltpu.make_async_copy(
            sg_ref.at[half, rows, :], sg_s.at[half, rows, :], arrived.at[half, step]
        )

    def steps_of(half):
        nothing = lambda kb, count: None
        count, wide, narrow = visible_blocks(shard * 2 + half, seg_ref, allow_ref, nothing)
        return wide * (WIDE // NARROW) + narrow

    def start_fetch(half, c):
        def one(step, c2):
            fetch(half, step).start()
            return c2

        return lax.fori_loop(0, steps_of(half), one, c)

    lax.fori_loop(0, 2, start_fetch, 0)
    copy.wait()

    def query_block(half, carry):
        def on_block(kb, count):
            lanes = block_rows(count % NARROW)
            k_blk = kv_ref[block_rows(kb - 2 * base), :HEAD_SIZE]
            kt_s[count // NARROW, :, lanes] = k_blk.astype(F32).T.astype(BF16)

        count, wide, narrow = visible_blocks(shard * 2 + half, seg_ref, allow_ref, on_block)
        steps = wide * (WIDE // NARROW) + narrow

        def fill(n, c):
            lanes = block_rows(n % NARROW)
            kt_s[n // NARROW, :, lanes] = jnp.zeros((HEAD_SIZE, BLK), BF16)
            return c

        lax.fori_loop(count, steps * NARROW, fill, 0)
        dqt_s[...] = jnp.zeros_like(dqt_s)

        def one_step(step, c):
            fetch(half, step).wait()
            dqt_s[...] += dot(kt_s[step], sg_s[half, block_rows(step * NARROW, NARROW), :])
            return c

        lax.fori_loop(0, steps, one_step, 0)
        for h in range(LOCAL_HEADS):
            block = dqt_s[:, h * BLK : (h + 1) * BLK] * SCALE
            dq_ref[block_rows(half), h * HEAD_SIZE : (h + 1) * HEAD_SIZE] = block.T.astype(BF16)
        return carry

    lax.fori_loop(0, 2, query_block, 0)


VMEM = pl.BlockSpec(memory_space=pltpu.VMEM)
SMEM = pl.BlockSpec(memory_space=pltpu.SMEM)
ANY = pl.BlockSpec(memory_space=pl.ANY)
HBM = pl.BlockSpec(memory_space=pltpu.HBM)


def call_permute(info, grad, own, mine, theirs):
    return pl.pallas_call(
        permute_kernel,
        in_specs=[SMEM] + [HBM] * (2 * RING + 2),
        out_specs=[VMEM] * 4,
        out_shape=[
            jax.ShapeDtypeStruct((WINDOW * TOK, 2 * HEAD_SIZE), BF16),
            jax.ShapeDtypeStruct((TOK, SHARDS * SLOTS), BF16),
            jax.ShapeDtypeStruct((2, LANES, HEAD_SIZE), BF16),
            jax.ShapeDtypeStruct((2, HEAD_SIZE, LANES), BF16),
        ],
        scratch_shapes=[pltpu.VMEM((SHARDS * SLOTS, TOK), F32)]
        + [pltpu.VMEM(x.shape, x.dtype) for x in (grad, own, *mine, *theirs)]
        + [pltpu.SemaphoreType.DMA((2 * RING + 2,))],
        compiler_params=pltpu.CompilerParams(vmem_limit_bytes=VMEM_LIMIT),
        name="permute",
    )(info, grad, own, *mine, *theirs)


def call_attention(info, segments, allow, unpack, q_recv, gr, gt, kv_window):
    return pl.pallas_call(
        attention_kernel,
        in_specs=[SMEM, SMEM, SMEM, VMEM] + [HBM] * 5,
        out_specs=[VMEM, VMEM, HBM],
        out_shape=[
            jax.ShapeDtypeStruct((SHARDS * TOK, HEAD_SIZE), BF16),
            jax.ShapeDtypeStruct((SHARDS * TOK, HEAD_SIZE), BF16),
            jax.ShapeDtypeStruct((2, MOST_BLOCKS * BLK, LANES), BF16),
        ],
        scratch_shapes=[
            pltpu.VMEM((LANES, HEAD_SIZE), BF16),
            pltpu.VMEM((HEAD_SIZE, LANES), BF16),
            pltpu.VMEM((MOST_BLOCKS * BLK, HEAD_SIZE), BF16),
            pltpu.VMEM((MOST_BLOCKS * BLK, HEAD_SIZE), BF16),
            pltpu.VMEM((MOST_BLOCKS * BLK, BLK), F32),
            pltpu.VMEM((MOST_BLOCKS * BLK, LANES), F32),
            pltpu.VMEM((MOST_BLOCKS * BLK, LANES), F32),
            pltpu.VMEM((MOST_BLOCKS // WIDE + 1, 1, LANES), F32),
            pltpu.VMEM((2, SHARDS * TOK + BLK, HEAD_SIZE), F32),
            pltpu.VMEM((3, WIDE * BLK, LANES), BF16),
            pltpu.SMEM((MOST_BLOCKS,), jnp.int32),
            pltpu.SemaphoreType.DMA((3,)),
        ]
        + [pltpu.VMEM(x.shape, x.dtype) for x in (kv_window, unpack, q_recv, gr, gt)]
        + [pltpu.SemaphoreType.DMA((5,))],
        compiler_params=pltpu.CompilerParams(vmem_limit_bytes=VMEM_LIMIT),
        name="attention",
    )(info, segments, allow, segments.reshape(-1, BLK), unpack, q_recv, gr, gt, kv_window)


def call_query_grad(info, segments, allow, kv_window, score_grad):
    return pl.pallas_call(
        query_grad_kernel,
        in_specs=[SMEM, SMEM, SMEM, HBM, HBM],
        out_specs=VMEM,
        out_shape=jax.ShapeDtypeStruct((TOK, LOCAL_HEADS * HEAD_SIZE), BF16),
        scratch_shapes=[
            pltpu.VMEM((MOST_BLOCKS // NARROW, HEAD_SIZE, NARROW * BLK), BF16),
            pltpu.VMEM((HEAD_SIZE, LANES), F32),
            pltpu.VMEM((2, MOST_BLOCKS * BLK, LANES), BF16),
            pltpu.SemaphoreType.DMA((2, MOST_BLOCKS // NARROW)),
            pltpu.VMEM(kv_window.shape, BF16),
            pltpu.SemaphoreType.DMA(()),
        ],
        compiler_params=pltpu.CompilerParams(vmem_limit_bytes=VMEM_LIMIT),
        cost_estimate=pl.CostEstimate(
            flops=2 * TOK * 2048 * LANES, bytes_accessed=12 * 2**20, transcendentals=0
        ),
        name="query_grad",
    )(info, segments, allow, kv_window, score_grad)


def on_device(queries, keys_values, out_grad, place, segments, allow):
    tp_index = lax.axis_index("tp")
    ctx_index = lax.axis_index(("z", "x"))
    tp_size = lax.axis_size("tp")
    width = LOCAL_HEADS * HEAD_SIZE
    info = jnp.stack([ctx_index, tp_index % 2]).astype(jnp.int32)
    staged = pl.pallas_call(
        stage_kernel,
        in_specs=[VMEM, pl.BlockSpec(memory_space=pl.ANY)],
        out_specs=VMEM,
        out_shape=jax.ShapeDtypeStruct((TOK + META, 2 * HEAD_SIZE), BF16),
        scratch_shapes=[pltpu.SemaphoreType.DMA((2,))],
        name="stage",
    )(place.reshape(1, TOK), keys_values)
    beside = lax.ppermute(staged, "x", [(0, 1), (1, 0)])
    own = jnp.stack([staged, beside])
    g_send = out_grad.reshape(-1, tp_size, width).transpose(1, 0, 2)
    own, g_send = lax.optimization_barrier((own, g_send))

    def around(hops):
        pairs = []
        for k in range(SHARDS * tp_size):
            ctx, tp = k // tp_size, k % tp_size
            far = (ctx + (2 * hops if tp % 2 == 0 else -2 * hops)) % SHARDS
            pairs.append((k, far * tp_size + tp))
        return pairs

    swap = [(k, k ^ 1) for k in range(tp_size)]
    first = lax.ppermute(own, ("z", "x", "tp"), around(1))
    second = lax.ppermute(first, ("z", "x", "tp"), around(1))
    third = lax.ppermute(second, ("z", "x", "tp"), around(1))
    half = lax.dynamic_index_in_dim(second, tp_index % 2, 0, keepdims=False)
    fourth = lax.ppermute(half, ("z", "x", "tp"), around(2))
    mine = [first, second, third, fourth]
    g_local = lax.all_to_all(g_send, "tp", split_axis=0, concat_axis=0, tiled=True)
    g_local = g_local.reshape(TOK, width)
    q_send = pl.pallas_call(
        pack_kernel,
        in_specs=[VMEM, VMEM],
        out_specs=VMEM,
        out_shape=jax.ShapeDtypeStruct((SHARDS * SLOTS, width), BF16),
        name="pack",
    )(place.reshape(1, TOK), queries)
    q_send, *mine = lax.optimization_barrier((q_send, *mine))
    theirs = [lax.ppermute(piece, "tp", swap) for piece in mine]
    q_recv = lax.all_to_all(q_send, ("z", "x"), split_axis=0, concat_axis=0, tiled=True)
    kv_window, unpack, gr, gt = call_permute(info, g_local, own, mine, theirs)
    keep, send, score_grad = call_attention(
        info, segments, allow, unpack, q_recv, gr, gt, kv_window
    )
    recv = lax.ppermute(send, "tp", swap)
    halves = (2, Z_CHIPS, TOK, HEAD_SIZE)
    x_index = lax.axis_index("x")

    def summed(parity):
        terms = [
            lax.dynamic_index_in_dim(term.reshape(halves), parity, 0, keepdims=False)
            for term in (keep, recv)
        ]
        return (terms[0].astype(F32) + terms[1].astype(F32)).astype(BF16)

    z_first = jnp.clip(ctx_index // 2 - Z_BACK, 0, Z_CHIPS - Z_SPAN)
    to_send = lax.dynamic_slice_in_dim(summed(1 - x_index), z_first, Z_SPAN, 0)
    to_send, score_grad = lax.optimization_barrier((to_send, score_grad))
    beside_part = lax.ppermute(to_send, "x", [(0, 1), (1, 0)])
    spare = Z_CHIPS - Z_SPAN
    wide = jnp.pad(beside_part, ((spare, spare), (0, 0), (0, 0)))
    placed = lax.dynamic_slice_in_dim(wide, spare - z_first, Z_CHIPS, 0)
    part = (summed(x_index).astype(F32) + placed.astype(F32)).astype(BF16)
    parts = lax.all_to_all(part, "z", split_axis=0, concat_axis=0, tiled=True)
    grad_q = call_query_grad(info, segments, allow, kv_window, score_grad)
    owned = jnp.sum(parts.astype(F32), axis=0).astype(BF16)
    owned, grad_q = lax.optimization_barrier((owned, grad_q))
    heads = lax.all_to_all(
        owned.reshape(tp_size, TOK // tp_size, HEAD_SIZE),
        "tp",
        split_axis=0,
        concat_axis=0,
        tiled=True,
    )
    key_value_gradient = (
        heads.reshape(KEY_VALUE_HEADS, 2, TOK // tp_size, HEAD_SIZE)
        .transpose(1, 2, 0, 3)
        .reshape(2, TOK // tp_size, KEY_VALUE_HEADS * HEAD_SIZE)
    )
    return (grad_q, key_value_gradient)


def solution(mesh):
    tp_size = mesh.shape["tp"]
    split = Mesh(mesh.devices.reshape(Z_CHIPS, 2, tp_size), ("z", "x", "tp"))
    ctx = ("z", "x")
    in_specs = (P(ctx, "tp"), P(None, ctx, None), P((*ctx, "tp"), None), P(ctx), P(), P())
    out_specs = (P(ctx, "tp"), P(None, (*ctx, "tp"), None))
    return jax.shard_map(
        on_device, mesh=split, in_specs=in_specs, out_specs=out_specs, check_vma=False
    )
```

```python
import functools
import math

import jax
import jax.numpy as jnp
from jax import lax
from jax.experimental import pallas as pl
from jax.experimental.pallas import tpu as pltpu
from jax.sharding import Mesh
from jax.sharding import PartitionSpec as P

QUERY_HEAD_COUNT = 128
KEY_VALUE_HEADS = 8
HEAD_SIZE = 128
BLK = 128
TOK = 256
SHARDS = 16
SLOTS = 32
META = 16
Z_CHIPS = SHARDS // 2
RING = Z_CHIPS // 2
DOC_MOST = 2304
BACK = -(-DOC_MOST // TOK)
WINDOW = BACK + 1
BLOCKS_BACK = -(-DOC_MOST // BLK)
WIDE = 4
NARROW = 2
MOST_BLOCKS = WIDE * -(-(BLOCKS_BACK + 1) // WIDE)
LOCAL_HEADS = 8
LANES = LOCAL_HEADS * BLK
NEG_FILL = -1e30
VMEM_LIMIT = 60 * 2**20
SCALE = 1.0 / math.sqrt(HEAD_SIZE)
EXP2_SCALE = SCALE * math.log2(math.e)
F32 = jnp.float32
BF16 = jnp.bfloat16


def iota(shape, dim):
    return lax.broadcasted_iota(jnp.int32, shape, dim)


def dot(a, b):
    return jnp.dot(a, b, preferred_element_type=F32)


def ranks_within(member):
    earlier = (iota((TOK, TOK), 0) < iota((TOK, TOK), 1)).astype(F32).astype(BF16)
    counts = dot(member.astype(F32).astype(BF16), earlier)
    return jnp.where(member, counts, -1.0)


def pack_kernel(place_ref, rows_ref, out_ref):
    owner = place_ref[...] >> 8
    rank = ranks_within(owner == iota((SHARDS, TOK), 0))
    slot = iota((SLOTS, TOK), 0).astype(F32)
    picks = jnp.concatenate(
        [(rank[s : s + 1, :] == slot).astype(F32) for s in range(SHARDS)], axis=0
    ).astype(BF16)
    for first in range(0, rows_ref.shape[1], 256):
        cols = pl.ds(first, 256)
        out_ref[:, cols] = dot(picks, rows_ref[:, cols]).astype(BF16)


def stage_kernel(place_ref, kv_ref, out_ref, arrived):
    cols = pl.ds(pl.multiple_of((lax.axis_index("tp") // 2) * HEAD_SIZE, HEAD_SIZE), HEAD_SIZE)
    copies = [
        pltpu.make_async_copy(
            kv_ref.at[i, :, cols],
            out_ref.at[pl.ds(0, TOK), pl.ds(i * HEAD_SIZE, HEAD_SIZE)],
            arrived.at[i],
        )
        for i in range(2)
    ]
    for copy in copies:
        copy.start()
    place = place_ref[...]
    row = iota((META, TOK), 0)
    owner = jnp.broadcast_to((place >> 8).astype(F32), (META, TOK))
    within = jnp.broadcast_to((place & (TOK - 1)).astype(F32), (META, TOK))
    meta = jnp.where(row == 0, owner, jnp.where(row == 1, within, 0.0))
    out_ref[TOK:, :] = meta.astype(BF16)
    for copy in copies:
        copy.wait()


def fetch_all(sources, buffers, arrived):
    copies = [
        pltpu.make_async_copy(source, buffer, arrived.at[i])
        for i, (source, buffer) in enumerate(zip(sources, buffers))
    ]
    for copy in copies:
        copy.start()
    return copies


def permute_kernel(info_ref, *refs):
    count = 2 * RING + 2
    out_ref, unpack_ref, gr_ref, gt_ref, slots_s = refs[count : count + 5]
    grad_ref, own_ref = refs[count + 5 : count + 7]
    mine = refs[count + 7 : count + 7 + RING]
    theirs = refs[count + 7 + RING : count + 7 + 2 * RING]
    for copy in fetch_all(refs[:count], refs[count + 5 : -1], refs[-1]):
        copy.wait()
    shard = info_ref[0]
    core = info_ref[1]
    base = jnp.maximum(shard - BACK, 0)
    z, x = shard // 2, shard % 2
    sources = [(own_ref.at[j], shard ^ j) for j in range(2)]
    for refs_k, side in ((mine, core), (theirs, 1 - core)):
        for k in range(1, RING):
            far = (z + k * (2 * side - 1) + Z_CHIPS) % Z_CHIPS
            sources += [(refs_k[k - 1].at[j], 2 * far + (x ^ j)) for j in range(2)]
        far = (z + RING) % Z_CHIPS
        sources += [(refs_k[RING - 1], 2 * far + (x ^ side))]
    owners = jnp.concatenate([ref[TOK : TOK + 1, :].astype(F32) for ref, _ in sources], axis=0)
    within = jnp.concatenate([ref[TOK + 1 : TOK + 2, :].astype(F32) for ref, _ in sources], axis=0)
    rank = ranks_within(owners == shard.astype(F32))
    slot = iota((SLOTS, TOK), 0).astype(F32)
    lane = iota((SLOTS, TOK), 1).astype(F32)
    for i, (_, source) in enumerate(sources):
        hit = rank[i : i + 1, :] == slot
        landing = jnp.sum(jnp.where(hit, within[i : i + 1, :] + 1.0, 0.0), axis=1, keepdims=True)
        rows = pl.ds(pl.multiple_of(source * SLOTS, SLOTS), SLOTS)
        slots_s[rows, :] = (landing == lane + 1.0).astype(F32)
    unpack_ref[...] = slots_s[...].T.astype(BF16)
    for half in range(2):
        for h in range(LOCAL_HEADS):
            block = grad_ref[half * BLK : (half + 1) * BLK, h * HEAD_SIZE : (h + 1) * HEAD_SIZE]
            gr_ref[half, h * BLK : (h + 1) * BLK, :] = block
            gt_ref[half, :, h * BLK : (h + 1) * BLK] = block.astype(F32).T.astype(BF16)

    def one_shard(i, carry):
        rows = iota((TOK, TOK), 0).astype(F32)
        goal = jnp.where(owners == (base + i).astype(F32), within, -1.0)
        total = jnp.zeros((TOK, 2 * HEAD_SIZE), F32)
        for n, (ref, _) in enumerate(sources):
            picks = (goal[n : n + 1, :] == rows).astype(F32).astype(BF16)
            total = total + dot(picks, ref[:TOK, :])
        out_ref[pl.ds(pl.multiple_of(i * TOK, TOK), TOK), :] = total.astype(BF16)
        return carry

    lax.fori_loop(0, shard - base + 1, one_shard, 0)


def visible_blocks(qb, seg_ref, allow_ref, on_block):
    q_first = seg_ref[qb * BLK]

    def scan(kb, count):
        seen = jnp.logical_and(seg_ref[kb * BLK + BLK - 1] >= q_first, allow_ref[qb, kb] != 0)

        @pl.when(seen)
        def _():
            on_block(kb, count)

        return count + seen.astype(jnp.int32)

    count = lax.fori_loop(jnp.maximum(qb - BLOCKS_BACK, 0), qb + 1, scan, 0)
    wide = (count + 1) // WIDE
    narrow = (count + WIDE - 1) // WIDE - wide
    return count, wide, narrow


def block_rows(n, blocks=1):
    return pl.ds(pl.multiple_of(n * BLK, BLK), blocks * BLK)


def attention_kernel(
    info_ref,
    seg_ref,
    allow_ref,
    segv_ref,
    unpack_in,
    recv_in,
    gr_in,
    gt_in,
    kv_in,
    keep_ref,
    send_ref,
    sg_ref,
    qr_s,
    qt_s,
    k_s,
    v_s,
    bias_s,
    e_s,
    dp_s,
    top_s,
    acc_s,
    sg_s,
    list_s,
    sent,
    kv_ref,
    unpack_ref,
    recv_ref,
    gr_ref,
    gt_ref,
    arrived,
):
    shard = info_ref[0]
    core = info_ref[1]
    base = jnp.maximum(shard - BACK, 0)
    copies = fetch_all(
        (kv_in, unpack_in, recv_in, gr_in, gt_in),
        (kv_ref, unpack_ref, recv_ref, gr_ref, gt_ref),
        arrived,
    )
    acc_s[...] = jnp.zeros_like(acc_s)
    copies[0].wait()

    def query_block(half, carry):
        qb = shard * 2 + half
        q_seg = segv_ref[pl.ds(qb, 1), :]
        q_last = seg_ref[qb * BLK + BLK - 1]

        def on_block(kb, count):
            list_s[count] = kb
            src = block_rows(kb - 2 * base)
            dst = block_rows(count)
            k_s[dst, :] = kv_ref[src, :HEAD_SIZE]
            v_s[dst, :] = kv_ref[src, HEAD_SIZE:]
            whole = jnp.logical_and(kb < qb, seg_ref[kb * BLK] == q_last)

            @pl.when(whole)
            def _():
                bias_s[dst, :] = jnp.zeros((BLK, BLK), F32)

            @pl.when(jnp.logical_not(whole))
            def _():
                k_seg = jnp.broadcast_to(segv_ref[pl.ds(kb, 1), :].astype(F32), (BLK, BLK)).T
                k_pos = kb * BLK + iota((BLK, BLK), 0)
                q_pos = qb * BLK + iota((BLK, BLK), 1)
                ok = (k_seg == q_seg.astype(F32)) & (k_pos <= q_pos)
                bias_s[dst, :] = jnp.where(ok, 0.0, NEG_FILL)

        count, wide, narrow = visible_blocks(qb, seg_ref, allow_ref, on_block)

        def fill(n, c):
            list_s[n] = 2 * SHARDS
            dst = block_rows(n)
            k_s[dst, :] = jnp.zeros((BLK, HEAD_SIZE), BF16)
            v_s[dst, :] = jnp.zeros((BLK, HEAD_SIZE), BF16)
            bias_s[dst, :] = jnp.full((BLK, BLK), NEG_FILL, F32)
            return c

        lax.fori_loop(count, wide * WIDE + narrow * NARROW, fill, 0)

        @pl.when(half == 0)
        def _():
            for copy in copies[1:]:
                copy.wait()

        picks = unpack_ref[block_rows(half), :]
        for pair in range(LOCAL_HEADS // 2):
            q_two = dot(picks, recv_ref[:, pair * 256 : (pair + 1) * 256])
            for i in range(2):
                mine = slice((2 * pair + i) * BLK, (2 * pair + i + 1) * BLK)
                q_one = q_two[:, i * HEAD_SIZE : (i + 1) * HEAD_SIZE]
                qr_s[mine, :] = q_one.astype(BF16)
                qt_s[:, mine] = q_one.T.astype(BF16)

        def first_pass(start, blocks, slot, state):
            top, total, weighed = state
            rows = block_rows(start, blocks)
            scores = dot(k_s[rows, :], qt_s[...])
            scores = scores + jnp.concatenate([bias_s[rows, :]] * LOCAL_HEADS, axis=1)
            new_top = jnp.maximum(top, jnp.max(scores, axis=0, keepdims=True))
            factor = jnp.exp2((top - new_top) * EXP2_SCALE)
            e = jnp.exp2((scores - new_top) * EXP2_SCALE)
            dp = dot(v_s[rows, :], gt_ref[half])
            e_s[rows, :] = e
            dp_s[rows, :] = dp
            top_s[slot] = new_top
            total = total * factor + jnp.sum(e.reshape(-1, 8, LANES), axis=0)
            weighed = weighed * factor + jnp.sum((e * dp).reshape(-1, 8, LANES), axis=0)
            return (new_top, total, weighed)

        state = (
            jnp.full((1, LANES), NEG_FILL, F32),
            jnp.zeros((8, LANES), F32),
            jnp.zeros((8, LANES), F32),
        )
        state = lax.fori_loop(
            0, wide, lambda n, st: first_pass(n * WIDE, WIDE, n, st), state
        )
        top, total, weighed = lax.fori_loop(
            0, narrow, lambda n, st: first_pass(wide * WIDE, NARROW, wide, st), state
        )
        inverse = 1.0 / jnp.sum(total, axis=0, keepdims=True)
        out_dot = jnp.sum(weighed, axis=0, keepdims=True) * inverse

        def copy_out(start, blocks, buffer):
            return pltpu.make_async_copy(
                sg_s.at[buffer, pl.ds(0, blocks * BLK), :],
                sg_ref.at[half, block_rows(start, blocks), :],
                sent.at[buffer],
            )

        def second_pass(start, blocks, slot, buffer):
            rows = block_rows(start, blocks)
            factor = jnp.exp2((top_s[slot] - top) * EXP2_SCALE) * inverse
            weights = e_s[rows, :] * factor
            score_grad = (weights * (dp_s[rows, :] - out_dot)).astype(BF16)
            sg_s[buffer, : blocks * BLK, :] = score_grad
            copy_out(start, blocks, buffer).start()
            value_terms = dot(weights.astype(BF16), gr_ref[half])
            key_terms = dot(score_grad, qr_s[...])
            for n in range(blocks):
                dst = block_rows(list_s[start + n])
                acc_s[0, dst, :] += key_terms[n * BLK : (n + 1) * BLK, :]
                acc_s[1, dst, :] += value_terms[n * BLK : (n + 1) * BLK, :]

        def wide_step(n, c):
            @pl.when(n >= 2)
            def _():
                copy_out((n - 2) * WIDE, WIDE, n % 2).wait()

            second_pass(n * WIDE, WIDE, n, n % 2)
            return c

        lax.fori_loop(0, wide, wide_step, 0)

        @pl.when(narrow > 0)
        def _():
            second_pass(wide * WIDE, NARROW, wide, 2)
            copy_out(wide * WIDE, NARROW, 2).wait()

        for late in (1, 2):

            @pl.when(wide >= late)
            def _():
                copy_out((wide - late) * WIDE, WIDE, (wide - late) % 2).wait()

        return carry

    lax.fori_loop(0, 2, query_block, 0)
    rows = slice(0, SHARDS * TOK)

    @pl.when(core == 0)
    def _():
        keep_ref[...] = (acc_s[0, rows, :] * SCALE).astype(BF16)
        send_ref[...] = acc_s[1, rows, :].astype(BF16)

    @pl.when(core == 1)
    def _():
        keep_ref[...] = acc_s[1, rows, :].astype(BF16)
        send_ref[...] = (acc_s[0, rows, :] * SCALE).astype(BF16)


def query_grad_kernel(
    info_ref, seg_ref, allow_ref, kv_in, sg_ref, dq_ref, kt_s, dqt_s, sg_s, arrived, kv_ref, kv_sem
):
    shard = info_ref[0]
    base = jnp.maximum(shard - BACK, 0)
    copy = pltpu.make_async_copy(kv_in, kv_ref, kv_sem)
    copy.start()

    def fetch(half, step):
        rows = block_rows(step * NARROW, NARROW)
        return pltpu.make_async_copy(
            sg_ref.at[half, rows, :], sg_s.at[half, rows, :], arrived.at[half, step]
        )

    def steps_of(half):
        nothing = lambda kb, count: None
        count, wide, narrow = visible_blocks(shard * 2 + half, seg_ref, allow_ref, nothing)
        return wide * (WIDE // NARROW) + narrow

    def start_fetch(half, c):
        def one(step, c2):
            fetch(half, step).start()
            return c2

        return lax.fori_loop(0, steps_of(half), one, c)

    lax.fori_loop(0, 2, start_fetch, 0)
    copy.wait()

    def query_block(half, carry):
        def on_block(kb, count):
            lanes = block_rows(count % NARROW)
            k_blk = kv_ref[block_rows(kb - 2 * base), :HEAD_SIZE]
            kt_s[count // NARROW, :, lanes] = k_blk.astype(F32).T.astype(BF16)

        count, wide, narrow = visible_blocks(shard * 2 + half, seg_ref, allow_ref, on_block)
        steps = wide * (WIDE // NARROW) + narrow

        def fill(n, c):
            lanes = block_rows(n % NARROW)
            kt_s[n // NARROW, :, lanes] = jnp.zeros((HEAD_SIZE, BLK), BF16)
            return c

        lax.fori_loop(count, steps * NARROW, fill, 0)
        dqt_s[...] = jnp.zeros_like(dqt_s)

        def one_step(step, c):
            fetch(half, step).wait()
            dqt_s[...] += dot(kt_s[step], sg_s[half, block_rows(step * NARROW, NARROW), :])
            return c

        lax.fori_loop(0, steps, one_step, 0)
        for h in range(LOCAL_HEADS):
            block = dqt_s[:, h * BLK : (h + 1) * BLK] * SCALE
            dq_ref[block_rows(half), h * HEAD_SIZE : (h + 1) * HEAD_SIZE] = block.T.astype(BF16)
        return carry

    lax.fori_loop(0, 2, query_block, 0)


VMEM = pl.BlockSpec(memory_space=pltpu.VMEM)
SMEM = pl.BlockSpec(memory_space=pltpu.SMEM)
ANY = pl.BlockSpec(memory_space=pl.ANY)
HBM = pl.BlockSpec(memory_space=pltpu.HBM)


def call_permute(info, grad, own, mine, theirs):
    return pl.pallas_call(
        permute_kernel,
        in_specs=[SMEM] + [HBM] * (2 * RING + 2),
        out_specs=[VMEM] * 4,
        out_shape=[
            jax.ShapeDtypeStruct((WINDOW * TOK, 2 * HEAD_SIZE), BF16),
            jax.ShapeDtypeStruct((TOK, SHARDS * SLOTS), BF16),
            jax.ShapeDtypeStruct((2, LANES, HEAD_SIZE), BF16),
            jax.ShapeDtypeStruct((2, HEAD_SIZE, LANES), BF16),
        ],
        scratch_shapes=[pltpu.VMEM((SHARDS * SLOTS, TOK), F32)]
        + [pltpu.VMEM(x.shape, x.dtype) for x in (grad, own, *mine, *theirs)]
        + [pltpu.SemaphoreType.DMA((2 * RING + 2,))],
        compiler_params=pltpu.CompilerParams(vmem_limit_bytes=VMEM_LIMIT),
        name="permute",
    )(info, grad, own, *mine, *theirs)


def call_attention(info, segments, allow, unpack, q_recv, gr, gt, kv_window):
    return pl.pallas_call(
        attention_kernel,
        in_specs=[SMEM, SMEM, SMEM, VMEM] + [HBM] * 5,
        out_specs=[VMEM, VMEM, HBM],
        out_shape=[
            jax.ShapeDtypeStruct((SHARDS * TOK, HEAD_SIZE), BF16),
            jax.ShapeDtypeStruct((SHARDS * TOK, HEAD_SIZE), BF16),
            jax.ShapeDtypeStruct((2, MOST_BLOCKS * BLK, LANES), BF16),
        ],
        scratch_shapes=[
            pltpu.VMEM((LANES, HEAD_SIZE), BF16),
            pltpu.VMEM((HEAD_SIZE, LANES), BF16),
            pltpu.VMEM((MOST_BLOCKS * BLK, HEAD_SIZE), BF16),
            pltpu.VMEM((MOST_BLOCKS * BLK, HEAD_SIZE), BF16),
            pltpu.VMEM((MOST_BLOCKS * BLK, BLK), F32),
            pltpu.VMEM((MOST_BLOCKS * BLK, LANES), F32),
            pltpu.VMEM((MOST_BLOCKS * BLK, LANES), F32),
            pltpu.VMEM((MOST_BLOCKS // WIDE + 1, 1, LANES), F32),
            pltpu.VMEM((2, SHARDS * TOK + BLK, HEAD_SIZE), F32),
            pltpu.VMEM((3, WIDE * BLK, LANES), BF16),
            pltpu.SMEM((MOST_BLOCKS,), jnp.int32),
            pltpu.SemaphoreType.DMA((3,)),
        ]
        + [pltpu.VMEM(x.shape, x.dtype) for x in (kv_window, unpack, q_recv, gr, gt)]
        + [pltpu.SemaphoreType.DMA((5,))],
        compiler_params=pltpu.CompilerParams(vmem_limit_bytes=VMEM_LIMIT),
        name="attention",
    )(info, segments, allow, segments.reshape(-1, BLK), unpack, q_recv, gr, gt, kv_window)


def call_query_grad(info, segments, allow, kv_window, score_grad):
    return pl.pallas_call(
        query_grad_kernel,
        in_specs=[SMEM, SMEM, SMEM, HBM, HBM],
        out_specs=VMEM,
        out_shape=jax.ShapeDtypeStruct((TOK, LOCAL_HEADS * HEAD_SIZE), BF16),
        scratch_shapes=[
            pltpu.VMEM((MOST_BLOCKS // NARROW, HEAD_SIZE, NARROW * BLK), BF16),
            pltpu.VMEM((HEAD_SIZE, LANES), F32),
            pltpu.VMEM((2, MOST_BLOCKS * BLK, LANES), BF16),
            pltpu.SemaphoreType.DMA((2, MOST_BLOCKS // NARROW)),
            pltpu.VMEM(kv_window.shape, BF16),
            pltpu.SemaphoreType.DMA(()),
        ],
        compiler_params=pltpu.CompilerParams(vmem_limit_bytes=VMEM_LIMIT),
        cost_estimate=pl.CostEstimate(
            flops=2 * TOK * 2048 * LANES, bytes_accessed=12 * 2**20, transcendentals=0
        ),
        name="query_grad",
    )(info, segments, allow, kv_window, score_grad)


def on_device(queries, keys_values, out_grad, place, segments, allow):
    tp_index = lax.axis_index("tp")
    ctx_index = lax.axis_index(("z", "x"))
    tp_size = lax.axis_size("tp")
    width = LOCAL_HEADS * HEAD_SIZE
    info = jnp.stack([ctx_index, tp_index % 2]).astype(jnp.int32)
    staged = pl.pallas_call(
        stage_kernel,
        in_specs=[VMEM, pl.BlockSpec(memory_space=pl.ANY)],
        out_specs=VMEM,
        out_shape=jax.ShapeDtypeStruct((TOK + META, 2 * HEAD_SIZE), BF16),
        scratch_shapes=[pltpu.SemaphoreType.DMA((2,))],
        name="stage",
    )(place.reshape(1, TOK), keys_values)
    beside = lax.ppermute(staged, "x", [(0, 1), (1, 0)])
    own = jnp.stack([staged, beside])
    g_send = out_grad.reshape(-1, tp_size, width).transpose(1, 0, 2)
    own, g_send = lax.optimization_barrier((own, g_send))

    def around(hops):
        pairs = []
        for k in range(SHARDS * tp_size):
            ctx, tp = k // tp_size, k % tp_size
            far = (ctx + (2 * hops if tp % 2 == 0 else -2 * hops)) % SHARDS
            pairs.append((k, far * tp_size + tp))
        return pairs

    swap = [(k, k ^ 1) for k in range(tp_size)]
    first = lax.ppermute(own, ("z", "x", "tp"), around(1))
    second = lax.ppermute(first, ("z", "x", "tp"), around(1))
    third = lax.ppermute(second, ("z", "x", "tp"), around(1))
    half = lax.dynamic_index_in_dim(second, tp_index % 2, 0, keepdims=False)
    fourth = lax.ppermute(half, ("z", "x", "tp"), around(2))
    mine = [first, second, third, fourth]
    g_local = lax.all_to_all(g_send, "tp", split_axis=0, concat_axis=0, tiled=True)
    g_local = g_local.reshape(TOK, width)
    q_send = pl.pallas_call(
        pack_kernel,
        in_specs=[VMEM, VMEM],
        out_specs=VMEM,
        out_shape=jax.ShapeDtypeStruct((SHARDS * SLOTS, width), BF16),
        name="pack",
    )(place.reshape(1, TOK), queries)
    q_send, *mine = lax.optimization_barrier((q_send, *mine))
    theirs = [lax.ppermute(piece, "tp", swap) for piece in mine]
    q_recv = lax.all_to_all(q_send, ("z", "x"), split_axis=0, concat_axis=0, tiled=True)
    kv_window, unpack, gr, gt = call_permute(info, g_local, own, mine, theirs)
    keep, send, score_grad = call_attention(
        info, segments, allow, unpack, q_recv, gr, gt, kv_window
    )
    recv = lax.ppermute(send, "tp", swap)
    part = (keep.astype(F32) + recv.astype(F32)).astype(BF16)
    part, score_grad = lax.optimization_barrier((part, score_grad))
    rows = TOK // tp_size
    parts = lax.all_to_all(
        part.reshape(SHARDS * tp_size, rows, HEAD_SIZE),
        ("z", "x", "tp"),
        split_axis=0,
        concat_axis=0,
        tiled=True,
    )
    grad_q = call_query_grad(info, segments, allow, kv_window, score_grad)
    parts, grad_q = lax.optimization_barrier((parts, grad_q))
    heads = jnp.sum(parts.reshape(SHARDS, tp_size, rows, HEAD_SIZE).astype(F32), axis=0)
    key_value_gradient = (
        heads.astype(BF16)
        .reshape(KEY_VALUE_HEADS, 2, rows, HEAD_SIZE)
        .transpose(1, 2, 0, 3)
        .reshape(2, rows, KEY_VALUE_HEADS * HEAD_SIZE)
    )
    return (grad_q, key_value_gradient)


def solution(mesh):
    tp_size = mesh.shape["tp"]
    split = Mesh(mesh.devices.reshape(Z_CHIPS, 2, tp_size), ("z", "x", "tp"))
    ctx = ("z", "x")
    in_specs = (P(ctx, "tp"), P(None, ctx, None), P((*ctx, "tp"), None), P(ctx), P(), P())
    out_specs = (P(ctx, "tp"), P(None, (*ctx, "tp"), None))
    return jax.shard_map(
        on_device, mesh=split, in_specs=in_specs, out_specs=out_specs, check_vma=False
    )
```

```python
import functools
import math

import jax
import jax.numpy as jnp
from jax import lax
from jax.experimental import pallas as pl
from jax.experimental.pallas import tpu as pltpu
from jax.sharding import Mesh
from jax.sharding import PartitionSpec as P

QUERY_HEAD_COUNT = 128
KEY_VALUE_HEADS = 8
HEAD_SIZE = 128
BLK = 128
TOK = 256
SHARDS = 16
SLOTS = 32
META = 16
Z_CHIPS = SHARDS // 2
RING = Z_CHIPS // 2
DOC_MOST = 2304
BACK = -(-DOC_MOST // TOK)
WINDOW = BACK + 1
BLOCKS_BACK = -(-DOC_MOST // BLK)
WIDE = 4
NARROW = 2
MOST_BLOCKS = WIDE * -(-(BLOCKS_BACK + 1) // WIDE)
LOCAL_HEADS = 8
LANES = LOCAL_HEADS * BLK
NEG_FILL = -1e30
VMEM_LIMIT = 60 * 2**20
SCALE = 1.0 / math.sqrt(HEAD_SIZE)
EXP2_SCALE = SCALE * math.log2(math.e)
F32 = jnp.float32
BF16 = jnp.bfloat16


def iota(shape, dim):
    return lax.broadcasted_iota(jnp.int32, shape, dim)


def dot(a, b):
    return jnp.dot(a, b, preferred_element_type=F32)


def ranks_within(member):
    earlier = (iota((TOK, TOK), 0) < iota((TOK, TOK), 1)).astype(F32).astype(BF16)
    counts = dot(member.astype(F32).astype(BF16), earlier)
    return jnp.where(member, counts, -1.0)


def pack_kernel(place_ref, rows_ref, out_ref):
    owner = place_ref[...] >> 8
    rank = ranks_within(owner == iota((SHARDS, TOK), 0))
    slot = iota((SLOTS, TOK), 0).astype(F32)
    picks = jnp.concatenate(
        [(rank[s : s + 1, :] == slot).astype(F32) for s in range(SHARDS)], axis=0
    ).astype(BF16)
    for first in range(0, rows_ref.shape[1], 256):
        cols = pl.ds(first, 256)
        out_ref[:, cols] = dot(picks, rows_ref[:, cols]).astype(BF16)


def stage_kernel(place_ref, kv_ref, out_ref, arrived):
    cols = pl.ds(pl.multiple_of((lax.axis_index("tp") // 2) * HEAD_SIZE, HEAD_SIZE), HEAD_SIZE)
    copies = [
        pltpu.make_async_copy(
            kv_ref.at[i, :, cols],
            out_ref.at[pl.ds(0, TOK), pl.ds(i * HEAD_SIZE, HEAD_SIZE)],
            arrived.at[i],
        )
        for i in range(2)
    ]
    for copy in copies:
        copy.start()
    place = place_ref[...]
    row = iota((META, TOK), 0)
    owner = jnp.broadcast_to((place >> 8).astype(F32), (META, TOK))
    within = jnp.broadcast_to((place & (TOK - 1)).astype(F32), (META, TOK))
    meta = jnp.where(row == 0, owner, jnp.where(row == 1, within, 0.0))
    out_ref[TOK:, :] = meta.astype(BF16)
    for copy in copies:
        copy.wait()


def fetch_all(sources, buffers, arrived):
    copies = [
        pltpu.make_async_copy(source, buffer, arrived.at[i])
        for i, (source, buffer) in enumerate(zip(sources, buffers))
    ]
    for copy in copies:
        copy.start()
    return copies


def permute_kernel(info_ref, *refs):
    count = 2 * RING + 2
    out_ref, unpack_ref, gr_ref, gt_ref, slots_s = refs[count : count + 5]
    grad_ref, own_ref = refs[count + 5 : count + 7]
    mine = refs[count + 7 : count + 7 + RING]
    theirs = refs[count + 7 + RING : count + 7 + 2 * RING]
    for copy in fetch_all(refs[:count], refs[count + 5 : -1], refs[-1]):
        copy.wait()
    shard = info_ref[0]
    core = info_ref[1]
    base = jnp.maximum(shard - BACK, 0)
    z, x = shard // 2, shard % 2
    sources = [(own_ref.at[j], shard ^ j) for j in range(2)]
    for refs_k, side in ((mine, core), (theirs, 1 - core)):
        for k in range(1, RING):
            far = (z + k * (2 * side - 1) + Z_CHIPS) % Z_CHIPS
            sources += [(refs_k[k - 1].at[j], 2 * far + (x ^ j)) for j in range(2)]
        far = (z + RING) % Z_CHIPS
        sources += [(refs_k[RING - 1], 2 * far + (x ^ side))]
    owners = jnp.concatenate([ref[TOK : TOK + 1, :].astype(F32) for ref, _ in sources], axis=0)
    within = jnp.concatenate([ref[TOK + 1 : TOK + 2, :].astype(F32) for ref, _ in sources], axis=0)
    rank = ranks_within(owners == shard.astype(F32))
    slot = iota((SLOTS, TOK), 0).astype(F32)
    lane = iota((SLOTS, TOK), 1).astype(F32)
    for i, (_, source) in enumerate(sources):
        hit = rank[i : i + 1, :] == slot
        landing = jnp.sum(jnp.where(hit, within[i : i + 1, :] + 1.0, 0.0), axis=1, keepdims=True)
        rows = pl.ds(pl.multiple_of(source * SLOTS, SLOTS), SLOTS)
        slots_s[rows, :] = (landing == lane + 1.0).astype(F32)
    unpack_ref[...] = slots_s[...].T.astype(BF16)
    for half in range(2):
        for h in range(LOCAL_HEADS):
            block = grad_ref[half * BLK : (half + 1) * BLK, h * HEAD_SIZE : (h + 1) * HEAD_SIZE]
            gr_ref[half, h * BLK : (h + 1) * BLK, :] = block
            gt_ref[half, :, h * BLK : (h + 1) * BLK] = block.astype(F32).T.astype(BF16)

    def one_shard(i, carry):
        rows = iota((TOK, TOK), 0).astype(F32)
        goal = jnp.where(owners == (base + i).astype(F32), within, -1.0)
        total = jnp.zeros((TOK, 2 * HEAD_SIZE), F32)
        for n, (ref, _) in enumerate(sources):
            picks = (goal[n : n + 1, :] == rows).astype(F32).astype(BF16)
            total = total + dot(picks, ref[:TOK, :])
        out_ref[pl.ds(pl.multiple_of(i * TOK, TOK), TOK), :] = total.astype(BF16)
        return carry

    lax.fori_loop(0, shard - base + 1, one_shard, 0)


def visible_blocks(qb, seg_ref, allow_ref, on_block):
    q_first = seg_ref[qb * BLK]

    def scan(kb, count):
        seen = jnp.logical_and(seg_ref[kb * BLK + BLK - 1] >= q_first, allow_ref[qb, kb] != 0)

        @pl.when(seen)
        def _():
            on_block(kb, count)

        return count + seen.astype(jnp.int32)

    count = lax.fori_loop(jnp.maximum(qb - BLOCKS_BACK, 0), qb + 1, scan, 0)
    wide = (count + 1) // WIDE
    narrow = (count + WIDE - 1) // WIDE - wide
    return count, wide, narrow


def block_rows(n, blocks=1):
    return pl.ds(pl.multiple_of(n * BLK, BLK), blocks * BLK)


def attention_kernel(
    info_ref,
    seg_ref,
    allow_ref,
    segv_ref,
    unpack_ref,
    recv_ref,
    gr_ref,
    gt_ref,
    kv_ref,
    keep_ref,
    send_ref,
    sg_ref,
    qr_s,
    qt_s,
    k_s,
    v_s,
    bias_s,
    e_s,
    dp_s,
    top_s,
    acc_s,
    sg_s,
    list_s,
    sent,
):
    shard = info_ref[0]
    core = info_ref[1]
    base = jnp.maximum(shard - BACK, 0)
    acc_s[...] = jnp.zeros_like(acc_s)

    def query_block(half, carry):
        qb = shard * 2 + half
        q_seg = segv_ref[pl.ds(qb, 1), :]
        q_last = seg_ref[qb * BLK + BLK - 1]
        picks = unpack_ref[block_rows(half), :]
        for pair in range(LOCAL_HEADS // 2):
            q_two = dot(picks, recv_ref[:, pair * 256 : (pair + 1) * 256])
            for i in range(2):
                mine = slice((2 * pair + i) * BLK, (2 * pair + i + 1) * BLK)
                q_one = q_two[:, i * HEAD_SIZE : (i + 1) * HEAD_SIZE]
                qr_s[mine, :] = q_one.astype(BF16)
                qt_s[:, mine] = q_one.T.astype(BF16)

        def on_block(kb, count):
            list_s[count] = kb
            src = block_rows(kb - 2 * base)
            dst = block_rows(count)
            k_s[dst, :] = kv_ref[src, :HEAD_SIZE]
            v_s[dst, :] = kv_ref[src, HEAD_SIZE:]
            whole = jnp.logical_and(kb < qb, seg_ref[kb * BLK] == q_last)

            @pl.when(whole)
            def _():
                bias_s[dst, :] = jnp.zeros((BLK, BLK), F32)

            @pl.when(jnp.logical_not(whole))
            def _():
                k_seg = jnp.broadcast_to(segv_ref[pl.ds(kb, 1), :].astype(F32), (BLK, BLK)).T
                k_pos = kb * BLK + iota((BLK, BLK), 0)
                q_pos = qb * BLK + iota((BLK, BLK), 1)
                ok = (k_seg == q_seg.astype(F32)) & (k_pos <= q_pos)
                bias_s[dst, :] = jnp.where(ok, 0.0, NEG_FILL)

        count, wide, narrow = visible_blocks(qb, seg_ref, allow_ref, on_block)

        def fill(n, c):
            list_s[n] = 2 * SHARDS
            dst = block_rows(n)
            k_s[dst, :] = jnp.zeros((BLK, HEAD_SIZE), BF16)
            v_s[dst, :] = jnp.zeros((BLK, HEAD_SIZE), BF16)
            bias_s[dst, :] = jnp.full((BLK, BLK), NEG_FILL, F32)
            return c

        lax.fori_loop(count, wide * WIDE + narrow * NARROW, fill, 0)

        def first_pass(start, blocks, slot, state):
            top, total, weighed = state
            rows = block_rows(start, blocks)
            scores = dot(k_s[rows, :], qt_s[...])
            scores = scores + jnp.concatenate([bias_s[rows, :]] * LOCAL_HEADS, axis=1)
            new_top = jnp.maximum(top, jnp.max(scores, axis=0, keepdims=True))
            factor = jnp.exp2((top - new_top) * EXP2_SCALE)
            e = jnp.exp2((scores - new_top) * EXP2_SCALE)
            dp = dot(v_s[rows, :], gt_ref[half])
            e_s[rows, :] = e
            dp_s[rows, :] = dp
            top_s[slot] = new_top
            total = total * factor + jnp.sum(e.reshape(-1, 8, LANES), axis=0)
            weighed = weighed * factor + jnp.sum((e * dp).reshape(-1, 8, LANES), axis=0)
            return (new_top, total, weighed)

        state = (
            jnp.full((1, LANES), NEG_FILL, F32),
            jnp.zeros((8, LANES), F32),
            jnp.zeros((8, LANES), F32),
        )
        state = lax.fori_loop(
            0, wide, lambda n, st: first_pass(n * WIDE, WIDE, n, st), state
        )
        top, total, weighed = lax.fori_loop(
            0, narrow, lambda n, st: first_pass(wide * WIDE, NARROW, wide, st), state
        )
        inverse = 1.0 / jnp.sum(total, axis=0, keepdims=True)
        out_dot = jnp.sum(weighed, axis=0, keepdims=True) * inverse

        def copy_out(start, blocks, buffer):
            return pltpu.make_async_copy(
                sg_s.at[buffer, pl.ds(0, blocks * BLK), :],
                sg_ref.at[half, block_rows(start, blocks), :],
                sent.at[buffer],
            )

        def second_pass(start, blocks, slot, buffer):
            rows = block_rows(start, blocks)
            factor = jnp.exp2((top_s[slot] - top) * EXP2_SCALE) * inverse
            weights = e_s[rows, :] * factor
            score_grad = (weights * (dp_s[rows, :] - out_dot)).astype(BF16)
            sg_s[buffer, : blocks * BLK, :] = score_grad
            copy_out(start, blocks, buffer).start()
            value_terms = dot(weights.astype(BF16), gr_ref[half])
            key_terms = dot(score_grad, qr_s[...])
            for n in range(blocks):
                dst = block_rows(list_s[start + n])
                acc_s[0, dst, :] += key_terms[n * BLK : (n + 1) * BLK, :]
                acc_s[1, dst, :] += value_terms[n * BLK : (n + 1) * BLK, :]

        def wide_step(n, c):
            @pl.when(n >= 2)
            def _():
                copy_out((n - 2) * WIDE, WIDE, n % 2).wait()

            second_pass(n * WIDE, WIDE, n, n % 2)
            return c

        lax.fori_loop(0, wide, wide_step, 0)

        @pl.when(narrow > 0)
        def _():
            second_pass(wide * WIDE, NARROW, wide, 2)
            copy_out(wide * WIDE, NARROW, 2).wait()

        for late in (1, 2):

            @pl.when(wide >= late)
            def _():
                copy_out((wide - late) * WIDE, WIDE, (wide - late) % 2).wait()

        return carry

    lax.fori_loop(0, 2, query_block, 0)
    rows = slice(0, SHARDS * TOK)

    @pl.when(core == 0)
    def _():
        keep_ref[...] = (acc_s[0, rows, :] * SCALE).astype(BF16)
        send_ref[...] = acc_s[1, rows, :].astype(BF16)

    @pl.when(core == 1)
    def _():
        keep_ref[...] = acc_s[1, rows, :].astype(BF16)
        send_ref[...] = (acc_s[0, rows, :] * SCALE).astype(BF16)


def query_grad_kernel(
    info_ref, seg_ref, allow_ref, kv_in, sg_ref, dq_ref, kt_s, dqt_s, sg_s, arrived, kv_ref, kv_sem
):
    shard = info_ref[0]
    base = jnp.maximum(shard - BACK, 0)
    copy = pltpu.make_async_copy(kv_in, kv_ref, kv_sem)
    copy.start()

    def fetch(half, step):
        rows = block_rows(step * NARROW, NARROW)
        return pltpu.make_async_copy(
            sg_ref.at[half, rows, :], sg_s.at[half, rows, :], arrived.at[half, step]
        )

    def steps_of(half):
        nothing = lambda kb, count: None
        count, wide, narrow = visible_blocks(shard * 2 + half, seg_ref, allow_ref, nothing)
        return wide * (WIDE // NARROW) + narrow

    def start_fetch(half, c):
        def one(step, c2):
            fetch(half, step).start()
            return c2

        return lax.fori_loop(0, steps_of(half), one, c)

    lax.fori_loop(0, 2, start_fetch, 0)
    copy.wait()

    def query_block(half, carry):
        def on_block(kb, count):
            lanes = block_rows(count % NARROW)
            k_blk = kv_ref[block_rows(kb - 2 * base), :HEAD_SIZE]
            kt_s[count // NARROW, :, lanes] = k_blk.astype(F32).T.astype(BF16)

        count, wide, narrow = visible_blocks(shard * 2 + half, seg_ref, allow_ref, on_block)
        steps = wide * (WIDE // NARROW) + narrow

        def fill(n, c):
            lanes = block_rows(n % NARROW)
            kt_s[n // NARROW, :, lanes] = jnp.zeros((HEAD_SIZE, BLK), BF16)
            return c

        lax.fori_loop(count, steps * NARROW, fill, 0)
        dqt_s[...] = jnp.zeros_like(dqt_s)

        def one_step(step, c):
            fetch(half, step).wait()
            dqt_s[...] += dot(kt_s[step], sg_s[half, block_rows(step * NARROW, NARROW), :])
            return c

        lax.fori_loop(0, steps, one_step, 0)
        for h in range(LOCAL_HEADS):
            block = dqt_s[:, h * BLK : (h + 1) * BLK] * SCALE
            dq_ref[block_rows(half), h * HEAD_SIZE : (h + 1) * HEAD_SIZE] = block.T.astype(BF16)
        return carry

    lax.fori_loop(0, 2, query_block, 0)


VMEM = pl.BlockSpec(memory_space=pltpu.VMEM)
SMEM = pl.BlockSpec(memory_space=pltpu.SMEM)
ANY = pl.BlockSpec(memory_space=pl.ANY)
HBM = pl.BlockSpec(memory_space=pltpu.HBM)


def call_permute(info, grad, own, mine, theirs):
    return pl.pallas_call(
        permute_kernel,
        in_specs=[SMEM] + [ANY] * (2 * RING + 2),
        out_specs=[VMEM] * 4,
        out_shape=[
            jax.ShapeDtypeStruct((WINDOW * TOK, 2 * HEAD_SIZE), BF16),
            jax.ShapeDtypeStruct((TOK, SHARDS * SLOTS), BF16),
            jax.ShapeDtypeStruct((2, LANES, HEAD_SIZE), BF16),
            jax.ShapeDtypeStruct((2, HEAD_SIZE, LANES), BF16),
        ],
        scratch_shapes=[pltpu.VMEM((SHARDS * SLOTS, TOK), F32)]
        + [pltpu.VMEM(x.shape, x.dtype) for x in (grad, own, *mine, *theirs)]
        + [pltpu.SemaphoreType.DMA((2 * RING + 2,))],
        compiler_params=pltpu.CompilerParams(vmem_limit_bytes=12 * 2**20),
        name="permute",
    )(info, grad, own, *mine, *theirs)


def call_attention(info, segments, allow, unpack, q_recv, gr, gt, kv_window):
    return pl.pallas_call(
        attention_kernel,
        in_specs=[SMEM, SMEM, SMEM] + [VMEM] * 6,
        out_specs=[VMEM, VMEM, HBM],
        out_shape=[
            jax.ShapeDtypeStruct((SHARDS * TOK, HEAD_SIZE), BF16),
            jax.ShapeDtypeStruct((SHARDS * TOK, HEAD_SIZE), BF16),
            jax.ShapeDtypeStruct((2, MOST_BLOCKS * BLK, LANES), BF16),
        ],
        scratch_shapes=[
            pltpu.VMEM((LANES, HEAD_SIZE), BF16),
            pltpu.VMEM((HEAD_SIZE, LANES), BF16),
            pltpu.VMEM((MOST_BLOCKS * BLK, HEAD_SIZE), BF16),
            pltpu.VMEM((MOST_BLOCKS * BLK, HEAD_SIZE), BF16),
            pltpu.VMEM((MOST_BLOCKS * BLK, BLK), F32),
            pltpu.VMEM((MOST_BLOCKS * BLK, LANES), F32),
            pltpu.VMEM((MOST_BLOCKS * BLK, LANES), F32),
            pltpu.VMEM((MOST_BLOCKS // WIDE + 1, 1, LANES), F32),
            pltpu.VMEM((2, SHARDS * TOK + BLK, HEAD_SIZE), F32),
            pltpu.VMEM((3, WIDE * BLK, LANES), BF16),
            pltpu.SMEM((MOST_BLOCKS,), jnp.int32),
            pltpu.SemaphoreType.DMA((3,)),
        ],
        compiler_params=pltpu.CompilerParams(vmem_limit_bytes=40 * 2**20),
        name="attention",
    )(info, segments, allow, segments.reshape(-1, BLK), unpack, q_recv, gr, gt, kv_window)


def call_query_grad(info, segments, allow, kv_window, score_grad):
    return pl.pallas_call(
        query_grad_kernel,
        in_specs=[SMEM, SMEM, SMEM, HBM, HBM],
        out_specs=VMEM,
        out_shape=jax.ShapeDtypeStruct((TOK, LOCAL_HEADS * HEAD_SIZE), BF16),
        scratch_shapes=[
            pltpu.VMEM((MOST_BLOCKS // NARROW, HEAD_SIZE, NARROW * BLK), BF16),
            pltpu.VMEM((HEAD_SIZE, LANES), F32),
            pltpu.VMEM((2, MOST_BLOCKS * BLK, LANES), BF16),
            pltpu.SemaphoreType.DMA((2, MOST_BLOCKS // NARROW)),
            pltpu.VMEM(kv_window.shape, BF16),
            pltpu.SemaphoreType.DMA(()),
        ],
        compiler_params=pltpu.CompilerParams(vmem_limit_bytes=VMEM_LIMIT),
        cost_estimate=pl.CostEstimate(
            flops=2 * TOK * 2048 * LANES, bytes_accessed=12 * 2**20, transcendentals=0
        ),
        name="query_grad",
    )(info, segments, allow, kv_window, score_grad)


def on_device(queries, keys_values, out_grad, place, segments, allow):
    tp_index = lax.axis_index("tp")
    ctx_index = lax.axis_index(("z", "x"))
    tp_size = lax.axis_size("tp")
    width = LOCAL_HEADS * HEAD_SIZE
    info = jnp.stack([ctx_index, tp_index % 2]).astype(jnp.int32)
    staged = pl.pallas_call(
        stage_kernel,
        in_specs=[VMEM, pl.BlockSpec(memory_space=pl.ANY)],
        out_specs=VMEM,
        out_shape=jax.ShapeDtypeStruct((TOK + META, 2 * HEAD_SIZE), BF16),
        scratch_shapes=[pltpu.SemaphoreType.DMA((2,))],
        name="stage",
    )(place.reshape(1, TOK), keys_values)
    beside = lax.ppermute(staged, "x", [(0, 1), (1, 0)])
    own = jnp.stack([staged, beside])
    g_send = out_grad.reshape(-1, tp_size, width).transpose(1, 0, 2)
    own, g_send = lax.optimization_barrier((own, g_send))

    def around(hops):
        pairs = []
        for k in range(SHARDS * tp_size):
            ctx, tp = k // tp_size, k % tp_size
            far = (ctx + (2 * hops if tp % 2 == 0 else -2 * hops)) % SHARDS
            pairs.append((k, far * tp_size + tp))
        return pairs

    swap = [(k, k ^ 1) for k in range(tp_size)]
    first = lax.ppermute(own, ("z", "x", "tp"), around(1))
    second = lax.ppermute(first, ("z", "x", "tp"), around(1))
    third = lax.ppermute(second, ("z", "x", "tp"), around(1))
    half = lax.dynamic_index_in_dim(second, tp_index % 2, 0, keepdims=False)
    fourth = lax.ppermute(half, ("z", "x", "tp"), around(2))
    mine = [first, second, third, fourth]
    g_local = lax.all_to_all(g_send, "tp", split_axis=0, concat_axis=0, tiled=True)
    g_local = g_local.reshape(TOK, width)
    q_send = pl.pallas_call(
        pack_kernel,
        in_specs=[VMEM, VMEM],
        out_specs=VMEM,
        out_shape=jax.ShapeDtypeStruct((SHARDS * SLOTS, width), BF16),
        name="pack",
    )(place.reshape(1, TOK), queries)
    q_send, *mine = lax.optimization_barrier((q_send, *mine))
    theirs = [lax.ppermute(piece, "tp", swap) for piece in mine]
    q_recv = lax.all_to_all(q_send, ("z", "x"), split_axis=0, concat_axis=0, tiled=True)
    kv_window, unpack, gr, gt = call_permute(info, g_local, own, mine, theirs)
    keep, send, score_grad = call_attention(
        info, segments, allow, unpack, q_recv, gr, gt, kv_window
    )
    recv = lax.ppermute(send, "tp", swap)
    part = (keep.astype(F32) + recv.astype(F32)).astype(BF16)
    part, score_grad = lax.optimization_barrier((part, score_grad))
    rows = TOK // tp_size
    parts = lax.all_to_all(
        part.reshape(SHARDS * tp_size, rows, HEAD_SIZE),
        ("z", "x", "tp"),
        split_axis=0,
        concat_axis=0,
        tiled=True,
    )
    grad_q = call_query_grad(info, segments, allow, kv_window, score_grad)
    parts, grad_q = lax.optimization_barrier((parts, grad_q))
    heads = jnp.sum(parts.reshape(SHARDS, tp_size, rows, HEAD_SIZE).astype(F32), axis=0)
    key_value_gradient = (
        heads.astype(BF16)
        .reshape(KEY_VALUE_HEADS, 2, rows, HEAD_SIZE)
        .transpose(1, 2, 0, 3)
        .reshape(2, rows, KEY_VALUE_HEADS * HEAD_SIZE)
    )
    return (grad_q, key_value_gradient)


def solution(mesh):
    tp_size = mesh.shape["tp"]
    split = Mesh(mesh.devices.reshape(Z_CHIPS, 2, tp_size), ("z", "x", "tp"))
    ctx = ("z", "x")
    in_specs = (P(ctx, "tp"), P(None, ctx, None), P((*ctx, "tp"), None), P(ctx), P(), P())
    out_specs = (P(ctx, "tp"), P(None, (*ctx, "tp"), None))
    return jax.shard_map(
        on_device, mesh=split, in_specs=in_specs, out_specs=out_specs, check_vma=False
    )
```

```python
import functools
import math

import jax
import jax.numpy as jnp
from jax import lax
from jax.experimental import pallas as pl
from jax.experimental.pallas import tpu as pltpu
from jax.sharding import Mesh
from jax.sharding import PartitionSpec as P

QUERY_HEAD_COUNT = 128
KEY_VALUE_HEADS = 8
HEAD_SIZE = 128
BLK = 128
TOK = 256
SHARDS = 16
SLOTS = 32
META = 16
Z_CHIPS = SHARDS // 2
RING = Z_CHIPS // 2
DOC_MOST = 2304
BACK = -(-DOC_MOST // TOK)
WINDOW = BACK + 1
BLOCKS_BACK = -(-DOC_MOST // BLK)
WIDE = 4
NARROW = 2
MOST_BLOCKS = WIDE * -(-(BLOCKS_BACK + 1) // WIDE)
LOCAL_HEADS = 8
LANES = LOCAL_HEADS * BLK
NEG_FILL = -1e30
VMEM_LIMIT = 60 * 2**20
SCALE = 1.0 / math.sqrt(HEAD_SIZE)
EXP2_SCALE = SCALE * math.log2(math.e)
F32 = jnp.float32
BF16 = jnp.bfloat16


def iota(shape, dim):
    return lax.broadcasted_iota(jnp.int32, shape, dim)


def dot(a, b):
    return jnp.dot(a, b, preferred_element_type=F32)


def ranks_within(member):
    earlier = (iota((TOK, TOK), 0) < iota((TOK, TOK), 1)).astype(F32).astype(BF16)
    counts = dot(member.astype(F32).astype(BF16), earlier)
    return jnp.where(member, counts, -1.0)


def pack_kernel(place_ref, rows_ref, out_ref):
    owner = place_ref[...] >> 8
    rank = ranks_within(owner == iota((SHARDS, TOK), 0))
    slot = iota((SLOTS, TOK), 0).astype(F32)
    picks = jnp.concatenate(
        [(rank[s : s + 1, :] == slot).astype(F32) for s in range(SHARDS)], axis=0
    ).astype(BF16)
    for first in range(0, rows_ref.shape[1], 256):
        cols = pl.ds(first, 256)
        out_ref[:, cols] = dot(picks, rows_ref[:, cols]).astype(BF16)


def stage_kernel(place_ref, kv_ref, out_ref, arrived):
    cols = pl.ds(pl.multiple_of((lax.axis_index("tp") // 2) * HEAD_SIZE, HEAD_SIZE), HEAD_SIZE)
    copies = [
        pltpu.make_async_copy(
            kv_ref.at[i, :, cols],
            out_ref.at[pl.ds(0, TOK), pl.ds(i * HEAD_SIZE, HEAD_SIZE)],
            arrived.at[i],
        )
        for i in range(2)
    ]
    for copy in copies:
        copy.start()
    place = place_ref[...]
    row = iota((META, TOK), 0)
    owner = jnp.broadcast_to((place >> 8).astype(F32), (META, TOK))
    within = jnp.broadcast_to((place & (TOK - 1)).astype(F32), (META, TOK))
    meta = jnp.where(row == 0, owner, jnp.where(row == 1, within, 0.0))
    out_ref[TOK:, :] = meta.astype(BF16)
    for copy in copies:
        copy.wait()


def fetch_all(sources, buffers, arrived):
    copies = [
        pltpu.make_async_copy(source, buffer, arrived.at[i])
        for i, (source, buffer) in enumerate(zip(sources, buffers))
    ]
    for copy in copies:
        copy.start()
    return copies


def permute_kernel(info_ref, *refs):
    count = 2 * RING + 1
    out_ref, unpack_ref, slots_s = refs[count : count + 3]
    buffers, arrived = refs[count + 3 : -1], refs[-1]
    own_ref, mine, theirs = buffers[0], buffers[1 : 1 + RING], buffers[1 + RING :]
    for copy in fetch_all(refs[:count], buffers, arrived):
        copy.wait()
    shard = info_ref[0]
    core = info_ref[1]
    base = jnp.maximum(shard - BACK, 0)
    z, x = shard // 2, shard % 2
    sources = [(own_ref.at[j], shard ^ j) for j in range(2)]
    for refs_k, side in ((mine, core), (theirs, 1 - core)):
        for k in range(1, RING):
            far = (z + k * (2 * side - 1) + Z_CHIPS) % Z_CHIPS
            sources += [(refs_k[k - 1].at[j], 2 * far + (x ^ j)) for j in range(2)]
        far = (z + RING) % Z_CHIPS
        sources += [(refs_k[RING - 1], 2 * far + (x ^ side))]
    owners = jnp.concatenate([ref[TOK : TOK + 1, :].astype(F32) for ref, _ in sources], axis=0)
    within = jnp.concatenate([ref[TOK + 1 : TOK + 2, :].astype(F32) for ref, _ in sources], axis=0)
    rank = ranks_within(owners == shard.astype(F32))
    slot = iota((SLOTS, TOK), 0).astype(F32)
    lane = iota((SLOTS, TOK), 1).astype(F32)
    for i, (_, source) in enumerate(sources):
        hit = rank[i : i + 1, :] == slot
        landing = jnp.sum(jnp.where(hit, within[i : i + 1, :] + 1.0, 0.0), axis=1, keepdims=True)
        rows = pl.ds(pl.multiple_of(source * SLOTS, SLOTS), SLOTS)
        slots_s[rows, :] = (landing == lane + 1.0).astype(F32)
    unpack_ref[...] = slots_s[...].T.astype(BF16)

    def one_shard(i, carry):
        rows = iota((TOK, TOK), 0).astype(F32)
        goal = jnp.where(owners == (base + i).astype(F32), within, -1.0)
        total = jnp.zeros((TOK, 2 * HEAD_SIZE), F32)
        for n, (ref, _) in enumerate(sources):
            picks = (goal[n : n + 1, :] == rows).astype(F32).astype(BF16)
            total = total + dot(picks, ref[:TOK, :])
        out_ref[pl.ds(pl.multiple_of(i * TOK, TOK), TOK), :] = total.astype(BF16)
        return carry

    lax.fori_loop(0, shard - base + 1, one_shard, 0)


def visible_blocks(qb, seg_ref, allow_ref, on_block):
    q_first = seg_ref[qb * BLK]

    def scan(kb, count):
        seen = jnp.logical_and(seg_ref[kb * BLK + BLK - 1] >= q_first, allow_ref[qb, kb] != 0)

        @pl.when(seen)
        def _():
            on_block(kb, count)

        return count + seen.astype(jnp.int32)

    count = lax.fori_loop(jnp.maximum(qb - BLOCKS_BACK, 0), qb + 1, scan, 0)
    wide = (count + 1) // WIDE
    narrow = (count + WIDE - 1) // WIDE - wide
    return count, wide, narrow


def block_rows(n, blocks=1):
    return pl.ds(pl.multiple_of(n * BLK, BLK), blocks * BLK)


def attention_kernel(
    info_ref,
    seg_ref,
    allow_ref,
    segv_ref,
    unpack_ref,
    recv_ref,
    grad_ref,
    kv_ref,
    keep_ref,
    send_ref,
    sg_ref,
    qr_s,
    qt_s,
    gr_s,
    gt_s,
    k_s,
    v_s,
    bias_s,
    e_s,
    dp_s,
    top_s,
    acc_s,
    sg_s,
    list_s,
    sent,
):
    shard = info_ref[0]
    core = info_ref[1]
    base = jnp.maximum(shard - BACK, 0)
    acc_s[...] = jnp.zeros_like(acc_s)

    def query_block(half, carry):
        qb = shard * 2 + half
        q_seg = segv_ref[pl.ds(qb, 1), :]
        q_last = seg_ref[qb * BLK + BLK - 1]
        picks = unpack_ref[block_rows(half), :]
        for pair in range(LOCAL_HEADS // 2):
            q_two = dot(picks, recv_ref[:, pair * 256 : (pair + 1) * 256])
            for i in range(2):
                mine = slice((2 * pair + i) * BLK, (2 * pair + i + 1) * BLK)
                q_one = q_two[:, i * HEAD_SIZE : (i + 1) * HEAD_SIZE]
                qr_s[mine, :] = q_one.astype(BF16)
                qt_s[:, mine] = q_one.T.astype(BF16)
                g_one = grad_ref[block_rows(half), pl.ds((2 * pair + i) * HEAD_SIZE, HEAD_SIZE)]
                gr_s[mine, :] = g_one
                gt_s[:, mine] = g_one.astype(F32).T.astype(BF16)

        def on_block(kb, count):
            list_s[count] = kb
            src = block_rows(kb - 2 * base)
            dst = block_rows(count)
            k_s[dst, :] = kv_ref[src, :HEAD_SIZE]
            v_s[dst, :] = kv_ref[src, HEAD_SIZE:]
            whole = jnp.logical_and(kb < qb, seg_ref[kb * BLK] == q_last)

            @pl.when(whole)
            def _():
                bias_s[dst, :] = jnp.zeros((BLK, BLK), F32)

            @pl.when(jnp.logical_not(whole))
            def _():
                k_seg = jnp.broadcast_to(segv_ref[pl.ds(kb, 1), :].astype(F32), (BLK, BLK)).T
                k_pos = kb * BLK + iota((BLK, BLK), 0)
                q_pos = qb * BLK + iota((BLK, BLK), 1)
                ok = (k_seg == q_seg.astype(F32)) & (k_pos <= q_pos)
                bias_s[dst, :] = jnp.where(ok, 0.0, NEG_FILL)

        count, wide, narrow = visible_blocks(qb, seg_ref, allow_ref, on_block)

        def fill(n, c):
            list_s[n] = 2 * SHARDS
            dst = block_rows(n)
            k_s[dst, :] = jnp.zeros((BLK, HEAD_SIZE), BF16)
            v_s[dst, :] = jnp.zeros((BLK, HEAD_SIZE), BF16)
            bias_s[dst, :] = jnp.full((BLK, BLK), NEG_FILL, F32)
            return c

        lax.fori_loop(count, wide * WIDE + narrow * NARROW, fill, 0)

        def first_pass(start, blocks, slot, state):
            top, total, weighed = state
            rows = block_rows(start, blocks)
            scores = dot(k_s[rows, :], qt_s[...])
            scores = scores + jnp.concatenate([bias_s[rows, :]] * LOCAL_HEADS, axis=1)
            new_top = jnp.maximum(top, jnp.max(scores, axis=0, keepdims=True))
            factor = jnp.exp2((top - new_top) * EXP2_SCALE)
            e = jnp.exp2((scores - new_top) * EXP2_SCALE)
            dp = dot(v_s[rows, :], gt_s[...])
            e_s[rows, :] = e
            dp_s[rows, :] = dp
            top_s[slot] = new_top
            total = total * factor + jnp.sum(e.reshape(-1, 8, LANES), axis=0)
            weighed = weighed * factor + jnp.sum((e * dp).reshape(-1, 8, LANES), axis=0)
            return (new_top, total, weighed)

        state = (
            jnp.full((1, LANES), NEG_FILL, F32),
            jnp.zeros((8, LANES), F32),
            jnp.zeros((8, LANES), F32),
        )
        state = lax.fori_loop(
            0, wide, lambda n, st: first_pass(n * WIDE, WIDE, n, st), state
        )
        top, total, weighed = lax.fori_loop(
            0, narrow, lambda n, st: first_pass(wide * WIDE, NARROW, wide, st), state
        )
        inverse = 1.0 / jnp.sum(total, axis=0, keepdims=True)
        out_dot = jnp.sum(weighed, axis=0, keepdims=True) * inverse

        def copy_out(start, blocks, buffer):
            return pltpu.make_async_copy(
                sg_s.at[buffer, pl.ds(0, blocks * BLK), :],
                sg_ref.at[half, block_rows(start, blocks), :],
                sent.at[buffer],
            )

        def second_pass(start, blocks, slot, buffer):
            rows = block_rows(start, blocks)
            factor = jnp.exp2((top_s[slot] - top) * EXP2_SCALE) * inverse
            weights = e_s[rows, :] * factor
            score_grad = (weights * (dp_s[rows, :] - out_dot)).astype(BF16)
            sg_s[buffer, : blocks * BLK, :] = score_grad
            copy_out(start, blocks, buffer).start()
            value_terms = dot(weights.astype(BF16), gr_s[...])
            key_terms = dot(score_grad, qr_s[...])
            for n in range(blocks):
                dst = block_rows(list_s[start + n])
                acc_s[0, dst, :] += key_terms[n * BLK : (n + 1) * BLK, :]
                acc_s[1, dst, :] += value_terms[n * BLK : (n + 1) * BLK, :]

        def wide_step(n, c):
            @pl.when(n >= 2)
            def _():
                copy_out((n - 2) * WIDE, WIDE, n % 2).wait()

            second_pass(n * WIDE, WIDE, n, n % 2)
            return c

        lax.fori_loop(0, wide, wide_step, 0)

        @pl.when(narrow > 0)
        def _():
            second_pass(wide * WIDE, NARROW, wide, 2)
            copy_out(wide * WIDE, NARROW, 2).wait()

        for late in (1, 2):

            @pl.when(wide >= late)
            def _():
                copy_out((wide - late) * WIDE, WIDE, (wide - late) % 2).wait()

        return carry

    lax.fori_loop(0, 2, query_block, 0)
    rows = slice(0, SHARDS * TOK)

    @pl.when(core == 0)
    def _():
        keep_ref[...] = (acc_s[0, rows, :] * SCALE).astype(BF16)
        send_ref[...] = acc_s[1, rows, :].astype(BF16)

    @pl.when(core == 1)
    def _():
        keep_ref[...] = acc_s[1, rows, :].astype(BF16)
        send_ref[...] = (acc_s[0, rows, :] * SCALE).astype(BF16)


def query_grad_kernel(
    info_ref, seg_ref, allow_ref, kv_in, sg_ref, dq_ref, kt_s, dqt_s, sg_s, arrived, kv_ref, kv_sem
):
    shard = info_ref[0]
    base = jnp.maximum(shard - BACK, 0)
    copy = pltpu.make_async_copy(kv_in, kv_ref, kv_sem)
    copy.start()

    def fetch(half, step):
        rows = block_rows(step * NARROW, NARROW)
        return pltpu.make_async_copy(
            sg_ref.at[half, rows, :], sg_s.at[half, rows, :], arrived.at[half, step]
        )

    def steps_of(half):
        nothing = lambda kb, count: None
        count, wide, narrow = visible_blocks(shard * 2 + half, seg_ref, allow_ref, nothing)
        return wide * (WIDE // NARROW) + narrow

    def start_fetch(half, c):
        def one(step, c2):
            fetch(half, step).start()
            return c2

        return lax.fori_loop(0, steps_of(half), one, c)

    lax.fori_loop(0, 2, start_fetch, 0)
    copy.wait()

    def query_block(half, carry):
        def on_block(kb, count):
            lanes = block_rows(count % NARROW)
            k_blk = kv_ref[block_rows(kb - 2 * base), :HEAD_SIZE]
            kt_s[count // NARROW, :, lanes] = k_blk.astype(F32).T.astype(BF16)

        count, wide, narrow = visible_blocks(shard * 2 + half, seg_ref, allow_ref, on_block)
        steps = wide * (WIDE // NARROW) + narrow

        def fill(n, c):
            lanes = block_rows(n % NARROW)
            kt_s[n // NARROW, :, lanes] = jnp.zeros((HEAD_SIZE, BLK), BF16)
            return c

        lax.fori_loop(count, steps * NARROW, fill, 0)
        dqt_s[...] = jnp.zeros_like(dqt_s)

        def one_step(step, c):
            fetch(half, step).wait()
            dqt_s[...] += dot(kt_s[step], sg_s[half, block_rows(step * NARROW, NARROW), :])
            return c

        lax.fori_loop(0, steps, one_step, 0)
        for h in range(LOCAL_HEADS):
            block = dqt_s[:, h * BLK : (h + 1) * BLK] * SCALE
            dq_ref[block_rows(half), h * HEAD_SIZE : (h + 1) * HEAD_SIZE] = block.T.astype(BF16)
        return carry

    lax.fori_loop(0, 2, query_block, 0)


VMEM = pl.BlockSpec(memory_space=pltpu.VMEM)
SMEM = pl.BlockSpec(memory_space=pltpu.SMEM)
ANY = pl.BlockSpec(memory_space=pl.ANY)
HBM = pl.BlockSpec(memory_space=pltpu.HBM)


def call_permute(info, own, mine, theirs):
    return pl.pallas_call(
        permute_kernel,
        in_specs=[SMEM] + [ANY] * (2 * RING + 1),
        out_specs=[VMEM] * 2,
        out_shape=[
            jax.ShapeDtypeStruct((WINDOW * TOK, 2 * HEAD_SIZE), BF16),
            jax.ShapeDtypeStruct((TOK, SHARDS * SLOTS), BF16),
        ],
        scratch_shapes=[pltpu.VMEM((SHARDS * SLOTS, TOK), F32)]
        + [pltpu.VMEM(x.shape, x.dtype) for x in (own, *mine, *theirs)]
        + [pltpu.SemaphoreType.DMA((2 * RING + 1,))],
        compiler_params=pltpu.CompilerParams(vmem_limit_bytes=12 * 2**20),
        name="permute",
    )(info, own, *mine, *theirs)


def call_attention(info, segments, allow, unpack, q_recv, grad, kv_window):
    return pl.pallas_call(
        attention_kernel,
        in_specs=[SMEM, SMEM, SMEM] + [VMEM] * 5,
        out_specs=[VMEM, VMEM, HBM],
        out_shape=[
            jax.ShapeDtypeStruct((SHARDS * TOK, HEAD_SIZE), BF16),
            jax.ShapeDtypeStruct((SHARDS * TOK, HEAD_SIZE), BF16),
            jax.ShapeDtypeStruct((2, MOST_BLOCKS * BLK, LANES), BF16),
        ],
        scratch_shapes=[
            pltpu.VMEM((LANES, HEAD_SIZE), BF16),
            pltpu.VMEM((HEAD_SIZE, LANES), BF16),
            pltpu.VMEM((LANES, HEAD_SIZE), BF16),
            pltpu.VMEM((HEAD_SIZE, LANES), BF16),
            pltpu.VMEM((MOST_BLOCKS * BLK, HEAD_SIZE), BF16),
            pltpu.VMEM((MOST_BLOCKS * BLK, HEAD_SIZE), BF16),
            pltpu.VMEM((MOST_BLOCKS * BLK, BLK), F32),
            pltpu.VMEM((MOST_BLOCKS * BLK, LANES), F32),
            pltpu.VMEM((MOST_BLOCKS * BLK, LANES), F32),
            pltpu.VMEM((MOST_BLOCKS // WIDE + 1, 1, LANES), F32),
            pltpu.VMEM((2, SHARDS * TOK + BLK, HEAD_SIZE), F32),
            pltpu.VMEM((3, WIDE * BLK, LANES), BF16),
            pltpu.SMEM((MOST_BLOCKS,), jnp.int32),
            pltpu.SemaphoreType.DMA((3,)),
        ],
        compiler_params=pltpu.CompilerParams(vmem_limit_bytes=40 * 2**20),
        name="attention",
    )(info, segments, allow, segments.reshape(-1, BLK), unpack, q_recv, grad, kv_window)


def call_query_grad(info, segments, allow, kv_window, score_grad):
    return pl.pallas_call(
        query_grad_kernel,
        in_specs=[SMEM, SMEM, SMEM, HBM, HBM],
        out_specs=VMEM,
        out_shape=jax.ShapeDtypeStruct((TOK, LOCAL_HEADS * HEAD_SIZE), BF16),
        scratch_shapes=[
            pltpu.VMEM((MOST_BLOCKS // NARROW, HEAD_SIZE, NARROW * BLK), BF16),
            pltpu.VMEM((HEAD_SIZE, LANES), F32),
            pltpu.VMEM((2, MOST_BLOCKS * BLK, LANES), BF16),
            pltpu.SemaphoreType.DMA((2, MOST_BLOCKS // NARROW)),
            pltpu.VMEM(kv_window.shape, BF16),
            pltpu.SemaphoreType.DMA(()),
        ],
        compiler_params=pltpu.CompilerParams(vmem_limit_bytes=VMEM_LIMIT),
        cost_estimate=pl.CostEstimate(
            flops=2 * TOK * 2048 * LANES, bytes_accessed=12 * 2**20, transcendentals=0
        ),
        name="query_grad",
    )(info, segments, allow, kv_window, score_grad)


def on_device(queries, keys_values, out_grad, place, segments, allow):
    tp_index = lax.axis_index("tp")
    ctx_index = lax.axis_index(("z", "x"))
    tp_size = lax.axis_size("tp")
    width = LOCAL_HEADS * HEAD_SIZE
    info = jnp.stack([ctx_index, tp_index % 2]).astype(jnp.int32)
    staged = pl.pallas_call(
        stage_kernel,
        in_specs=[VMEM, pl.BlockSpec(memory_space=pl.ANY)],
        out_specs=VMEM,
        out_shape=jax.ShapeDtypeStruct((TOK + META, 2 * HEAD_SIZE), BF16),
        scratch_shapes=[pltpu.SemaphoreType.DMA((2,))],
        name="stage",
    )(place.reshape(1, TOK), keys_values)
    beside = lax.ppermute(staged, "x", [(0, 1), (1, 0)])
    own = jnp.stack([staged, beside])
    g_send = out_grad.reshape(-1, tp_size, width).transpose(1, 0, 2)
    own, g_send = lax.optimization_barrier((own, g_send))

    def around(hops):
        pairs = []
        for k in range(SHARDS * tp_size):
            ctx, tp = k // tp_size, k % tp_size
            far = (ctx + (2 * hops if tp % 2 == 0 else -2 * hops)) % SHARDS
            pairs.append((k, far * tp_size + tp))
        return pairs

    swap = [(k, k ^ 1) for k in range(tp_size)]
    first = lax.ppermute(own, ("z", "x", "tp"), around(1))
    second = lax.ppermute(first, ("z", "x", "tp"), around(1))
    third = lax.ppermute(second, ("z", "x", "tp"), around(1))
    half = lax.dynamic_index_in_dim(second, tp_index % 2, 0, keepdims=False)
    fourth = lax.ppermute(half, ("z", "x", "tp"), around(2))
    mine = [first, second, third, fourth]
    g_local = lax.all_to_all(g_send, "tp", split_axis=0, concat_axis=0, tiled=True)
    g_local = g_local.reshape(TOK, width)
    q_send = pl.pallas_call(
        pack_kernel,
        in_specs=[VMEM, VMEM],
        out_specs=VMEM,
        out_shape=jax.ShapeDtypeStruct((SHARDS * SLOTS, width), BF16),
        name="pack",
    )(place.reshape(1, TOK), queries)
    q_send, *mine = lax.optimization_barrier((q_send, *mine))
    theirs = [lax.ppermute(piece, "tp", swap) for piece in mine]
    q_recv = lax.all_to_all(q_send, ("z", "x"), split_axis=0, concat_axis=0, tiled=True)
    kv_window, unpack = call_permute(info, own, mine, theirs)
    keep, send, score_grad = call_attention(
        info, segments, allow, unpack, q_recv, g_local, kv_window
    )
    recv = lax.ppermute(send, "tp", swap)
    part = (keep.astype(F32) + recv.astype(F32)).astype(BF16)
    part, score_grad, late_ctx = lax.optimization_barrier((part, score_grad, ctx_index))
    rows = TOK // tp_size
    parts = lax.all_to_all(
        part.reshape(SHARDS * tp_size, rows, HEAD_SIZE),
        ("z", "x", "tp"),
        split_axis=0,
        concat_axis=0,
        tiled=True,
    )
    late_info = jnp.stack([late_ctx, late_ctx]).astype(jnp.int32)
    grad_q = call_query_grad(late_info, segments, allow, kv_window, score_grad)
    parts, grad_q = lax.optimization_barrier((parts, grad_q))
    heads = jnp.sum(parts.reshape(SHARDS, tp_size, rows, HEAD_SIZE).astype(F32), axis=0)
    key_value_gradient = (
        heads.astype(BF16)
        .reshape(KEY_VALUE_HEADS, 2, rows, HEAD_SIZE)
        .transpose(1, 2, 0, 3)
        .reshape(2, rows, KEY_VALUE_HEADS * HEAD_SIZE)
    )
    return (grad_q, key_value_gradient)


def solution(mesh):
    tp_size = mesh.shape["tp"]
    split = Mesh(mesh.devices.reshape(Z_CHIPS, 2, tp_size), ("z", "x", "tp"))
    ctx = ("z", "x")
    in_specs = (P(ctx, "tp"), P(None, ctx, None), P((*ctx, "tp"), None), P(ctx), P(), P())
    out_specs = (P(ctx, "tp"), P(None, (*ctx, "tp"), None))
    return jax.shard_map(
        on_device, mesh=split, in_specs=in_specs, out_specs=out_specs, check_vma=False
    )
```

```python
import functools
import math

import jax
import jax.numpy as jnp
from jax import lax
from jax.experimental import pallas as pl
from jax.experimental.pallas import tpu as pltpu
from jax.sharding import Mesh
from jax.sharding import PartitionSpec as P

QUERY_HEAD_COUNT = 128
KEY_VALUE_HEADS = 8
HEAD_SIZE = 128
BLK = 128
TOK = 256
SHARDS = 16
SLOTS = 32
META = 16
Z_CHIPS = SHARDS // 2
RING = Z_CHIPS // 2
DOC_MOST = 2304
BACK = -(-DOC_MOST // TOK)
WINDOW = BACK + 1
BLOCKS_BACK = -(-DOC_MOST // BLK)
WIDE = 8
MIDDLE = 4
NARROW = 2
MOST_BLOCKS = MIDDLE * -(-(BLOCKS_BACK + 1) // MIDDLE)
LOCAL_HEADS = 8
LANES = LOCAL_HEADS * BLK
PICKS_FIRST = WINDOW * TOK
PICKS_PARTS = SHARDS * SLOTS // (2 * HEAD_SIZE)
NEG_FILL = -1e30
VMEM_LIMIT = 60 * 2**20
SCALE = 1.0 / math.sqrt(HEAD_SIZE)
EXP2_SCALE = SCALE * math.log2(math.e)
F32 = jnp.float32
BF16 = jnp.bfloat16


def iota(shape, dim):
    return lax.broadcasted_iota(jnp.int32, shape, dim)


def dot(a, b):
    return jnp.dot(a, b, preferred_element_type=F32)


def ranks_within(member):
    earlier = (iota((TOK, TOK), 0) < iota((TOK, TOK), 1)).astype(F32).astype(BF16)
    counts = dot(member.astype(F32).astype(BF16), earlier)
    return jnp.where(member, counts, -1.0)


def pack_kernel(place_ref, rows_ref, out_ref):
    owner = place_ref[...] >> 8
    rank = ranks_within(owner == iota((SHARDS, TOK), 0))
    slot = iota((SLOTS, TOK), 0).astype(F32)
    picks = jnp.concatenate(
        [(rank[s : s + 1, :] == slot).astype(F32) for s in range(SHARDS)], axis=0
    ).astype(BF16)
    for first in range(0, rows_ref.shape[1], 256):
        cols = pl.ds(first, 256)
        out_ref[:, cols] = dot(picks, rows_ref[:, cols]).astype(BF16)


def stage_kernel(place_ref, kv_ref, out_ref, arrived):
    cols = pl.ds(pl.multiple_of((lax.axis_index("tp") // 2) * HEAD_SIZE, HEAD_SIZE), HEAD_SIZE)
    copies = [
        pltpu.make_async_copy(
            kv_ref.at[i, :, cols],
            out_ref.at[pl.ds(0, TOK), pl.ds(i * HEAD_SIZE, HEAD_SIZE)],
            arrived.at[i],
        )
        for i in range(2)
    ]
    for copy in copies:
        copy.start()
    place = place_ref[...]
    row = iota((META, TOK), 0)
    owner = jnp.broadcast_to((place >> 8).astype(F32), (META, TOK))
    within = jnp.broadcast_to((place & (TOK - 1)).astype(F32), (META, TOK))
    meta = jnp.where(row == 0, owner, jnp.where(row == 1, within, 0.0))
    out_ref[TOK:, :] = meta.astype(BF16)
    for copy in copies:
        copy.wait()


def fetch_all(sources, buffers, arrived):
    copies = [
        pltpu.make_async_copy(source, buffer, arrived.at[i])
        for i, (source, buffer) in enumerate(zip(sources, buffers))
    ]
    for copy in copies:
        copy.start()
    return copies


def permute_kernel(info_ref, *refs):
    count = 2 * RING + 1
    out_ref, slots_s = refs[count : count + 2]
    buffers, arrived = refs[count + 2 : -1], refs[-1]
    own_ref, mine, theirs = buffers[0], buffers[1 : 1 + RING], buffers[1 + RING :]
    for copy in fetch_all(refs[:count], buffers, arrived):
        copy.wait()
    shard = info_ref[0]
    core = info_ref[1]
    base = jnp.maximum(shard - BACK, 0)
    z, x = shard // 2, shard % 2
    sources = [(own_ref.at[j], shard ^ j) for j in range(2)]
    for refs_k, side in ((mine, core), (theirs, 1 - core)):
        for k in range(1, RING):
            far = (z + k * (2 * side - 1) + Z_CHIPS) % Z_CHIPS
            sources += [(refs_k[k - 1].at[j], 2 * far + (x ^ j)) for j in range(2)]
        far = (z + RING) % Z_CHIPS
        sources += [(refs_k[RING - 1], 2 * far + (x ^ side))]
    owners = jnp.concatenate([ref[TOK : TOK + 1, :].astype(F32) for ref, _ in sources], axis=0)
    within = jnp.concatenate([ref[TOK + 1 : TOK + 2, :].astype(F32) for ref, _ in sources], axis=0)
    rank = ranks_within(owners == shard.astype(F32))
    slot = iota((SLOTS, TOK), 0).astype(F32)
    lane = iota((SLOTS, TOK), 1).astype(F32)
    for i, (_, source) in enumerate(sources):
        hit = rank[i : i + 1, :] == slot
        landing = jnp.sum(jnp.where(hit, within[i : i + 1, :] + 1.0, 0.0), axis=1, keepdims=True)
        rows = pl.ds(pl.multiple_of(source * SLOTS, SLOTS), SLOTS)
        slots_s[rows, :] = (landing == lane + 1.0).astype(F32)
    for j in range(PICKS_PARTS):
        part = slots_s[j * TOK : (j + 1) * TOK, :].T.astype(BF16)
        out_ref[PICKS_FIRST + j * TOK : PICKS_FIRST + (j + 1) * TOK, :] = part

    def one_shard(i, carry):
        rows = iota((TOK, TOK), 0).astype(F32)
        goal = jnp.where(owners == (base + i).astype(F32), within, -1.0)
        total = jnp.zeros((TOK, 2 * HEAD_SIZE), F32)
        for n, (ref, _) in enumerate(sources):
            picks = (goal[n : n + 1, :] == rows).astype(F32).astype(BF16)
            total = total + dot(picks, ref[:TOK, :])
        out_ref[pl.ds(pl.multiple_of(i * TOK, TOK), TOK), :] = total.astype(BF16)
        return carry

    lax.fori_loop(0, shard - base + 1, one_shard, 0)


def visible_blocks(qb, seg_ref, allow_ref, on_block):
    q_first = seg_ref[qb * BLK]

    def scan(kb, count):
        seen = jnp.logical_and(seg_ref[kb * BLK + BLK - 1] >= q_first, allow_ref[qb, kb] != 0)

        @pl.when(seen)
        def _():
            on_block(kb, count)

        return count + seen.astype(jnp.int32)

    count = lax.fori_loop(jnp.maximum(qb - BLOCKS_BACK, 0), qb + 1, scan, 0)
    wide = count // WIDE
    rest = count - wide * WIDE
    middle = (rest + 1) // MIDDLE
    narrow = (rest + MIDDLE - 1) // MIDDLE - middle
    return count, wide, middle, narrow


def block_rows(n, blocks=1):
    return pl.ds(pl.multiple_of(n * BLK, BLK), blocks * BLK)


def attention_kernel(
    info_ref,
    seg_ref,
    allow_ref,
    segv_ref,
    recv_ref,
    grad_ref,
    kv_ref,
    keep_ref,
    send_ref,
    sg_ref,
    qr_s,
    qt_s,
    gr_s,
    gt_s,
    k_s,
    v_s,
    bias_s,
    e_s,
    dp_s,
    top_s,
    acc_s,
    sg_s,
    list_s,
    sent,
):
    shard = info_ref[0]
    core = info_ref[1]
    base = jnp.maximum(shard - BACK, 0)
    acc_s[...] = jnp.zeros_like(acc_s)

    def query_block(half, carry):
        qb = shard * 2 + half
        q_seg = segv_ref[pl.ds(qb, 1), :]
        q_last = seg_ref[qb * BLK + BLK - 1]
        picks = jnp.concatenate(
            [kv_ref[block_rows(PICKS_FIRST // BLK + 2 * j + half), :] for j in range(PICKS_PARTS)],
            axis=1,
        )
        for pair in range(LOCAL_HEADS // 2):
            q_two = dot(picks, recv_ref[:, pair * 256 : (pair + 1) * 256])
            for i in range(2):
                mine = slice((2 * pair + i) * BLK, (2 * pair + i + 1) * BLK)
                q_one = q_two[:, i * HEAD_SIZE : (i + 1) * HEAD_SIZE]
                qr_s[mine, :] = q_one.astype(BF16)
                qt_s[:, mine] = q_one.T.astype(BF16)
                g_one = grad_ref[block_rows(half), pl.ds((2 * pair + i) * HEAD_SIZE, HEAD_SIZE)]
                gr_s[mine, :] = g_one
                gt_s[:, mine] = g_one.astype(F32).T.astype(BF16)

        def on_block(kb, count):
            list_s[count] = kb
            src = block_rows(kb - 2 * base)
            dst = block_rows(count)
            k_s[dst, :] = kv_ref[src, :HEAD_SIZE]
            v_s[dst, :] = kv_ref[src, HEAD_SIZE:]
            whole = jnp.logical_and(kb < qb, seg_ref[kb * BLK] == q_last)

            @pl.when(whole)
            def _():
                bias_s[dst, :] = jnp.zeros((BLK, BLK), F32)

            @pl.when(jnp.logical_not(whole))
            def _():
                k_seg = jnp.broadcast_to(segv_ref[pl.ds(kb, 1), :].astype(F32), (BLK, BLK)).T
                k_pos = kb * BLK + iota((BLK, BLK), 0)
                q_pos = qb * BLK + iota((BLK, BLK), 1)
                ok = (k_seg == q_seg.astype(F32)) & (k_pos <= q_pos)
                bias_s[dst, :] = jnp.where(ok, 0.0, NEG_FILL)

        count, wide, middle, narrow = visible_blocks(qb, seg_ref, allow_ref, on_block)
        middle_first = wide * WIDE
        narrow_first = middle_first + middle * MIDDLE

        def fill(n, c):
            list_s[n] = 2 * SHARDS
            dst = block_rows(n)
            k_s[dst, :] = jnp.zeros((BLK, HEAD_SIZE), BF16)
            v_s[dst, :] = jnp.zeros((BLK, HEAD_SIZE), BF16)
            bias_s[dst, :] = jnp.full((BLK, BLK), NEG_FILL, F32)
            return c

        lax.fori_loop(count, narrow_first + narrow * NARROW, fill, 0)

        def first_pass(start, blocks, slot, state):
            top, total, weighed = state
            rows = block_rows(start, blocks)
            scores = dot(k_s[rows, :], qt_s[...])
            scores = scores + jnp.concatenate([bias_s[rows, :]] * LOCAL_HEADS, axis=1)
            new_top = jnp.maximum(top, jnp.max(scores, axis=0, keepdims=True))
            factor = jnp.exp2((top - new_top) * EXP2_SCALE)
            e = jnp.exp2((scores - new_top) * EXP2_SCALE)
            dp = dot(v_s[rows, :], gt_s[...])
            e_s[rows, :] = e
            dp_s[rows, :] = dp
            top_s[slot] = new_top
            total = total * factor + jnp.sum(e.reshape(-1, 8, LANES), axis=0)
            weighed = weighed * factor + jnp.sum((e * dp).reshape(-1, 8, LANES), axis=0)
            return (new_top, total, weighed)

        state = (
            jnp.full((1, LANES), NEG_FILL, F32),
            jnp.zeros((8, LANES), F32),
            jnp.zeros((8, LANES), F32),
        )
        state = lax.fori_loop(0, wide, lambda n, st: first_pass(n * WIDE, WIDE, n, st), state)
        state = lax.fori_loop(
            0,
            middle,
            lambda n, st: first_pass(middle_first + n * MIDDLE, MIDDLE, wide + n, st),
            state,
        )
        top, total, weighed = lax.fori_loop(
            0,
            narrow,
            lambda n, st: first_pass(narrow_first, NARROW, wide + middle, st),
            state,
        )
        inverse = 1.0 / jnp.sum(total, axis=0, keepdims=True)
        out_dot = jnp.sum(weighed, axis=0, keepdims=True) * inverse

        def copy_out(start, blocks, slot):
            rows = block_rows(start, blocks)
            return pltpu.make_async_copy(sg_s.at[rows, :], sg_ref.at[half, rows, :], sent.at[slot])

        def second_pass(start, blocks, slot):
            rows = block_rows(start, blocks)
            factor = jnp.exp2((top_s[slot] - top) * EXP2_SCALE) * inverse
            weights = e_s[rows, :] * factor
            score_grad = (weights * (dp_s[rows, :] - out_dot)).astype(BF16)
            sg_s[rows, :] = score_grad
            copy_out(start, blocks, slot).start()
            value_terms = dot(weights.astype(BF16), gr_s[...])
            key_terms = dot(score_grad, qr_s[...])
            for n in range(blocks):
                dst = block_rows(list_s[start + n])
                acc_s[0, dst, :] += key_terms[n * BLK : (n + 1) * BLK, :]
                acc_s[1, dst, :] += value_terms[n * BLK : (n + 1) * BLK, :]

        def finish(step, steps):
            lax.fori_loop(0, steps, lambda n, c: step(n) or c, 0)

        finish(lambda n: second_pass(n * WIDE, WIDE, n), wide)
        finish(lambda n: second_pass(middle_first + n * MIDDLE, MIDDLE, wide + n), middle)
        finish(lambda n: second_pass(narrow_first, NARROW, wide + middle), narrow)
        finish(lambda n: copy_out(n * WIDE, WIDE, n).wait(), wide)
        finish(lambda n: copy_out(middle_first + n * MIDDLE, MIDDLE, wide + n).wait(), middle)
        finish(lambda n: copy_out(narrow_first, NARROW, wide + middle).wait(), narrow)
        return carry

    lax.fori_loop(0, 2, query_block, 0)
    rows = slice(0, SHARDS * TOK)

    @pl.when(core == 0)
    def _():
        keep_ref[...] = (acc_s[0, rows, :] * SCALE).astype(BF16)
        send_ref[...] = acc_s[1, rows, :].astype(BF16)

    @pl.when(core == 1)
    def _():
        keep_ref[...] = acc_s[1, rows, :].astype(BF16)
        send_ref[...] = (acc_s[0, rows, :] * SCALE).astype(BF16)


def query_grad_kernel(
    info_ref, seg_ref, allow_ref, kv_in, sg_ref, dq_ref, kt_s, dqt_s, sg_s, arrived, kv_ref, kv_sem
):
    shard = info_ref[0]
    base = jnp.maximum(shard - BACK, 0)
    copy = pltpu.make_async_copy(kv_in.at[pl.ds(0, PICKS_FIRST), :], kv_ref, kv_sem)
    copy.start()

    def fetch(half, step):
        rows = block_rows(step * NARROW, NARROW)
        return pltpu.make_async_copy(
            sg_ref.at[half, rows, :], sg_s.at[half, rows, :], arrived.at[half, step]
        )

    def steps_of(half):
        nothing = lambda kb, count: None
        count, *_ = visible_blocks(shard * 2 + half, seg_ref, allow_ref, nothing)
        return (count + NARROW - 1) // NARROW

    def start_fetch(half, c):
        def one(step, c2):
            fetch(half, step).start()
            return c2

        return lax.fori_loop(0, steps_of(half), one, c)

    lax.fori_loop(0, 2, start_fetch, 0)
    copy.wait()

    def query_block(half, carry):
        def on_block(kb, count):
            lanes = block_rows(count % NARROW)
            k_blk = kv_ref[block_rows(kb - 2 * base), :HEAD_SIZE]
            kt_s[count // NARROW, :, lanes] = k_blk.astype(F32).T.astype(BF16)

        count, *_ = visible_blocks(shard * 2 + half, seg_ref, allow_ref, on_block)
        steps = (count + NARROW - 1) // NARROW

        def fill(n, c):
            lanes = block_rows(n % NARROW)
            kt_s[n // NARROW, :, lanes] = jnp.zeros((HEAD_SIZE, BLK), BF16)
            return c

        lax.fori_loop(count, steps * NARROW, fill, 0)
        dqt_s[...] = jnp.zeros_like(dqt_s)

        def one_step(step, c):
            fetch(half, step).wait()
            dqt_s[...] += dot(kt_s[step], sg_s[half, block_rows(step * NARROW, NARROW), :])
            return c

        lax.fori_loop(0, steps, one_step, 0)
        for h in range(LOCAL_HEADS):
            block = dqt_s[:, h * BLK : (h + 1) * BLK] * SCALE
            dq_ref[block_rows(half), h * HEAD_SIZE : (h + 1) * HEAD_SIZE] = block.T.astype(BF16)
        return carry

    lax.fori_loop(0, 2, query_block, 0)


VMEM = pl.BlockSpec(memory_space=pltpu.VMEM)
SMEM = pl.BlockSpec(memory_space=pltpu.SMEM)
ANY = pl.BlockSpec(memory_space=pl.ANY)
HBM = pl.BlockSpec(memory_space=pltpu.HBM)


def call_permute(info, own, mine, theirs):
    return pl.pallas_call(
        permute_kernel,
        in_specs=[SMEM] + [ANY] * (2 * RING + 1),
        out_specs=VMEM,
        out_shape=jax.ShapeDtypeStruct((PICKS_FIRST + PICKS_PARTS * TOK, 2 * HEAD_SIZE), BF16),
        scratch_shapes=[pltpu.VMEM((SHARDS * SLOTS, TOK), F32)]
        + [pltpu.VMEM(x.shape, x.dtype) for x in (own, *mine, *theirs)]
        + [pltpu.SemaphoreType.DMA((2 * RING + 1,))],
        compiler_params=pltpu.CompilerParams(vmem_limit_bytes=12 * 2**20),
        name="permute",
    )(info, own, *mine, *theirs)


def call_attention(info, segments, allow, q_recv, grad, kv_window):
    return pl.pallas_call(
        attention_kernel,
        in_specs=[SMEM, SMEM, SMEM] + [VMEM] * 4,
        out_specs=[VMEM, VMEM, HBM],
        out_shape=[
            jax.ShapeDtypeStruct((SHARDS * TOK, HEAD_SIZE), BF16),
            jax.ShapeDtypeStruct((SHARDS * TOK, HEAD_SIZE), BF16),
            jax.ShapeDtypeStruct((2, MOST_BLOCKS * BLK, LANES), BF16),
        ],
        scratch_shapes=[
            pltpu.VMEM((LANES, HEAD_SIZE), BF16),
            pltpu.VMEM((HEAD_SIZE, LANES), BF16),
            pltpu.VMEM((LANES, HEAD_SIZE), BF16),
            pltpu.VMEM((HEAD_SIZE, LANES), BF16),
            pltpu.VMEM((MOST_BLOCKS * BLK, HEAD_SIZE), BF16),
            pltpu.VMEM((MOST_BLOCKS * BLK, HEAD_SIZE), BF16),
            pltpu.VMEM((MOST_BLOCKS * BLK, BLK), F32),
            pltpu.VMEM((MOST_BLOCKS * BLK, LANES), F32),
            pltpu.VMEM((MOST_BLOCKS * BLK, LANES), F32),
            pltpu.VMEM((MOST_BLOCKS // WIDE + 3, 1, LANES), F32),
            pltpu.VMEM((2, SHARDS * TOK + BLK, HEAD_SIZE), F32),
            pltpu.VMEM((MOST_BLOCKS * BLK, LANES), BF16),
            pltpu.SMEM((MOST_BLOCKS,), jnp.int32),
            pltpu.SemaphoreType.DMA((MOST_BLOCKS // WIDE + 3,)),
        ],
        compiler_params=pltpu.CompilerParams(vmem_limit_bytes=48 * 2**20),
        name="attention",
    )(info, segments, allow, segments.reshape(-1, BLK), q_recv, grad, kv_window)


def call_query_grad(info, segments, allow, kv_window, score_grad):
    return pl.pallas_call(
        query_grad_kernel,
        in_specs=[SMEM, SMEM, SMEM, HBM, HBM],
        out_specs=VMEM,
        out_shape=jax.ShapeDtypeStruct((TOK, LOCAL_HEADS * HEAD_SIZE), BF16),
        scratch_shapes=[
            pltpu.VMEM((MOST_BLOCKS // NARROW, HEAD_SIZE, NARROW * BLK), BF16),
            pltpu.VMEM((HEAD_SIZE, LANES), F32),
            pltpu.VMEM((2, MOST_BLOCKS * BLK, LANES), BF16),
            pltpu.SemaphoreType.DMA((2, MOST_BLOCKS // NARROW)),
            pltpu.VMEM((PICKS_FIRST, 2 * HEAD_SIZE), BF16),
            pltpu.SemaphoreType.DMA(()),
        ],
        compiler_params=pltpu.CompilerParams(vmem_limit_bytes=VMEM_LIMIT),
        cost_estimate=pl.CostEstimate(
            flops=2 * TOK * 2048 * LANES, bytes_accessed=12 * 2**20, transcendentals=0
        ),
        name="query_grad",
    )(info, segments, allow, kv_window, score_grad)


def on_device(queries, keys_values, out_grad, place, segments, allow):
    tp_index = lax.axis_index("tp")
    ctx_index = lax.axis_index(("z", "x"))
    tp_size = lax.axis_size("tp")
    width = LOCAL_HEADS * HEAD_SIZE
    info = jnp.stack([ctx_index, tp_index % 2]).astype(jnp.int32)
    staged = pl.pallas_call(
        stage_kernel,
        in_specs=[VMEM, pl.BlockSpec(memory_space=pl.ANY)],
        out_specs=VMEM,
        out_shape=jax.ShapeDtypeStruct((TOK + META, 2 * HEAD_SIZE), BF16),
        scratch_shapes=[pltpu.SemaphoreType.DMA((2,))],
        name="stage",
    )(place.reshape(1, TOK), keys_values)
    beside = lax.ppermute(staged, "x", [(0, 1), (1, 0)])
    own = jnp.stack([staged, beside])
    g_send = out_grad.reshape(-1, tp_size, width).transpose(1, 0, 2)
    own, g_send = lax.optimization_barrier((own, g_send))

    def around(hops):
        pairs = []
        for k in range(SHARDS * tp_size):
            ctx, tp = k // tp_size, k % tp_size
            far = (ctx + (2 * hops if tp % 2 == 0 else -2 * hops)) % SHARDS
            pairs.append((k, far * tp_size + tp))
        return pairs

    swap = [(k, k ^ 1) for k in range(tp_size)]
    first = lax.ppermute(own, ("z", "x", "tp"), around(1))
    second = lax.ppermute(first, ("z", "x", "tp"), around(1))
    third = lax.ppermute(second, ("z", "x", "tp"), around(1))
    half = lax.dynamic_index_in_dim(second, tp_index % 2, 0, keepdims=False)
    fourth = lax.ppermute(half, ("z", "x", "tp"), around(2))
    mine = [first, second, third, fourth]
    g_local = lax.all_to_all(g_send, "tp", split_axis=0, concat_axis=0, tiled=True)
    g_local = g_local.reshape(TOK, width)
    q_send = pl.pallas_call(
        pack_kernel,
        in_specs=[VMEM, VMEM],
        out_specs=VMEM,
        out_shape=jax.ShapeDtypeStruct((SHARDS * SLOTS, width), BF16),
        name="pack",
    )(place.reshape(1, TOK), queries)
    q_send, *mine = lax.optimization_barrier((q_send, *mine))
    theirs = [lax.ppermute(piece, "tp", swap) for piece in mine]
    q_recv = lax.all_to_all(q_send, ("z", "x"), split_axis=0, concat_axis=0, tiled=True)
    kv_window = call_permute(info, own, mine, theirs)
    keep, send, score_grad = call_attention(
        info, segments, allow, q_recv, g_local, kv_window
    )
    recv = lax.ppermute(send, "tp", swap)
    part = (keep.astype(F32) + recv.astype(F32)).astype(BF16)
    part, score_grad, late_ctx = lax.optimization_barrier((part, score_grad, ctx_index))
    rows = TOK // tp_size
    parts = lax.all_to_all(
        part.reshape(SHARDS * tp_size, rows, HEAD_SIZE),
        ("z", "x", "tp"),
        split_axis=0,
        concat_axis=0,
        tiled=True,
    )
    late_info = jnp.stack([late_ctx, late_ctx]).astype(jnp.int32)
    grad_q = call_query_grad(late_info, segments, allow, kv_window, score_grad)
    parts, grad_q = lax.optimization_barrier((parts, grad_q))
    heads = jnp.sum(parts.reshape(SHARDS, tp_size, rows, HEAD_SIZE).astype(F32), axis=0)
    key_value_gradient = (
        heads.astype(BF16)
        .reshape(KEY_VALUE_HEADS, 2, rows, HEAD_SIZE)
        .transpose(1, 2, 0, 3)
        .reshape(2, rows, KEY_VALUE_HEADS * HEAD_SIZE)
    )
    return (grad_q, key_value_gradient)


def solution(mesh):
    tp_size = mesh.shape["tp"]
    split = Mesh(mesh.devices.reshape(Z_CHIPS, 2, tp_size), ("z", "x", "tp"))
    ctx = ("z", "x")
    in_specs = (P(ctx, "tp"), P(None, ctx, None), P((*ctx, "tp"), None), P(ctx), P(), P())
    out_specs = (P(ctx, "tp"), P(None, (*ctx, "tp"), None))
    return jax.shard_map(
        on_device, mesh=split, in_specs=in_specs, out_specs=out_specs, check_vma=False
    )
```

```python
import functools
import math

import jax
import jax.numpy as jnp
from jax import lax
from jax.experimental import pallas as pl
from jax.experimental.pallas import tpu as pltpu
from jax.sharding import Mesh
from jax.sharding import PartitionSpec as P

QUERY_HEAD_COUNT = 128
KEY_VALUE_HEADS = 8
HEAD_SIZE = 128
BLK = 128
TOK = 256
SHARDS = 16
SLOTS = 32
META = 16
Z_CHIPS = SHARDS // 2
RING = Z_CHIPS // 2
DOC_MOST = 2304
BACK = -(-DOC_MOST // TOK)
WINDOW = BACK + 1
BLOCKS_BACK = -(-DOC_MOST // BLK)
WIDE = 8
MIDDLE = 4
NARROW = 2
MOST_BLOCKS = MIDDLE * -(-(BLOCKS_BACK + 1) // MIDDLE)
LOCAL_HEADS = 8
LANES = LOCAL_HEADS * BLK
PICKS_FIRST = WINDOW * TOK
PICKS_PARTS = SHARDS * SLOTS // (2 * HEAD_SIZE)
NEG_FILL = -1e30
VMEM_LIMIT = 60 * 2**20
SCALE = 1.0 / math.sqrt(HEAD_SIZE)
EXP2_SCALE = SCALE * math.log2(math.e)
F32 = jnp.float32
BF16 = jnp.bfloat16


def iota(shape, dim):
    return lax.broadcasted_iota(jnp.int32, shape, dim)


def dot(a, b):
    return jnp.dot(a, b, preferred_element_type=F32)


def ranks_within(member):
    earlier = (iota((TOK, TOK), 0) < iota((TOK, TOK), 1)).astype(F32).astype(BF16)
    counts = dot(member.astype(F32).astype(BF16), earlier)
    return jnp.where(member, counts, -1.0)


def pack_kernel(place_ref, rows_ref, out_ref):
    owner = place_ref[...] >> 8
    rank = ranks_within(owner == iota((SHARDS, TOK), 0))
    slot = iota((SLOTS, TOK), 0).astype(F32)
    picks = jnp.concatenate(
        [(rank[s : s + 1, :] == slot).astype(F32) for s in range(SHARDS)], axis=0
    ).astype(BF16)
    for first in range(0, rows_ref.shape[1], 256):
        cols = pl.ds(first, 256)
        out_ref[:, cols] = dot(picks, rows_ref[:, cols]).astype(BF16)


def stage_kernel(place_ref, kv_ref, out_ref, arrived):
    cols = pl.ds(pl.multiple_of((lax.axis_index("tp") // 2) * HEAD_SIZE, HEAD_SIZE), HEAD_SIZE)
    copies = [
        pltpu.make_async_copy(
            kv_ref.at[i, :, cols],
            out_ref.at[pl.ds(0, TOK), pl.ds(i * HEAD_SIZE, HEAD_SIZE)],
            arrived.at[i],
        )
        for i in range(2)
    ]
    for copy in copies:
        copy.start()
    place = place_ref[...]
    row = iota((META, TOK), 0)
    owner = jnp.broadcast_to((place >> 8).astype(F32), (META, TOK))
    within = jnp.broadcast_to((place & (TOK - 1)).astype(F32), (META, TOK))
    meta = jnp.where(row == 0, owner, jnp.where(row == 1, within, 0.0))
    out_ref[TOK:, :] = meta.astype(BF16)
    for copy in copies:
        copy.wait()


def fetch_all(sources, buffers, arrived):
    copies = [
        pltpu.make_async_copy(source, buffer, arrived.at[i])
        for i, (source, buffer) in enumerate(zip(sources, buffers))
    ]
    for copy in copies:
        copy.start()
    return copies


def permute_kernel(info_ref, *refs):
    count = 2 * RING + 1
    out_ref, slots_s = refs[count : count + 2]
    buffers, arrived = refs[count + 2 : -1], refs[-1]
    own_ref, mine, theirs = buffers[0], buffers[1 : 1 + RING], buffers[1 + RING :]
    for copy in fetch_all(refs[:count], buffers, arrived):
        copy.wait()
    shard = info_ref[0]
    core = info_ref[1]
    base = jnp.maximum(shard - BACK, 0)
    z, x = shard // 2, shard % 2
    sources = [(own_ref.at[j], shard ^ j) for j in range(2)]
    for refs_k, side in ((mine, core), (theirs, 1 - core)):
        for k in range(1, RING):
            far = (z + k * (2 * side - 1) + Z_CHIPS) % Z_CHIPS
            sources += [(refs_k[k - 1].at[j], 2 * far + (x ^ j)) for j in range(2)]
        far = (z + RING) % Z_CHIPS
        sources += [(refs_k[RING - 1], 2 * far + (x ^ side))]
    notes = [ref[TOK : TOK + META, :].astype(F32) for ref, _ in sources]
    owners = jnp.concatenate([note[:1, :] for note in notes], axis=0)
    within = jnp.concatenate([note[1:2, :] for note in notes], axis=0)
    rank = ranks_within(owners == shard.astype(F32))
    slot = iota((SLOTS, TOK), 0).astype(F32)
    lane = iota((SLOTS, TOK), 1).astype(F32)
    for i, (_, source) in enumerate(sources):
        hit = rank[i : i + 1, :] == slot
        landing = jnp.sum(jnp.where(hit, within[i : i + 1, :] + 1.0, 0.0), axis=1, keepdims=True)
        rows = pl.ds(pl.multiple_of(source * SLOTS, SLOTS), SLOTS)
        slots_s[rows, :] = (landing == lane + 1.0).astype(F32)
    for j in range(PICKS_PARTS):
        part = slots_s[j * TOK : (j + 1) * TOK, :].T.astype(BF16)
        out_ref[PICKS_FIRST + j * TOK : PICKS_FIRST + (j + 1) * TOK, :] = part

    def one_shard(i, carry):
        rows = iota((TOK, TOK), 0).astype(F32)
        goal = jnp.where(owners == (base + i).astype(F32), within, -1.0)
        total = jnp.zeros((TOK, 2 * HEAD_SIZE), F32)
        for n, (ref, _) in enumerate(sources):
            picks = (goal[n : n + 1, :] == rows).astype(F32).astype(BF16)
            total = total + dot(picks, ref[:TOK, :])
        out_ref[pl.ds(pl.multiple_of(i * TOK, TOK), TOK), :] = total.astype(BF16)
        return carry

    lax.fori_loop(0, shard - base + 1, one_shard, 0)


def visible_blocks(qb, seg_ref, allow_ref, on_block):
    q_first = seg_ref[0, qb]

    def scan(kb, count):
        seen = jnp.logical_and(seg_ref[1, kb] >= q_first, allow_ref[qb, kb] != 0)

        @pl.when(seen)
        def _():
            on_block(kb, count)

        return count + seen.astype(jnp.int32)

    count = lax.fori_loop(jnp.maximum(qb - BLOCKS_BACK, 0), qb + 1, scan, 0)
    wide = count // WIDE
    rest = count - wide * WIDE
    middle = (rest + 1) // MIDDLE
    narrow = (rest + MIDDLE - 1) // MIDDLE - middle
    return count, wide, middle, narrow


def block_rows(n, blocks=1):
    return pl.ds(pl.multiple_of(n * BLK, BLK), blocks * BLK)


def attention_kernel(
    info_ref,
    seg_ref,
    allow_ref,
    segv_ref,
    recv_ref,
    grad_ref,
    kv_ref,
    keep_ref,
    send_ref,
    sg_ref,
    qr_s,
    qt_s,
    gr_s,
    gt_s,
    k_s,
    v_s,
    bias_s,
    e_s,
    dp_s,
    top_s,
    acc_s,
    sg_s,
    list_s,
    sent,
):
    shard = info_ref[0]
    core = info_ref[1]
    base = jnp.maximum(shard - BACK, 0)
    acc_s[...] = jnp.zeros_like(acc_s)

    def query_block(half, carry):
        qb = shard * 2 + half
        q_seg = segv_ref[pl.ds(qb, 1), :]
        q_last = seg_ref[1, qb]
        picks = jnp.concatenate(
            [kv_ref[block_rows(PICKS_FIRST // BLK + 2 * j + half), :] for j in range(PICKS_PARTS)],
            axis=1,
        )
        for pair in range(LOCAL_HEADS // 2):
            q_two = dot(picks, recv_ref[:, pair * 256 : (pair + 1) * 256])
            for i in range(2):
                mine = slice((2 * pair + i) * BLK, (2 * pair + i + 1) * BLK)
                q_one = q_two[:, i * HEAD_SIZE : (i + 1) * HEAD_SIZE]
                qr_s[mine, :] = q_one.astype(BF16)
                qt_s[:, mine] = q_one.T.astype(BF16)
                g_one = grad_ref[block_rows(half), pl.ds((2 * pair + i) * HEAD_SIZE, HEAD_SIZE)]
                gr_s[mine, :] = g_one
                gt_s[:, mine] = g_one.astype(F32).T.astype(BF16)

        def on_block(kb, count):
            list_s[count] = kb
            src = block_rows(kb - 2 * base)
            dst = block_rows(count)
            k_s[dst, :] = kv_ref[src, :HEAD_SIZE]
            v_s[dst, :] = kv_ref[src, HEAD_SIZE:]
            whole = jnp.logical_and(kb < qb, seg_ref[0, kb] == q_last)

            @pl.when(whole)
            def _():
                bias_s[dst, :] = jnp.zeros((BLK, BLK), F32)

            @pl.when(jnp.logical_not(whole))
            def _():
                k_seg = jnp.broadcast_to(segv_ref[pl.ds(kb, 1), :].astype(F32), (BLK, BLK)).T
                k_pos = kb * BLK + iota((BLK, BLK), 0)
                q_pos = qb * BLK + iota((BLK, BLK), 1)
                ok = (k_seg == q_seg.astype(F32)) & (k_pos <= q_pos)
                bias_s[dst, :] = jnp.where(ok, 0.0, NEG_FILL)

        count, wide, middle, narrow = visible_blocks(qb, seg_ref, allow_ref, on_block)
        middle_first = wide * WIDE
        narrow_first = middle_first + middle * MIDDLE

        def fill(n, c):
            list_s[n] = 2 * SHARDS
            dst = block_rows(n)
            k_s[dst, :] = jnp.zeros((BLK, HEAD_SIZE), BF16)
            v_s[dst, :] = jnp.zeros((BLK, HEAD_SIZE), BF16)
            bias_s[dst, :] = jnp.full((BLK, BLK), NEG_FILL, F32)
            return c

        lax.fori_loop(count, narrow_first + narrow * NARROW, fill, 0)

        def first_pass(start, blocks, slot, state):
            top, total, weighed = state
            rows = block_rows(start, blocks)
            scores = dot(k_s[rows, :], qt_s[...])
            scores = scores + jnp.concatenate([bias_s[rows, :]] * LOCAL_HEADS, axis=1)
            new_top = jnp.maximum(top, jnp.max(scores, axis=0, keepdims=True))
            factor = jnp.exp2((top - new_top) * EXP2_SCALE)
            e = jnp.exp2((scores - new_top) * EXP2_SCALE)
            dp = dot(v_s[rows, :], gt_s[...])
            e_s[rows, :] = e
            dp_s[rows, :] = dp
            top_s[slot] = new_top
            total = total * factor + jnp.sum(e.reshape(-1, 8, LANES), axis=0)
            weighed = weighed * factor + jnp.sum((e * dp).reshape(-1, 8, LANES), axis=0)
            return (new_top, total, weighed)

        state = (
            jnp.full((1, LANES), NEG_FILL, F32),
            jnp.zeros((8, LANES), F32),
            jnp.zeros((8, LANES), F32),
        )
        state = lax.fori_loop(0, wide, lambda n, st: first_pass(n * WIDE, WIDE, n, st), state)
        state = lax.fori_loop(
            0,
            middle,
            lambda n, st: first_pass(middle_first + n * MIDDLE, MIDDLE, wide + n, st),
            state,
        )
        top, total, weighed = lax.fori_loop(
            0,
            narrow,
            lambda n, st: first_pass(narrow_first, NARROW, wide + middle, st),
            state,
        )
        inverse = 1.0 / jnp.sum(total, axis=0, keepdims=True)
        out_dot = jnp.sum(weighed, axis=0, keepdims=True) * inverse

        def copy_out(start, blocks, slot):
            rows = block_rows(start, blocks)
            return pltpu.make_async_copy(sg_s.at[rows, :], sg_ref.at[half, rows, :], sent.at[slot])

        def second_pass(start, blocks, slot):
            rows = block_rows(start, blocks)
            factor = jnp.exp2((top_s[slot] - top) * EXP2_SCALE) * inverse
            weights = e_s[rows, :] * factor
            score_grad = (weights * (dp_s[rows, :] - out_dot)).astype(BF16)
            sg_s[rows, :] = score_grad
            copy_out(start, blocks, slot).start()
            value_terms = dot(weights.astype(BF16), gr_s[...])
            key_terms = dot(score_grad, qr_s[...])
            for n in range(blocks):
                dst = block_rows(list_s[start + n])
                acc_s[0, dst, :] += key_terms[n * BLK : (n + 1) * BLK, :]
                acc_s[1, dst, :] += value_terms[n * BLK : (n + 1) * BLK, :]

        def finish(step, steps):
            lax.fori_loop(0, steps, lambda n, c: step(n) or c, 0)

        finish(lambda n: second_pass(n * WIDE, WIDE, n), wide)
        finish(lambda n: second_pass(middle_first + n * MIDDLE, MIDDLE, wide + n), middle)
        finish(lambda n: second_pass(narrow_first, NARROW, wide + middle), narrow)
        finish(lambda n: copy_out(n * WIDE, WIDE, n).wait(), wide)
        finish(lambda n: copy_out(middle_first + n * MIDDLE, MIDDLE, wide + n).wait(), middle)
        finish(lambda n: copy_out(narrow_first, NARROW, wide + middle).wait(), narrow)
        return carry

    lax.fori_loop(0, 2, query_block, 0)
    rows = slice(0, SHARDS * TOK)

    @pl.when(core == 0)
    def _():
        keep_ref[...] = (acc_s[0, rows, :] * SCALE).astype(BF16)
        send_ref[...] = acc_s[1, rows, :].astype(BF16)

    @pl.when(core == 1)
    def _():
        keep_ref[...] = acc_s[1, rows, :].astype(BF16)
        send_ref[...] = (acc_s[0, rows, :] * SCALE).astype(BF16)


def query_grad_kernel(
    info_ref, seg_ref, allow_ref, kv_in, sg_ref, dq_ref, kt_s, dqt_s, sg_s, arrived, kv_ref, kv_sem
):
    shard = info_ref[0]
    base = jnp.maximum(shard - BACK, 0)
    copy = pltpu.make_async_copy(kv_in.at[pl.ds(0, PICKS_FIRST), :], kv_ref, kv_sem)
    copy.start()

    def fetch(half, step):
        rows = block_rows(step * NARROW, NARROW)
        return pltpu.make_async_copy(
            sg_ref.at[half, rows, :], sg_s.at[half, rows, :], arrived.at[half, step]
        )

    def steps_of(half):
        nothing = lambda kb, count: None
        count, *_ = visible_blocks(shard * 2 + half, seg_ref, allow_ref, nothing)
        return (count + NARROW - 1) // NARROW

    def start_fetch(half, c):
        def one(step, c2):
            fetch(half, step).start()
            return c2

        return lax.fori_loop(0, steps_of(half), one, c)

    lax.fori_loop(0, 2, start_fetch, 0)
    copy.wait()

    def query_block(half, carry):
        def on_block(kb, count):
            lanes = block_rows(count % NARROW)
            k_blk = kv_ref[block_rows(kb - 2 * base), :HEAD_SIZE]
            kt_s[count // NARROW, :, lanes] = k_blk.astype(F32).T.astype(BF16)

        count, *_ = visible_blocks(shard * 2 + half, seg_ref, allow_ref, on_block)
        steps = (count + NARROW - 1) // NARROW

        def fill(n, c):
            lanes = block_rows(n % NARROW)
            kt_s[n // NARROW, :, lanes] = jnp.zeros((HEAD_SIZE, BLK), BF16)
            return c

        lax.fori_loop(count, steps * NARROW, fill, 0)
        dqt_s[...] = jnp.zeros_like(dqt_s)

        def one_step(step, c):
            fetch(half, step).wait()
            dqt_s[...] += dot(kt_s[step], sg_s[half, block_rows(step * NARROW, NARROW), :])
            return c

        lax.fori_loop(0, steps, one_step, 0)
        for h in range(LOCAL_HEADS):
            block = dqt_s[:, h * BLK : (h + 1) * BLK] * SCALE
            dq_ref[block_rows(half), h * HEAD_SIZE : (h + 1) * HEAD_SIZE] = block.T.astype(BF16)
        return carry

    lax.fori_loop(0, 2, query_block, 0)


VMEM = pl.BlockSpec(memory_space=pltpu.VMEM)
SMEM = pl.BlockSpec(memory_space=pltpu.SMEM)
ANY = pl.BlockSpec(memory_space=pl.ANY)
HBM = pl.BlockSpec(memory_space=pltpu.HBM)


def call_permute(info, own, mine, theirs):
    return pl.pallas_call(
        permute_kernel,
        in_specs=[SMEM] + [ANY] * (2 * RING + 1),
        out_specs=VMEM,
        out_shape=jax.ShapeDtypeStruct((PICKS_FIRST + PICKS_PARTS * TOK, 2 * HEAD_SIZE), BF16),
        scratch_shapes=[pltpu.VMEM((SHARDS * SLOTS, TOK), F32)]
        + [pltpu.VMEM(x.shape, x.dtype) for x in (own, *mine, *theirs)]
        + [pltpu.SemaphoreType.DMA((2 * RING + 1,))],
        compiler_params=pltpu.CompilerParams(vmem_limit_bytes=12 * 2**20),
        name="permute",
    )(info, own, *mine, *theirs)


def call_attention(info, ends, segments, allow, q_recv, grad, kv_window):
    return pl.pallas_call(
        attention_kernel,
        in_specs=[SMEM, SMEM, SMEM] + [VMEM] * 4,
        out_specs=[VMEM, VMEM, HBM],
        out_shape=[
            jax.ShapeDtypeStruct((SHARDS * TOK, HEAD_SIZE), BF16),
            jax.ShapeDtypeStruct((SHARDS * TOK, HEAD_SIZE), BF16),
            jax.ShapeDtypeStruct((2, MOST_BLOCKS * BLK, LANES), BF16),
        ],
        scratch_shapes=[
            pltpu.VMEM((LANES, HEAD_SIZE), BF16),
            pltpu.VMEM((HEAD_SIZE, LANES), BF16),
            pltpu.VMEM((LANES, HEAD_SIZE), BF16),
            pltpu.VMEM((HEAD_SIZE, LANES), BF16),
            pltpu.VMEM((MOST_BLOCKS * BLK, HEAD_SIZE), BF16),
            pltpu.VMEM((MOST_BLOCKS * BLK, HEAD_SIZE), BF16),
            pltpu.VMEM((MOST_BLOCKS * BLK, BLK), F32),
            pltpu.VMEM((MOST_BLOCKS * BLK, LANES), F32),
            pltpu.VMEM((MOST_BLOCKS * BLK, LANES), F32),
            pltpu.VMEM((MOST_BLOCKS // WIDE + 3, 1, LANES), F32),
            pltpu.VMEM((2, SHARDS * TOK + BLK, HEAD_SIZE), F32),
            pltpu.VMEM((MOST_BLOCKS * BLK, LANES), BF16),
            pltpu.SMEM((MOST_BLOCKS,), jnp.int32),
            pltpu.SemaphoreType.DMA((MOST_BLOCKS // WIDE + 3,)),
        ],
        compiler_params=pltpu.CompilerParams(vmem_limit_bytes=48 * 2**20),
        name="attention",
    )(info, ends, allow, segments.reshape(-1, BLK), q_recv, grad, kv_window)


def call_query_grad(info, ends, allow, kv_window, score_grad):
    return pl.pallas_call(
        query_grad_kernel,
        in_specs=[SMEM, SMEM, SMEM, HBM, HBM],
        out_specs=VMEM,
        out_shape=jax.ShapeDtypeStruct((TOK, LOCAL_HEADS * HEAD_SIZE), BF16),
        scratch_shapes=[
            pltpu.VMEM((MOST_BLOCKS // NARROW, HEAD_SIZE, NARROW * BLK), BF16),
            pltpu.VMEM((HEAD_SIZE, LANES), F32),
            pltpu.VMEM((2, MOST_BLOCKS * BLK, LANES), BF16),
            pltpu.SemaphoreType.DMA((2, MOST_BLOCKS // NARROW)),
            pltpu.VMEM((PICKS_FIRST, 2 * HEAD_SIZE), BF16),
            pltpu.SemaphoreType.DMA(()),
        ],
        compiler_params=pltpu.CompilerParams(vmem_limit_bytes=VMEM_LIMIT),
        cost_estimate=pl.CostEstimate(
            flops=2 * TOK * 2048 * LANES, bytes_accessed=12 * 2**20, transcendentals=0
        ),
        name="query_grad",
    )(info, ends, allow, kv_window, score_grad)


def on_device(queries, keys_values, out_grad, place, segments, allow):
    tp_index = lax.axis_index("tp")
    ctx_index = lax.axis_index(("z", "x"))
    tp_size = lax.axis_size("tp")
    width = LOCAL_HEADS * HEAD_SIZE
    info = jnp.stack([ctx_index, tp_index % 2]).astype(jnp.int32)
    staged = pl.pallas_call(
        stage_kernel,
        in_specs=[VMEM, pl.BlockSpec(memory_space=pl.ANY)],
        out_specs=VMEM,
        out_shape=jax.ShapeDtypeStruct((TOK + META, 2 * HEAD_SIZE), BF16),
        scratch_shapes=[pltpu.SemaphoreType.DMA((2,))],
        name="stage",
    )(place.reshape(1, TOK), keys_values)
    beside = lax.ppermute(staged, "x", [(0, 1), (1, 0)])
    own = jnp.stack([staged, beside])
    g_send = out_grad.reshape(-1, tp_size, width).transpose(1, 0, 2)
    own, g_send = lax.optimization_barrier((own, g_send))

    def around(hops):
        pairs = []
        for k in range(SHARDS * tp_size):
            ctx, tp = k // tp_size, k % tp_size
            far = (ctx + (2 * hops if tp % 2 == 0 else -2 * hops)) % SHARDS
            pairs.append((k, far * tp_size + tp))
        return pairs

    swap = [(k, k ^ 1) for k in range(tp_size)]
    first = lax.ppermute(own, ("z", "x", "tp"), around(1))
    second = lax.ppermute(first, ("z", "x", "tp"), around(1))
    third = lax.ppermute(second, ("z", "x", "tp"), around(1))
    half = lax.dynamic_index_in_dim(second, tp_index % 2, 0, keepdims=False)
    fourth = lax.ppermute(half, ("z", "x", "tp"), around(2))
    mine = [first, second, third, fourth]
    g_local = lax.all_to_all(g_send, "tp", split_axis=0, concat_axis=0, tiled=True)
    g_local = g_local.reshape(TOK, width)
    q_send = pl.pallas_call(
        pack_kernel,
        in_specs=[VMEM, VMEM],
        out_specs=VMEM,
        out_shape=jax.ShapeDtypeStruct((SHARDS * SLOTS, width), BF16),
        name="pack",
    )(place.reshape(1, TOK), queries)
    q_send, *mine = lax.optimization_barrier((q_send, *mine))
    theirs = [lax.ppermute(piece, "tp", swap) for piece in mine]
    q_recv = lax.all_to_all(q_send, ("z", "x"), split_axis=0, concat_axis=0, tiled=True)
    blocks = segments.reshape(-1, BLK)
    ends = jnp.stack([blocks[:, 0], blocks[:, BLK - 1]])
    kv_window = call_permute(info, own, mine, theirs)
    keep, send, score_grad = call_attention(
        info, ends, segments, allow, q_recv, g_local, kv_window
    )
    recv = lax.ppermute(send, "tp", swap)
    part = (keep.astype(F32) + recv.astype(F32)).astype(BF16)
    part, score_grad, late_ctx = lax.optimization_barrier((part, score_grad, ctx_index))
    rows = TOK // tp_size
    parts = lax.all_to_all(
        part.reshape(SHARDS * tp_size, rows, HEAD_SIZE),
        ("z", "x", "tp"),
        split_axis=0,
        concat_axis=0,
        tiled=True,
    )
    late_info = jnp.stack([late_ctx, late_ctx]).astype(jnp.int32)
    grad_q = call_query_grad(late_info, ends, allow, kv_window, score_grad)
    parts, grad_q = lax.optimization_barrier((parts, grad_q))
    heads = jnp.sum(parts.reshape(SHARDS, tp_size, rows, HEAD_SIZE).astype(F32), axis=0)
    key_value_gradient = (
        heads.astype(BF16)
        .reshape(KEY_VALUE_HEADS, 2, rows, HEAD_SIZE)
        .transpose(1, 2, 0, 3)
        .reshape(2, rows, KEY_VALUE_HEADS * HEAD_SIZE)
    )
    return (grad_q, key_value_gradient)


def solution(mesh):
    tp_size = mesh.shape["tp"]
    split = Mesh(mesh.devices.reshape(Z_CHIPS, 2, tp_size), ("z", "x", "tp"))
    ctx = ("z", "x")
    in_specs = (P(ctx, "tp"), P(None, ctx, None), P((*ctx, "tp"), None), P(ctx), P(), P())
    out_specs = (P(ctx, "tp"), P(None, (*ctx, "tp"), None))
    return jax.shard_map(
        on_device, mesh=split, in_specs=in_specs, out_specs=out_specs, check_vma=False
    )
```

```python
import functools
import math

import jax
import jax.numpy as jnp
from jax import lax
from jax.experimental import pallas as pl
from jax.experimental.pallas import tpu as pltpu
from jax.sharding import Mesh
from jax.sharding import PartitionSpec as P

QUERY_HEAD_COUNT = 128
KEY_VALUE_HEADS = 8
HEAD_SIZE = 128
BLK = 128
TOK = 256
SHARDS = 16
SLOTS = 32
META = 16
Z_CHIPS = SHARDS // 2
RING = Z_CHIPS // 2
DOC_MOST = 2304
BACK = -(-DOC_MOST // TOK)
WINDOW = BACK + 1
BLOCKS_BACK = -(-DOC_MOST // BLK)
WIDE = 8
MIDDLE = 4
NARROW = 2
MOST_BLOCKS = MIDDLE * -(-(BLOCKS_BACK + 1) // MIDDLE)
LOCAL_HEADS = 8
LANES = LOCAL_HEADS * BLK
PICKS_FIRST = WINDOW * TOK
PICKS_PARTS = SHARDS * SLOTS // (2 * HEAD_SIZE)
NEG_FILL = -1e30
VMEM_LIMIT = 60 * 2**20
SCALE = 1.0 / math.sqrt(HEAD_SIZE)
EXP2_SCALE = SCALE * math.log2(math.e)
F32 = jnp.float32
BF16 = jnp.bfloat16


def iota(shape, dim):
    return lax.broadcasted_iota(jnp.int32, shape, dim)


def dot(a, b):
    return jnp.dot(a, b, preferred_element_type=F32)


def ranks_within(member):
    earlier = (iota((TOK, TOK), 0) < iota((TOK, TOK), 1)).astype(F32).astype(BF16)
    counts = dot(member.astype(F32).astype(BF16), earlier)
    return jnp.where(member, counts, -1.0)


def pack_kernel(place_ref, rows_ref, out_ref):
    owner = place_ref[...] >> 8
    rank = ranks_within(owner == iota((SHARDS, TOK), 0))
    slot = iota((SLOTS, TOK), 0).astype(F32)
    picks = jnp.concatenate(
        [(rank[s : s + 1, :] == slot).astype(F32) for s in range(SHARDS)], axis=0
    ).astype(BF16)
    for first in range(0, rows_ref.shape[1], 256):
        cols = pl.ds(first, 256)
        out_ref[:, cols] = dot(picks, rows_ref[:, cols]).astype(BF16)


def stage_kernel(place_ref, kv_ref, out_ref, arrived):
    cols = pl.ds(pl.multiple_of((lax.axis_index("tp") // 2) * HEAD_SIZE, HEAD_SIZE), HEAD_SIZE)
    copies = [
        pltpu.make_async_copy(
            kv_ref.at[i, :, cols],
            out_ref.at[pl.ds(0, TOK), pl.ds(i * HEAD_SIZE, HEAD_SIZE)],
            arrived.at[i],
        )
        for i in range(2)
    ]
    for copy in copies:
        copy.start()
    place = place_ref[...]
    row = iota((META, TOK), 0)
    owner = jnp.broadcast_to((place >> 8).astype(F32), (META, TOK))
    within = jnp.broadcast_to((place & (TOK - 1)).astype(F32), (META, TOK))
    meta = jnp.where(row == 0, owner, jnp.where(row == 1, within, 0.0))
    out_ref[TOK:, :] = meta.astype(BF16)
    for copy in copies:
        copy.wait()


def fetch_all(sources, buffers, arrived):
    copies = [
        pltpu.make_async_copy(source, buffer, arrived.at[i])
        for i, (source, buffer) in enumerate(zip(sources, buffers))
    ]
    for copy in copies:
        copy.start()
    return copies


def permute_kernel(info_ref, *refs):
    count = 2 * RING + 1
    out_ref, slots_s = refs[count : count + 2]
    buffers, arrived = refs[count + 2 : -1], refs[-1]
    own_ref, mine, theirs = buffers[0], buffers[1 : 1 + RING], buffers[1 + RING :]
    for copy in fetch_all(refs[:count], buffers, arrived):
        copy.wait()
    shard = info_ref[0]
    core = info_ref[1]
    base = jnp.maximum(shard - BACK, 0)
    z, x = shard // 2, shard % 2
    sources = [(own_ref.at[j], shard ^ j) for j in range(2)]
    for refs_k, side in ((mine, core), (theirs, 1 - core)):
        for k in range(1, RING):
            far = (z + k * (2 * side - 1) + Z_CHIPS) % Z_CHIPS
            sources += [(refs_k[k - 1].at[j], 2 * far + (x ^ j)) for j in range(2)]
        far = (z + RING) % Z_CHIPS
        sources += [(refs_k[RING - 1], 2 * far + (x ^ side))]
    notes = [ref[TOK : TOK + META, :].astype(F32) for ref, _ in sources]
    owners = jnp.concatenate([note[:1, :] for note in notes], axis=0)
    within = jnp.concatenate([note[1:2, :] for note in notes], axis=0)
    rank = ranks_within(owners == shard.astype(F32))
    slot = iota((SLOTS, TOK), 0).astype(F32)
    lane = iota((SLOTS, TOK), 1).astype(F32)
    for i, (_, source) in enumerate(sources):
        hit = rank[i : i + 1, :] == slot
        landing = jnp.sum(jnp.where(hit, within[i : i + 1, :] + 1.0, 0.0), axis=1, keepdims=True)
        rows = pl.ds(pl.multiple_of(source * SLOTS, SLOTS), SLOTS)
        slots_s[rows, :] = (landing == lane + 1.0).astype(F32)
    for j in range(PICKS_PARTS):
        part = slots_s[j * TOK : (j + 1) * TOK, :].T.astype(BF16)
        out_ref[PICKS_FIRST + j * TOK : PICKS_FIRST + (j + 1) * TOK, :] = part

    def one_shard(i, carry):
        rows = iota((TOK, TOK), 0).astype(F32)
        goal = jnp.where(owners == (base + i).astype(F32), within, -1.0)
        total = jnp.zeros((TOK, 2 * HEAD_SIZE), F32)
        for n, (ref, _) in enumerate(sources):
            picks = (goal[n : n + 1, :] == rows).astype(F32).astype(BF16)
            total = total + dot(picks, ref[:TOK, :])
        out_ref[pl.ds(pl.multiple_of(i * TOK, TOK), TOK), :] = total.astype(BF16)
        return carry

    lax.fori_loop(0, shard - base + 1, one_shard, 0)


def visible_blocks(qb, seg_ref, allow_ref, on_block):
    q_first = seg_ref[0, qb]

    def scan(kb, count):
        seen = jnp.logical_and(seg_ref[1, kb] >= q_first, allow_ref[qb, kb] != 0)

        @pl.when(seen)
        def _():
            on_block(kb, count)

        return count + seen.astype(jnp.int32)

    count = lax.fori_loop(jnp.maximum(qb - BLOCKS_BACK, 0), qb + 1, scan, 0)
    wide = count // WIDE
    rest = count - wide * WIDE
    middle = (rest + 1) // MIDDLE
    narrow = (rest + MIDDLE - 1) // MIDDLE - middle
    return count, wide, middle, narrow


def block_rows(n, blocks=1):
    return pl.ds(pl.multiple_of(n * BLK, BLK), blocks * BLK)


def attention_kernel(
    info_ref,
    seg_ref,
    allow_ref,
    segv_ref,
    recv_ref,
    grad_ref,
    kv_ref,
    keep_ref,
    send_ref,
    sg_ref,
    qr_s,
    qt_s,
    gr_s,
    gt_s,
    k_s,
    v_s,
    bias_s,
    e_s,
    dp_s,
    top_s,
    acc_s,
    sg_s,
    list_s,
    sent,
):
    shard = info_ref[0]
    core = info_ref[1]
    base = jnp.maximum(shard - BACK, 0)
    acc_s[...] = jnp.zeros_like(acc_s)

    def query_block(half, carry):
        qb = shard * 2 + half
        q_seg = segv_ref[pl.ds(qb, 1), :]
        q_last = seg_ref[1, qb]
        picks = jnp.concatenate(
            [kv_ref[block_rows(PICKS_FIRST // BLK + 2 * j + half), :] for j in range(PICKS_PARTS)],
            axis=1,
        )
        for pair in range(LOCAL_HEADS // 2):
            q_two = dot(picks, recv_ref[:, pair * 256 : (pair + 1) * 256])
            for i in range(2):
                mine = slice((2 * pair + i) * BLK, (2 * pair + i + 1) * BLK)
                q_one = q_two[:, i * HEAD_SIZE : (i + 1) * HEAD_SIZE]
                qr_s[mine, :] = q_one.astype(BF16)
                qt_s[:, mine] = q_one.T.astype(BF16)
                g_one = grad_ref[block_rows(half), pl.ds((2 * pair + i) * HEAD_SIZE, HEAD_SIZE)]
                gr_s[mine, :] = g_one
                gt_s[:, mine] = g_one.astype(F32).T.astype(BF16)

        def on_block(kb, count):
            list_s[count] = kb
            src = block_rows(kb - 2 * base)
            dst = block_rows(count)
            k_s[dst, :] = kv_ref[src, :HEAD_SIZE]
            v_s[dst, :] = kv_ref[src, HEAD_SIZE:]
            whole = jnp.logical_and(kb < qb, seg_ref[0, kb] == q_last)

            @pl.when(whole)
            def _():
                bias_s[dst, :] = jnp.zeros((BLK, BLK), F32)

            @pl.when(jnp.logical_not(whole))
            def _():
                k_seg = jnp.broadcast_to(segv_ref[pl.ds(kb, 1), :].astype(F32), (BLK, BLK)).T
                k_pos = kb * BLK + iota((BLK, BLK), 0)
                q_pos = qb * BLK + iota((BLK, BLK), 1)
                ok = (k_seg == q_seg.astype(F32)) & (k_pos <= q_pos)
                bias_s[dst, :] = jnp.where(ok, 0.0, NEG_FILL)

        count, wide, middle, narrow = visible_blocks(qb, seg_ref, allow_ref, on_block)
        middle_first = wide * WIDE
        narrow_first = middle_first + middle * MIDDLE

        def fill(n, c):
            list_s[n] = 2 * SHARDS
            dst = block_rows(n)
            k_s[dst, :] = jnp.zeros((BLK, HEAD_SIZE), BF16)
            v_s[dst, :] = jnp.zeros((BLK, HEAD_SIZE), BF16)
            bias_s[dst, :] = jnp.full((BLK, BLK), NEG_FILL, F32)
            return c

        lax.fori_loop(count, narrow_first + narrow * NARROW, fill, 0)

        def first_pass(start, blocks, slot, state):
            top, total, weighed = state
            rows = block_rows(start, blocks)
            scores = dot(k_s[rows, :], qt_s[...])
            scores = scores + jnp.concatenate([bias_s[rows, :]] * LOCAL_HEADS, axis=1)
            new_top = jnp.maximum(top, jnp.max(scores, axis=0, keepdims=True))
            factor = jnp.exp2((top - new_top) * EXP2_SCALE)
            e = jnp.exp2((scores - new_top) * EXP2_SCALE)
            dp = dot(v_s[rows, :], gt_s[...])
            e_s[rows, :] = e
            dp_s[rows, :] = dp
            top_s[slot] = new_top
            total = total * factor + jnp.sum(e.reshape(-1, 8, LANES), axis=0)
            weighed = weighed * factor + jnp.sum((e * dp).reshape(-1, 8, LANES), axis=0)
            return (new_top, total, weighed)

        state = (
            jnp.full((1, LANES), NEG_FILL, F32),
            jnp.zeros((8, LANES), F32),
            jnp.zeros((8, LANES), F32),
        )
        state = lax.fori_loop(0, wide, lambda n, st: first_pass(n * WIDE, WIDE, n, st), state)
        state = lax.fori_loop(
            0,
            middle,
            lambda n, st: first_pass(middle_first + n * MIDDLE, MIDDLE, wide + n, st),
            state,
        )
        top, total, weighed = lax.fori_loop(
            0,
            narrow,
            lambda n, st: first_pass(narrow_first, NARROW, wide + middle, st),
            state,
        )
        inverse = 1.0 / jnp.sum(total, axis=0, keepdims=True)
        out_dot = jnp.sum(weighed, axis=0, keepdims=True) * inverse

        def copy_out(start, blocks, slot):
            rows = block_rows(start, blocks)
            return pltpu.make_async_copy(sg_s.at[rows, :], sg_ref.at[half, rows, :], sent.at[slot])

        def second_pass(start, blocks, slot):
            rows = block_rows(start, blocks)
            factor = jnp.exp2((top_s[slot] - top) * EXP2_SCALE) * inverse
            weights = e_s[rows, :] * factor
            score_grad = (weights * (dp_s[rows, :] - out_dot)).astype(BF16)
            sg_s[rows, :] = score_grad
            copy_out(start, blocks, slot).start()
            value_terms = dot(weights.astype(BF16), gr_s[...])
            key_terms = dot(score_grad, qr_s[...])
            for n in range(blocks):
                dst = block_rows(list_s[start + n])
                acc_s[0, dst, :] += key_terms[n * BLK : (n + 1) * BLK, :]
                acc_s[1, dst, :] += value_terms[n * BLK : (n + 1) * BLK, :]

        def finish(step, steps):
            lax.fori_loop(0, steps, lambda n, c: step(n) or c, 0)

        finish(lambda n: second_pass(n * WIDE, WIDE, n), wide)
        finish(lambda n: second_pass(middle_first + n * MIDDLE, MIDDLE, wide + n), middle)
        finish(lambda n: second_pass(narrow_first, NARROW, wide + middle), narrow)
        finish(lambda n: copy_out(n * WIDE, WIDE, n).wait(), wide)
        finish(lambda n: copy_out(middle_first + n * MIDDLE, MIDDLE, wide + n).wait(), middle)
        finish(lambda n: copy_out(narrow_first, NARROW, wide + middle).wait(), narrow)
        return carry

    lax.fori_loop(0, 2, query_block, 0)
    rows = slice(0, SHARDS * TOK)

    @pl.when(core == 0)
    def _():
        keep_ref[...] = (acc_s[0, rows, :] * SCALE).astype(BF16)
        send_ref[...] = acc_s[1, rows, :].astype(BF16)

    @pl.when(core == 1)
    def _():
        keep_ref[...] = acc_s[1, rows, :].astype(BF16)
        send_ref[...] = (acc_s[0, rows, :] * SCALE).astype(BF16)


def query_grad_kernel(
    info_ref, seg_ref, allow_ref, kv_in, sg_ref, dq_ref, kt_s, dqt_s, sg_s, arrived, kv_ref, kv_sem
):
    shard = info_ref[0]
    base = jnp.maximum(shard - BACK, 0)
    copy = pltpu.make_async_copy(kv_in.at[pl.ds(0, PICKS_FIRST), :], kv_ref, kv_sem)
    copy.start()

    def fetch(half, step):
        rows = block_rows(step * NARROW, NARROW)
        return pltpu.make_async_copy(
            sg_ref.at[half, rows, :], sg_s.at[half, rows, :], arrived.at[half, step]
        )

    def steps_of(half):
        nothing = lambda kb, count: None
        count, *_ = visible_blocks(shard * 2 + half, seg_ref, allow_ref, nothing)
        return (count + NARROW - 1) // NARROW

    def start_fetch(half, c):
        def one(step, c2):
            fetch(half, step).start()
            return c2

        return lax.fori_loop(0, steps_of(half), one, c)

    lax.fori_loop(0, 2, start_fetch, 0)
    copy.wait()

    def query_block(half, carry):
        def on_block(kb, count):
            lanes = block_rows(count % NARROW)
            k_blk = kv_ref[block_rows(kb - 2 * base), :HEAD_SIZE]
            kt_s[count // NARROW, :, lanes] = k_blk.astype(F32).T.astype(BF16)

        count, *_ = visible_blocks(shard * 2 + half, seg_ref, allow_ref, on_block)
        steps = (count + NARROW - 1) // NARROW

        def fill(n, c):
            lanes = block_rows(n % NARROW)
            kt_s[n // NARROW, :, lanes] = jnp.zeros((HEAD_SIZE, BLK), BF16)
            return c

        lax.fori_loop(count, steps * NARROW, fill, 0)
        dqt_s[...] = jnp.zeros_like(dqt_s)

        def one_step(step, c):
            fetch(half, step).wait()
            dqt_s[...] += dot(kt_s[step], sg_s[half, block_rows(step * NARROW, NARROW), :])
            return c

        lax.fori_loop(0, steps, one_step, 0)
        for h in range(LOCAL_HEADS):
            block = dqt_s[:, h * BLK : (h + 1) * BLK] * SCALE
            dq_ref[block_rows(half), h * HEAD_SIZE : (h + 1) * HEAD_SIZE] = block.T.astype(BF16)
        return carry

    lax.fori_loop(0, 2, query_block, 0)


VMEM = pl.BlockSpec(memory_space=pltpu.VMEM)
SMEM = pl.BlockSpec(memory_space=pltpu.SMEM)
ANY = pl.BlockSpec(memory_space=pl.ANY)
HBM = pl.BlockSpec(memory_space=pltpu.HBM)


def call_permute(info, own, mine, theirs):
    return pl.pallas_call(
        permute_kernel,
        in_specs=[SMEM] + [ANY] * (2 * RING + 1),
        out_specs=VMEM,
        out_shape=jax.ShapeDtypeStruct((PICKS_FIRST + PICKS_PARTS * TOK, 2 * HEAD_SIZE), BF16),
        scratch_shapes=[pltpu.VMEM((SHARDS * SLOTS, TOK), F32)]
        + [pltpu.VMEM(x.shape, x.dtype) for x in (own, *mine, *theirs)]
        + [pltpu.SemaphoreType.DMA((2 * RING + 1,))],
        compiler_params=pltpu.CompilerParams(vmem_limit_bytes=12 * 2**20),
        name="permute",
    )(info, own, *mine, *theirs)


def call_attention(info, ends, segments, allow, q_recv, grad, kv_window):
    return pl.pallas_call(
        attention_kernel,
        in_specs=[SMEM, SMEM, SMEM] + [VMEM] * 4,
        out_specs=[VMEM, VMEM, HBM],
        out_shape=[
            jax.ShapeDtypeStruct((SHARDS * TOK, HEAD_SIZE), BF16),
            jax.ShapeDtypeStruct((SHARDS * TOK, HEAD_SIZE), BF16),
            jax.ShapeDtypeStruct((2, MOST_BLOCKS * BLK, LANES), BF16),
        ],
        scratch_shapes=[
            pltpu.VMEM((LANES, HEAD_SIZE), BF16),
            pltpu.VMEM((HEAD_SIZE, LANES), BF16),
            pltpu.VMEM((LANES, HEAD_SIZE), BF16),
            pltpu.VMEM((HEAD_SIZE, LANES), BF16),
            pltpu.VMEM((MOST_BLOCKS * BLK, HEAD_SIZE), BF16),
            pltpu.VMEM((MOST_BLOCKS * BLK, HEAD_SIZE), BF16),
            pltpu.VMEM((MOST_BLOCKS * BLK, BLK), F32),
            pltpu.VMEM((MOST_BLOCKS * BLK, LANES), F32),
            pltpu.VMEM((MOST_BLOCKS * BLK, LANES), F32),
            pltpu.VMEM((MOST_BLOCKS // WIDE + 3, 1, LANES), F32),
            pltpu.VMEM((2, SHARDS * TOK + BLK, HEAD_SIZE), F32),
            pltpu.VMEM((MOST_BLOCKS * BLK, LANES), BF16),
            pltpu.SMEM((MOST_BLOCKS,), jnp.int32),
            pltpu.SemaphoreType.DMA((MOST_BLOCKS // WIDE + 3,)),
        ],
        compiler_params=pltpu.CompilerParams(vmem_limit_bytes=48 * 2**20),
        name="attention",
    )(info, ends, allow, segments.reshape(-1, BLK), q_recv, grad, kv_window)


def call_query_grad(info, ends, allow, kv_window, score_grad):
    return pl.pallas_call(
        query_grad_kernel,
        in_specs=[SMEM, SMEM, SMEM, HBM, HBM],
        out_specs=VMEM,
        out_shape=jax.ShapeDtypeStruct((TOK, LOCAL_HEADS * HEAD_SIZE), BF16),
        scratch_shapes=[
            pltpu.VMEM((MOST_BLOCKS // NARROW, HEAD_SIZE, NARROW * BLK), BF16),
            pltpu.VMEM((HEAD_SIZE, LANES), F32),
            pltpu.VMEM((2, MOST_BLOCKS * BLK, LANES), BF16),
            pltpu.SemaphoreType.DMA((2, MOST_BLOCKS // NARROW)),
            pltpu.VMEM((PICKS_FIRST, 2 * HEAD_SIZE), BF16),
            pltpu.SemaphoreType.DMA(()),
        ],
        compiler_params=pltpu.CompilerParams(vmem_limit_bytes=VMEM_LIMIT),
        cost_estimate=pl.CostEstimate(
            flops=2 * TOK * 2048 * LANES, bytes_accessed=12 * 2**20, transcendentals=0
        ),
        name="query_grad",
    )(info, ends, allow, kv_window, score_grad)


def block_ends(segments):
    blocks = segments.reshape(-1, BLK)
    return jnp.stack([blocks[:, 0], blocks[:, BLK - 1]])


def on_device(queries, keys_values, out_grad, place, segments, allow):
    tp_index = lax.axis_index("tp")
    ctx_index = lax.axis_index(("z", "x"))
    tp_size = lax.axis_size("tp")
    width = LOCAL_HEADS * HEAD_SIZE
    info = jnp.stack([ctx_index, tp_index % 2]).astype(jnp.int32)
    staged = pl.pallas_call(
        stage_kernel,
        in_specs=[VMEM, pl.BlockSpec(memory_space=pl.ANY)],
        out_specs=VMEM,
        out_shape=jax.ShapeDtypeStruct((TOK + META, 2 * HEAD_SIZE), BF16),
        scratch_shapes=[pltpu.SemaphoreType.DMA((2,))],
        name="stage",
    )(place.reshape(1, TOK), keys_values)
    beside = lax.ppermute(staged, "x", [(0, 1), (1, 0)])
    own = jnp.stack([staged, beside])
    g_send = out_grad.reshape(-1, tp_size, width).transpose(1, 0, 2)
    own, g_send = lax.optimization_barrier((own, g_send))

    def around(hops):
        pairs = []
        for k in range(SHARDS * tp_size):
            ctx, tp = k // tp_size, k % tp_size
            far = (ctx + (2 * hops if tp % 2 == 0 else -2 * hops)) % SHARDS
            pairs.append((k, far * tp_size + tp))
        return pairs

    swap = [(k, k ^ 1) for k in range(tp_size)]
    first = lax.ppermute(own, ("z", "x", "tp"), around(1))
    second = lax.ppermute(first, ("z", "x", "tp"), around(1))
    third = lax.ppermute(second, ("z", "x", "tp"), around(1))
    half = lax.dynamic_index_in_dim(second, tp_index % 2, 0, keepdims=False)
    fourth = lax.ppermute(half, ("z", "x", "tp"), around(2))
    mine = [first, second, third, fourth]
    g_local = lax.all_to_all(g_send, "tp", split_axis=0, concat_axis=0, tiled=True)
    g_local = g_local.reshape(TOK, width)
    q_send = pl.pallas_call(
        pack_kernel,
        in_specs=[VMEM, VMEM],
        out_specs=VMEM,
        out_shape=jax.ShapeDtypeStruct((SHARDS * SLOTS, width), BF16),
        name="pack",
    )(place.reshape(1, TOK), queries)
    q_send, *mine = lax.optimization_barrier((q_send, *mine))
    theirs = [lax.ppermute(piece, "tp", swap) for piece in mine]
    q_recv = lax.all_to_all(q_send, ("z", "x"), split_axis=0, concat_axis=0, tiled=True)
    ends = block_ends(segments)
    kv_window = call_permute(info, own, mine, theirs)
    keep, send, score_grad = call_attention(
        info, ends, segments, allow, q_recv, g_local, kv_window
    )
    recv = lax.ppermute(send, "tp", swap)
    part = (keep.astype(F32) + recv.astype(F32)).astype(BF16)
    part, score_grad, late_ctx, late_segments = lax.optimization_barrier(
        (part, score_grad, ctx_index, segments)
    )
    rows = TOK // tp_size
    parts = lax.all_to_all(
        part.reshape(SHARDS * tp_size, rows, HEAD_SIZE),
        ("z", "x", "tp"),
        split_axis=0,
        concat_axis=0,
        tiled=True,
    )
    late_info = jnp.stack([late_ctx, late_ctx]).astype(jnp.int32)
    grad_q = call_query_grad(late_info, block_ends(late_segments), allow, kv_window, score_grad)
    parts, grad_q = lax.optimization_barrier((parts, grad_q))
    heads = jnp.sum(parts.reshape(SHARDS, tp_size, rows, HEAD_SIZE).astype(F32), axis=0)
    key_value_gradient = (
        heads.astype(BF16)
        .reshape(KEY_VALUE_HEADS, 2, rows, HEAD_SIZE)
        .transpose(1, 2, 0, 3)
        .reshape(2, rows, KEY_VALUE_HEADS * HEAD_SIZE)
    )
    return (grad_q, key_value_gradient)


def solution(mesh):
    tp_size = mesh.shape["tp"]
    split = Mesh(mesh.devices.reshape(Z_CHIPS, 2, tp_size), ("z", "x", "tp"))
    ctx = ("z", "x")
    in_specs = (P(ctx, "tp"), P(None, ctx, None), P((*ctx, "tp"), None), P(ctx), P(), P())
    out_specs = (P(ctx, "tp"), P(None, (*ctx, "tp"), None))
    return jax.shard_map(
        on_device, mesh=split, in_specs=in_specs, out_specs=out_specs, check_vma=False
    )
```
